32 devices in a mesh: groups: 2 (over y), tensor: 4 (over z), section: 2 (over core), replica: 2 (over x).
Axes of the slice: x: 2, y: 2, z: 4, core: 2. Of those that a mesh axis runs over, the one named last changes fastest.
Arguments:
- tokens: bfloat16 [768, 8192], P(('groups', 'replica'), 'tensor'), parts along dimension 0
- cotangent: bfloat16 [768, 8192], P(('groups', 'replica'), 'tensor'), parts along dimension 0, may hold values from -0.29882812 to 0.29882812
- gain: float32 [2, 8192], P('section', 'tensor'), may hold values from 0.5 to 1.5
- frozen_base_weight: bfloat16 [2, 8192, 8192], P('section', 'tensor'), may hold values from -0.0625 to 0.0625
- adapter_down_factors: bfloat16 [2, 8192, 256], P('section', 'tensor'), may hold values from -0.0625 to 0.0625
- adapter_up_factors: bfloat16 [2, 256, 8192], P('section', None, 'tensor'), may hold values from -0.375 to 0.375
- tenant_adapter_scale: float32 [4], replicated, may hold values from 0.5 to 4
- row_tenant_owner: int32 [768], P(('groups', 'replica')), parts along dimension 0, may hold values from 0 to 4
Outputs:
- grad_down: float32 [2, 8192, 512], P('section', 'tensor', 'groups'), parts along dimension 2
- grad_up: float32 [2, 512, 8192], P('section', 'groups', 'tensor'), parts along dimension 1
The draws below stay inside these ranges and needn't reach their ends.
There are 2 independent parts, one for each index of `groups`. The reference program is written for one: setup_inputs(seed, part) draws one part's arguments, and reference() takes and returns one part's arrays. A program takes and returns all parts, laid end to end along the dimension named above; an argument that names none is the same for every part. Nothing has to cross between parts.
Inputs may be any that keep to these rules, and one draw needn't show every extreme that they name: `row_tenant_owner`: a row whose owner is 4 is padding and belongs to no tenant.
All inputs are finite; a program needn't handle non-finite values.
Results may differ from the reference program's by a relative error of at most 0.02.
Values may be sent and summed in bfloat16 or wider, within the bound.
No kernel may reach another device: no remote copies, remote signals or barrier semaphores. Data moves between devices by JAX's collectives and lax.ppermute only.
A program may use at most 128 MiB of HBM per device.

```python
import math
import jax
import jax.numpy as jnp
from jax import lax

D = 8192
TENANT_COUNT = 4
R = 64
ROWS_ALL = 384
N_TENSOR = 4


def draw_tokens(key, part):
    key = jax.random.fold_in(key, 11)
    keys = jax.random.split(key, 3)
    row_scale = jnp.exp(jax.random.uniform(keys[0], (ROWS_ALL, 1), jnp.float32, 0.0, math.log(10.0)))
    col_rise = jnp.power(3.0, jnp.arange(D, dtype=jnp.float32) / D)[None, :]
    col_scale = jnp.exp(jax.random.uniform(keys[1], (1, D), jnp.float32, 0.0, math.log(4.0))) * col_rise
    values = jax.random.normal(keys[2], (ROWS_ALL, D), jnp.float32)
    return (values * row_scale * col_scale * 0.1).astype(jnp.bfloat16)


def plant(drawn, key, low, top_value):
    dims = drawn.shape
    spot = [jax.random.randint(jax.random.fold_in(key, axis), (), 0, dims[axis]) for axis in range(len(dims))]
    drawn = drawn.at[tuple(spot)].set(low)
    longest = dims.index(max(dims))
    spot[longest] = (spot[longest] + 1) % dims[longest]
    return drawn.at[tuple(spot)].set(top_value)


def steps_of(rng, dims, pieces, low, largest):
    factor_of = 1.0
    for dim, blocks in pieces:
        draws = jax.random.uniform(jax.random.fold_in(jax.random.fold_in(rng, 6), dim), (blocks,), jnp.float32, low / len(pieces), largest / len(pieces))
        factor_of = factor_of * jnp.repeat(jnp.exp(draws), dims[dim] // blocks).reshape((-1,) + (1,) * (len(dims) - 1 - dim))
    return factor_of


def noise(stream_key, extent, scale, most, shards=(), kind=jnp.bfloat16):
    values = jax.random.normal(stream_key, extent, jnp.float32) * scale
    if len(shards) > 0:
        values = steps_of(stream_key, extent, shards, -0.22, 0.18) * values
    return jnp.clip(values, min=-most, max=most).astype(kind)


def setup_inputs(seed: int = 0, part: int = 0) -> dict:
    seeds = jax.random.split(jax.random.key(seed), 9)
    own_keys = jax.random.split(jax.random.fold_in(seeds[8], part), 9)
    return {
        "tokens": draw_tokens(jax.random.fold_in(jax.random.fold_in(seeds[8], part), 71), part),
        "cotangent": noise(own_keys[1], (ROWS_ALL, D), 0.05, 0.29882812, ((0, 2), (1, 4))),
        "gain": jnp.clip(1.0 + 0.1 * jax.random.normal(seeds[2], (2, D), jnp.float32), 0.5, 1.5),
        "frozen_base_weight": noise(seeds[3], (2, D, D), D ** -0.5, 0.0625, ((0, 2), (1, 4))),
        "adapter_down_factors": noise(seeds[4], (2, D, TENANT_COUNT * R), D ** -0.5, 0.0625, ((0, 2), (1, 4))),
        "adapter_up_factors": noise(seeds[5], (2, TENANT_COUNT * R, D), (TENANT_COUNT * R) ** -0.5, 0.375, ((0, 2), (2, 4))),
        "tenant_adapter_scale": jnp.clip(jnp.exp(jax.random.uniform(seeds[6], (TENANT_COUNT,), jnp.float32, math.log(0.5), math.log(4.0))), 0.5, 4.0),
        "row_tenant_owner": plant(jax.random.randint(own_keys[7], (ROWS_ALL,), 0, TENANT_COUNT + 1), jax.random.fold_in(own_keys[7], 1), 0, TENANT_COUNT).astype(jnp.int32),
    }


EPSILON = 1e-05

def per_tenant(values, coefficients):
    count = values.shape[0]
    return (values.reshape(count, TENANT_COUNT, R) * coefficients[:, :, None]).reshape(count, TENANT_COUNT * R)

def blocked_product(scaled, weight):
    width = D // N_TENSOR

    def add_block(running, block_no):
        offset = block_no * width
        piece_cols = lax.dynamic_slice_in_dim(scaled, offset, width, 1)
        piece_rows = lax.dynamic_slice_in_dim(weight, offset, width, 0)
        partial_sum = jnp.dot(piece_cols, piece_rows, preferred_element_type=jnp.float32).astype(jnp.bfloat16)
        partial_sum = lax.optimization_barrier(partial_sum)
        return (running + partial_sum.astype(jnp.float32), None)
    start_value = jnp.zeros((scaled.shape[0], weight.shape[1]), jnp.float32)
    result, unused = lax.scan(add_block, start_value, jnp.arange(N_TENSOR, dtype=jnp.int32))
    return result

def forward_section(inputs, gain_row, weight, down, upper, coefficients):
    x_float = inputs.astype(jnp.float32)
    inv_rms = lax.rsqrt(lax.optimization_barrier(jnp.mean(x_float * x_float, axis=1)) + EPSILON)
    scaled = (x_float * gain_row[None, :]).astype(jnp.bfloat16)
    base_part = blocked_product(scaled, weight)
    low_rank = per_tenant(jnp.dot(scaled, down, preferred_element_type=jnp.float32), coefficients).astype(jnp.bfloat16)
    projected = base_part + jnp.dot(low_rank, upper, preferred_element_type=jnp.float32)
    outputs = (x_float + inv_rms[:, None] * projected).astype(jnp.bfloat16)
    return (outputs, (x_float, scaled, inv_rms, projected, low_rank))

def backward_section(out_grad, stored, gain_row, weight, down, upper, coefficients):
    x_float, scaled, inv_rms, projected, low_rank = stored
    grad_float = out_grad.astype(jnp.float32)
    proj_grad = (inv_rms[:, None] * grad_float).astype(jnp.bfloat16)
    value_grad = jnp.dot(proj_grad, weight.T, preferred_element_type=jnp.float32)
    rank_grad = jnp.dot(proj_grad, upper.T, preferred_element_type=jnp.float32)
    row_dot = lax.optimization_barrier(jnp.sum(grad_float * projected, axis=1))
    low_grad = per_tenant(rank_grad, coefficients).astype(jnp.bfloat16)
    value_grad = value_grad + jnp.dot(low_grad, down.T, preferred_element_type=jnp.float32)
    cubed = inv_rms * inv_rms * inv_rms
    in_grad = (grad_float + gain_row[None, :] * value_grad - (row_dot * cubed)[:, None] * x_float / D).astype(jnp.bfloat16)
    grad_down = jnp.dot(scaled.T, low_grad, preferred_element_type=jnp.float32)
    grad_up = jnp.dot(low_rank.T, proj_grad, preferred_element_type=jnp.float32)
    return (in_grad, grad_down, grad_up)

def reference(tokens, cotangent, gain, frozen_base_weight, adapter_down_factors, adapter_up_factors, tenant_adapter_scale, row_tenant_owner):
    tenant_index_list = jnp.arange(TENANT_COUNT, dtype=jnp.int32)
    coefficients = tenant_adapter_scale[None, :] * (row_tenant_owner[:, None] == tenant_index_list[None, :]).astype(jnp.float32)
    hidden_one, first_store = forward_section(tokens, gain[0], frozen_base_weight[0], adapter_down_factors[0], adapter_up_factors[0], coefficients)
    unused_out, second_store = forward_section(hidden_one, gain[1], frozen_base_weight[1], adapter_down_factors[1], adapter_up_factors[1], coefficients)
    grad_one, down_one, up_one = backward_section(cotangent, second_store, gain[1], frozen_base_weight[1], adapter_down_factors[1], adapter_up_factors[1], coefficients)
    unused_grad, down_zero, up_zero = backward_section(grad_one, first_store, gain[0], frozen_base_weight[0], adapter_down_factors[0], adapter_up_factors[0], coefficients)
    return (jnp.stack([down_zero, down_one]), jnp.stack([up_zero, up_one]))
```

```python
import functools

import jax
import jax.numpy as jnp
from jax import lax
from jax.experimental import pallas as pl
from jax.experimental.pallas import tpu as pltpu
from jax.sharding import PartitionSpec as P

TENANT_COUNT = 4
EPSILON = 1e-05
CONTRACT_LAST = (((1,), (1,)), ((), ()))
CONTRACT_FIRST = (((0,), (0,)), ((), ()))
BF16 = jnp.bfloat16
F32 = jnp.float32


def block_kernel(table, own_ref, from_left_ref, from_right_ref, weight_ref, right_ref, left_ref, total_ref, *, tile):
    side = pl.program_id(0)
    step = pl.program_id(1)
    section = table[0]
    live = jnp.where(side == 0, table[2], table[4]) == 1
    columns = pl.ds(pl.multiple_of(step * tile, tile), tile)

    @pl.when((side == 0) & (step == 0) & (section == 1))
    def _():
        total_ref[...] = jnp.zeros_like(total_ref)

    @pl.when(live & (section == 0) & (side == 0))
    def _():
        right_ref[:, columns] = jnp.dot(
            own_ref[...], weight_ref[...], preferred_element_type=F32
        ).astype(BF16)

    @pl.when(live & (section == 0) & (side == 1))
    def _():
        left_ref[:, columns] = jnp.dot(
            own_ref[...], weight_ref[...], preferred_element_type=F32
        ).astype(BF16)

    @pl.when(live & (section == 1) & (side == 0))
    def _():
        total_ref[...] += lax.dot_general(
            from_left_ref[:, columns], weight_ref[...], CONTRACT_LAST, preferred_element_type=F32
        )

    @pl.when(live & (section == 1) & (side == 1))
    def _():
        total_ref[...] += lax.dot_general(
            from_right_ref[:, columns], weight_ref[...], CONTRACT_LAST, preferred_element_type=F32
        )


def block_products(table, own, from_left, from_right, weight):
    rows, width = own.shape
    tile = min(512, width)
    tiles = width // tile

    def weight_index(side, step, table):
        first = jnp.where(table[2] == 1, table[1] * tiles + step, table[3] * tiles)
        second = jnp.where(table[4] == 1, table[3] * tiles + step, table[1] * tiles + tiles - 1)
        return (0, jnp.where(side == 0, first, second))

    whole = pl.BlockSpec((rows, width), lambda side, step, table: (0, 0))
    return pl.pallas_call(
        functools.partial(block_kernel, tile=tile),
        grid_spec=pltpu.PrefetchScalarGridSpec(
            num_scalar_prefetch=1,
            grid=(2, tiles),
            in_specs=[whole, whole, whole, pl.BlockSpec((width, tile), weight_index)],
            out_specs=[whole, whole, whole],
        ),
        out_shape=[
            jax.ShapeDtypeStruct((rows, width), BF16),
            jax.ShapeDtypeStruct((rows, width), BF16),
            jax.ShapeDtypeStruct((rows, width), F32),
        ],
        compiler_params=pltpu.CompilerParams(vmem_limit_bytes=24 * 1024 * 1024),
        cost_estimate=pl.CostEstimate(
            flops=2 * rows * width * width, bytes_accessed=2 * width * width, transcendentals=0
        ),
    )(table, own, from_left, from_right, weight)


def sum_over_tensor(value, wire):
    count = lax.axis_size("tensor")
    if count & (count - 1):
        return lax.psum(value.astype(wire), "tensor").astype(F32)
    distance = 1
    while distance < count:
        other = lax.ppermute(
            value.astype(wire), "tensor", [(place, place ^ distance) for place in range(count)]
        )
        value = value + other.astype(F32)
        distance *= 2
    return value


def with_other_replicas(value):
    count = lax.axis_size("replica")
    return [value] + [
        lax.ppermute(value, "replica", [(place, (place + step) % count) for place in range(count)])
        for step in range(1, count)
    ]


def on_device(
    tokens,
    cotangent,
    gain,
    frozen_base_weight,
    adapter_down_factors,
    adapter_up_factors,
    tenant_adapter_scale,
    row_tenant_owner,
):
    section = lax.axis_index("section")
    place = lax.axis_index("tensor")
    count = lax.axis_size("tensor")
    is_first = section == 0
    weight = frozen_base_weight[0]
    gain_row = gain[0][None, :]
    down = adapter_down_factors[0]
    up = adapter_up_factors[0]
    rows, width = tokens.shape
    features = width * count
    rank = down.shape[1] // TENANT_COUNT

    owners = jnp.arange(TENANT_COUNT, dtype=jnp.int32)
    coefficients = tenant_adapter_scale[None, :] * (
        row_tenant_owner[:, None] == owners[None, :]
    ).astype(F32)
    coefficients = jnp.repeat(coefficients, rank, axis=1)

    token_float = tokens.astype(F32)
    early = jnp.where(is_first, (token_float * gain_row).astype(BF16), cotangent)

    def line(value, first_pairs, second_pairs, toward):
        pairs = [(2 * z, 2 * (z + toward)) for z in first_pairs] + [
            (2 * z + 1, 2 * (z + toward) + 1) for z in second_pairs
        ]
        return lax.ppermute(value, ("tensor", "section"), pairs)

    def table_of(first_right, first_right_live, first_left, first_left_live, step):
        from_left, from_right = place - step, place + step
        entries = [
            section,
            jnp.clip(jnp.where(is_first, first_right, from_left), 0, count - 1),
            jnp.where(is_first, first_right_live, from_left >= 0),
            jnp.clip(jnp.where(is_first, first_left, from_right), 0, count - 1),
            jnp.where(is_first, first_left_live, (from_right < count) & (step > 0)),
        ]
        return jnp.stack([entry.astype(jnp.int32) for entry in entries])

    everyone = range(count)
    from_left = line(cotangent, [], [z for z in everyone if z + 1 < count], 1)
    from_right = line(cotangent, [], [z for z in everyone if z > 0], -1)
    early_all = with_other_replicas(early)

    total = jnp.zeros((rows, width), F32)
    arrived_left, arrived_right = early, early
    for step in range(count):
        slot = step + 1
        if slot < count:
            table = table_of(
                count - slot + place, place + 1 <= slot, place + slot - count, place >= count - slot, step
            )
        else:
            table = table_of(place, place >= 0, place, place < 0, step)
        to_right, to_left, part = block_products(table, early, arrived_left, arrived_right, weight)
        total = total + part
        if slot < count:
            arrived_left, arrived_right = from_left, from_right
            to_right = jnp.where(
                is_first, to_right.astype(F32) + from_left.astype(F32), from_left.astype(F32)
            ).astype(BF16)
            to_left = jnp.where(
                is_first, to_left.astype(F32) + from_right.astype(F32), from_right.astype(F32)
            ).astype(BF16)
            passing = slot + 1
            from_left = line(
                to_right,
                [z for z in everyone if z + 1 <= slot and z + 1 < count],
                [z for z in everyone if passing < count and z >= passing - 1 and z + 1 < count],
                1,
            )
            from_right = line(
                to_left,
                [z for z in everyone if z >= count - slot and z > 0],
                [z for z in everyone if passing < count and z <= count - passing and z > 0],
                -1,
            )
    own_block = to_right

    rank_early = jnp.where(
        is_first,
        jnp.dot(early, down, preferred_element_type=F32),
        lax.dot_general(early, up, CONTRACT_LAST, preferred_element_type=F32),
    )
    squares = jnp.sum(token_float * token_float, axis=1, keepdims=True)
    summed = sum_over_tensor(
        jnp.concatenate([rank_early, jnp.broadcast_to(squares, (rows, 128))], axis=1), BF16
    )
    rank_early = summed[:, : down.shape[1]]
    inv_first = lax.rsqrt(summed[:, down.shape[1] :][:, :1] / features + EPSILON)
    small_early = (coefficients * rank_early).astype(BF16)
    low_product = jnp.where(
        is_first,
        jnp.dot(small_early, up, preferred_element_type=F32),
        lax.dot_general(small_early, down, CONTRACT_LAST, preferred_element_type=F32),
    )

    pulled = (gain_row * (total + low_product)).astype(BF16)
    pulled = lax.ppermute(pulled, "section", [(1, 0)]).astype(F32)

    projected = (
        own_block.astype(F32) + from_left.astype(F32) + from_right.astype(F32) + low_product
    )
    hidden = (token_float + inv_first * projected).astype(BF16)
    hidden_on_second = lax.ppermute(hidden, "section", [(0, 1)])
    hidden_float = hidden.astype(F32)
    row_sums = jnp.stack(
        [jnp.sum(hidden_float * hidden_float, axis=1), jnp.sum(hidden_float * pulled, axis=1)]
    )
    row_sums = sum_over_tensor(row_sums, F32)
    inv_second = lax.rsqrt(row_sums[0] / features + EPSILON)
    toward_hidden = row_sums[1] * inv_second * inv_second * inv_second / features
    inv_on_second = lax.ppermute(inv_second, "section", [(0, 1)])
    hidden_grad = (
        cotangent.astype(F32)
        + inv_second[:, None] * pulled
        - toward_hidden[:, None] * hidden_float
    ).astype(BF16)
    late = jnp.where(
        is_first, hidden_grad, (hidden_on_second.astype(F32) * gain_row).astype(BF16)
    )
    late_all = with_other_replicas(late)
    rank_late = jnp.where(
        is_first,
        lax.dot_general(late, up, CONTRACT_LAST, preferred_element_type=F32),
        jnp.dot(late, down, preferred_element_type=F32),
    )
    rank_late = sum_over_tensor(rank_late, BF16)
    row_scale = jnp.where(is_first, inv_first, inv_on_second[:, None])
    small_late = (coefficients * rank_late * row_scale).astype(BF16)
    small_early = (small_early.astype(F32) * row_scale).astype(BF16)
    smalls = jnp.where(
        is_first,
        jnp.concatenate([small_late, small_early], axis=1),
        jnp.concatenate([small_early, small_late], axis=1),
    )
    smalls = jnp.concatenate(with_other_replicas(smalls), axis=0)
    early_all = jnp.concatenate(early_all, axis=0)
    late_all = jnp.concatenate(late_all, axis=0)
    grad_down = lax.dot_general(
        jnp.where(is_first, early_all, late_all),
        smalls[:, : down.shape[1]],
        CONTRACT_FIRST,
        preferred_element_type=F32,
    )
    grad_up = lax.dot_general(
        smalls[:, down.shape[1] :],
        jnp.where(is_first, late_all, early_all),
        CONTRACT_FIRST,
        preferred_element_type=F32,
    )
    return (grad_down[None], grad_up[None])


def solution(mesh):
    return jax.shard_map(
        on_device,
        mesh=mesh,
        in_specs=(
            P(("groups", "replica"), "tensor"),
            P(("groups", "replica"), "tensor"),
            P("section", "tensor"),
            P("section", "tensor", None),
            P("section", "tensor", None),
            P("section", None, "tensor"),
            P(),
            P(("groups", "replica")),
        ),
        out_specs=(P("section", "tensor", "groups"), P("section", "groups", "tensor")),
        check_vma=False,
    )
```

```python
import functools

import jax
import jax.numpy as jnp
from jax import lax
from jax.experimental import pallas as pl
from jax.experimental.pallas import tpu as pltpu
from jax.sharding import PartitionSpec as P

TENANT_COUNT = 4
EPSILON = 1e-05
CONTRACT_LAST = (((1,), (1,)), ((), ()))
CONTRACT_FIRST = (((0,), (0,)), ((), ()))
BF16 = jnp.bfloat16
F32 = jnp.float32


def block_kernel(table, own_ref, from_left_ref, from_right_ref, weight_ref, right_ref, left_ref, total_ref, *, tile):
    side = pl.program_id(0)
    step = pl.program_id(1)
    section = table[0]
    live = jnp.where(side == 0, table[2], table[4]) == 1
    columns = pl.ds(pl.multiple_of(step * tile, tile), tile)

    @pl.when((side == 0) & (step == 0) & (section == 1))
    def _():
        total_ref[...] = jnp.zeros_like(total_ref)

    @pl.when(live & (section == 0) & (side == 0))
    def _():
        right_ref[:, columns] = jnp.dot(
            own_ref[...], weight_ref[...], preferred_element_type=F32
        ).astype(BF16)

    @pl.when(live & (section == 0) & (side == 1))
    def _():
        left_ref[:, columns] = jnp.dot(
            own_ref[...], weight_ref[...], preferred_element_type=F32
        ).astype(BF16)

    @pl.when(live & (section == 1) & (side == 0))
    def _():
        total_ref[...] += lax.dot_general(
            from_left_ref[:, columns], weight_ref[...], CONTRACT_LAST, preferred_element_type=F32
        )

    @pl.when(live & (section == 1) & (side == 1))
    def _():
        total_ref[...] += lax.dot_general(
            from_right_ref[:, columns], weight_ref[...], CONTRACT_LAST, preferred_element_type=F32
        )


def block_products(table, own, from_left, from_right, weight):
    rows, width = own.shape
    tile = min(512, width)
    tiles = width // tile

    def weight_index(side, step, table):
        first = jnp.where(table[2] == 1, table[1] * tiles + step, table[3] * tiles)
        second = jnp.where(table[4] == 1, table[3] * tiles + step, table[1] * tiles + tiles - 1)
        return (0, jnp.where(side == 0, first, second))

    whole = pl.BlockSpec((rows, width), lambda side, step, table: (0, 0))
    return pl.pallas_call(
        functools.partial(block_kernel, tile=tile),
        grid_spec=pltpu.PrefetchScalarGridSpec(
            num_scalar_prefetch=1,
            grid=(2, tiles),
            in_specs=[whole, whole, whole, pl.BlockSpec((width, tile), weight_index)],
            out_specs=[whole, whole, whole],
        ),
        out_shape=[
            jax.ShapeDtypeStruct((rows, width), BF16),
            jax.ShapeDtypeStruct((rows, width), BF16),
            jax.ShapeDtypeStruct((rows, width), F32),
        ],
        compiler_params=pltpu.CompilerParams(vmem_limit_bytes=24 * 1024 * 1024),
        cost_estimate=pl.CostEstimate(
            flops=2 * rows * width * width, bytes_accessed=2 * width * width, transcendentals=0
        ),
    )(table, own, from_left, from_right, weight)


def sum_over_tensor(value, wire):
    count = lax.axis_size("tensor")
    if count & (count - 1):
        return lax.psum(value.astype(wire), "tensor").astype(F32)
    distance = 1
    while distance < count:
        other = lax.ppermute(
            value.astype(wire), "tensor", [(place, place ^ distance) for place in range(count)]
        )
        value = value + other.astype(F32)
        distance *= 2
    return value


def with_other_replicas(value):
    count = lax.axis_size("replica")
    return [value] + [
        lax.ppermute(value, "replica", [(place, (place + step) % count) for place in range(count)])
        for step in range(1, count)
    ]


def on_device(
    tokens,
    cotangent,
    gain,
    frozen_base_weight,
    adapter_down_factors,
    adapter_up_factors,
    tenant_adapter_scale,
    row_tenant_owner,
):
    section = lax.axis_index("section")
    place = lax.axis_index("tensor")
    count = lax.axis_size("tensor")
    is_first = section == 0
    weight = frozen_base_weight[0]
    gain_row = gain[0][None, :]
    down = adapter_down_factors[0]
    up = adapter_up_factors[0]
    rows, width = tokens.shape
    features = width * count
    rank = down.shape[1] // TENANT_COUNT

    owners = jnp.arange(TENANT_COUNT, dtype=jnp.int32)
    coefficients = tenant_adapter_scale[None, :] * (
        row_tenant_owner[:, None] == owners[None, :]
    ).astype(F32)
    coefficients = jnp.repeat(coefficients, rank, axis=1)

    token_float = tokens.astype(F32)
    early = jnp.where(is_first, (token_float * gain_row).astype(BF16), cotangent)

    def small_product(value, first_factor, second_factor):
        return jnp.where(
            is_first,
            jnp.dot(value, first_factor, preferred_element_type=F32),
            lax.dot_general(value, second_factor, CONTRACT_LAST, preferred_element_type=F32),
        )

    def line(value, first_pairs, second_pairs, toward):
        pairs = [(2 * z, 2 * (z + toward)) for z in first_pairs] + [
            (2 * z + 1, 2 * (z + toward) + 1) for z in second_pairs
        ]
        return lax.ppermute(value, ("tensor", "section"), pairs)

    def table_of(first_right, first_right_live, first_left, first_left_live, step):
        from_left, from_right = place - step, place + step
        entries = [
            section,
            jnp.clip(jnp.where(is_first, first_right, from_left), 0, count - 1),
            jnp.where(is_first, first_right_live, from_left >= 0),
            jnp.clip(jnp.where(is_first, first_left, from_right), 0, count - 1),
            jnp.where(is_first, first_left_live, (from_right < count) & (step > 0)),
        ]
        return jnp.stack([entry.astype(jnp.int32) for entry in entries])

    everyone = range(count)
    from_left = line(cotangent, [], [z for z in everyone if z + 1 < count], 1)
    from_right = line(cotangent, [], [z for z in everyone if z > 0], -1)
    early_all = with_other_replicas(early)

    total = jnp.zeros((rows, width), F32)
    arrived_left, arrived_right = early, early
    small_sum = None
    for step in range(count):
        slot = step + 1
        if slot < count:
            table = table_of(
                count - slot + place, place + 1 <= slot, place + slot - count, place >= count - slot, step
            )
        else:
            table = table_of(place, place >= 0, place, place < 0, step)
        to_right, to_left, part = block_products(table, early, arrived_left, arrived_right, weight)
        total = total + part
        if step == 0:
            after, to_right = lax.optimization_barrier((early, to_right))
            small_sum = small_product(after, down, up)
            squares = jnp.sum(token_float * token_float, axis=1, keepdims=True)
            small_sum = sum_over_tensor(
                jnp.concatenate([small_sum, jnp.broadcast_to(squares, (rows, 128))], axis=1), BF16
            )
        if step == 1:
            to_right, *early_all = lax.optimization_barrier((to_right, *early_all))
        if step == count - 2:
            to_right, small_sum = lax.optimization_barrier((to_right, small_sum))
        if slot < count:
            arrived_left, arrived_right = from_left, from_right
            to_right = jnp.where(
                is_first, to_right.astype(F32) + from_left.astype(F32), from_left.astype(F32)
            ).astype(BF16)
            to_left = jnp.where(
                is_first, to_left.astype(F32) + from_right.astype(F32), from_right.astype(F32)
            ).astype(BF16)
            to_right, to_left, arrived_left, arrived_right = lax.optimization_barrier(
                (to_right, to_left, arrived_left, arrived_right)
            )
            passing = slot + 1
            from_left = line(
                to_right,
                [z for z in everyone if z + 1 <= slot and z + 1 < count],
                [z for z in everyone if passing < count and z >= passing - 1 and z + 1 < count],
                1,
            )
            from_right = line(
                to_left,
                [z for z in everyone if z >= count - slot and z > 0],
                [z for z in everyone if passing < count and z <= count - passing and z > 0],
                -1,
            )
    own_block = to_right

    rank_early = small_sum[:, : down.shape[1]]
    inv_first = lax.rsqrt(small_sum[:, down.shape[1] :][:, :1] / features + EPSILON)
    small_early = (coefficients * rank_early).astype(BF16)
    low_product = jnp.where(
        is_first,
        jnp.dot(small_early, up, preferred_element_type=F32),
        lax.dot_general(small_early, down, CONTRACT_LAST, preferred_element_type=F32),
    )

    pulled = (gain_row * (total + low_product)).astype(BF16)
    pulled = lax.ppermute(pulled, "section", [(1, 0)]).astype(F32)

    projected = (
        own_block.astype(F32) + from_left.astype(F32) + from_right.astype(F32) + low_product
    )
    hidden = (token_float + inv_first * projected).astype(BF16)
    hidden_on_second = lax.ppermute(hidden, "section", [(0, 1)])
    hidden_float = hidden.astype(F32)
    row_sums = jnp.stack(
        [jnp.sum(hidden_float * hidden_float, axis=1), jnp.sum(hidden_float * pulled, axis=1)]
    )
    row_sums = sum_over_tensor(row_sums, F32)
    inv_second = lax.rsqrt(row_sums[0] / features + EPSILON)
    toward_hidden = row_sums[1] * inv_second * inv_second * inv_second / features
    inv_on_second = lax.ppermute(inv_second, "section", [(0, 1)])
    hidden_grad = (
        cotangent.astype(F32)
        + inv_second[:, None] * pulled
        - toward_hidden[:, None] * hidden_float
    ).astype(BF16)
    late = jnp.where(
        is_first, hidden_grad, (hidden_on_second.astype(F32) * gain_row).astype(BF16)
    )
    late_all = with_other_replicas(late)
    rank_late = jnp.where(
        is_first,
        lax.dot_general(late, up, CONTRACT_LAST, preferred_element_type=F32),
        jnp.dot(late, down, preferred_element_type=F32),
    )
    rank_late = sum_over_tensor(rank_late, BF16)
    row_scale = jnp.where(is_first, inv_first, inv_on_second[:, None])
    small_late = (coefficients * rank_late * row_scale).astype(BF16)
    small_early = (small_early.astype(F32) * row_scale).astype(BF16)
    smalls = jnp.where(
        is_first,
        jnp.concatenate([small_late, small_early], axis=1),
        jnp.concatenate([small_early, small_late], axis=1),
    )
    smalls = jnp.concatenate(with_other_replicas(smalls), axis=0)
    early_all = jnp.concatenate(early_all, axis=0)
    late_all = jnp.concatenate(late_all, axis=0)
    grad_down = lax.dot_general(
        jnp.where(is_first, early_all, late_all),
        smalls[:, : down.shape[1]],
        CONTRACT_FIRST,
        preferred_element_type=F32,
    )
    grad_up = lax.dot_general(
        smalls[:, down.shape[1] :],
        jnp.where(is_first, late_all, early_all),
        CONTRACT_FIRST,
        preferred_element_type=F32,
    )
    return (grad_down[None], grad_up[None])


def solution(mesh):
    return jax.shard_map(
        on_device,
        mesh=mesh,
        in_specs=(
            P(("groups", "replica"), "tensor"),
            P(("groups", "replica"), "tensor"),
            P("section", "tensor"),
            P("section", "tensor", None),
            P("section", "tensor", None),
            P("section", None, "tensor"),
            P(),
            P(("groups", "replica")),
        ),
        out_specs=(P("section", "tensor", "groups"), P("section", "groups", "tensor")),
        check_vma=False,
    )
```

```python
import functools

import jax
import jax.numpy as jnp
from jax import lax
from jax.experimental import pallas as pl
from jax.experimental.pallas import tpu as pltpu
from jax.sharding import PartitionSpec as P

TENANT_COUNT = 4
EPSILON = 1e-05
CONTRACT_LAST = (((1,), (1,)), ((), ()))
CONTRACT_FIRST = (((0,), (0,)), ((), ()))
BF16 = jnp.bfloat16
F32 = jnp.float32
AHEAD = 2


def block_kernel(table, value_ref, weight_ref, out_ref, wide, tall, arrived, *, stage, tile, tiles):
    section = table[0]
    block = table[1 + stage]
    step = pl.program_id(0)
    width = tile * tiles

    def copy_of(index, is_wide):
        whole = pl.ds(pl.multiple_of(block * width, width), width)
        part = pl.ds(pl.multiple_of(block * width + index * tile, tile), tile)
        if is_wide:
            return pltpu.make_async_copy(weight_ref.at[:, part], wide.at[index], arrived.at[index])
        rows = pl.ds(pl.multiple_of(index * tile, tile), tile)
        return pltpu.make_async_copy(weight_ref.at[rows, whole], tall.at[index], arrived.at[index])

    for number, is_wide in ((0, True), (1, False)):

        @pl.when(section == number)
        def _():
            @pl.when(step == 0)
            def _():
                for index in range(min(AHEAD, tiles)):
                    copy_of(index, is_wide).start()

            @pl.when(step + AHEAD < tiles)
            def _():
                copy_of(step + AHEAD, is_wide).start()

            copy_of(step, is_wide).wait()
            if is_wide:
                out_ref[...] = jnp.dot(value_ref[...], wide[step], preferred_element_type=F32)
            else:
                out_ref[...] = lax.dot_general(
                    value_ref[...], tall[step], CONTRACT_LAST, preferred_element_type=F32
                )


def block_product(table, value, weight, stage):
    rows, width = value.shape
    tile = min(256, width)
    tiles = width // tile
    return pl.pallas_call(
        functools.partial(block_kernel, stage=stage, tile=tile, tiles=tiles),
        grid_spec=pltpu.PrefetchScalarGridSpec(
            num_scalar_prefetch=1,
            grid=(tiles,),
            in_specs=[
                pl.BlockSpec((rows, width), lambda step, table: (0, 0)),
                pl.BlockSpec(memory_space=pl.ANY),
            ],
            out_specs=pl.BlockSpec((rows, tile), lambda step, table: (0, step)),
            scratch_shapes=[
                pltpu.VMEM((tiles, width, tile), BF16),
                pltpu.VMEM((tiles, tile, width), BF16),
                pltpu.SemaphoreType.DMA((tiles,)),
            ],
        ),
        out_shape=jax.ShapeDtypeStruct((rows, width), F32),
        compiler_params=pltpu.CompilerParams(vmem_limit_bytes=24 * 1024 * 1024),
        cost_estimate=pl.CostEstimate(
            flops=2 * rows * width * width, bytes_accessed=2 * width * width, transcendentals=0
        ),
    )(table, value, weight)


def gradient_kernel(table, *refs, replicas):
    early, late, small_early, small_late = (
        refs[kind * replicas : (kind + 1) * replicas] for kind in range(4)
    )
    down_ref, up_ref = refs[4 * replicas :]

    def products(down_rows, down_small, up_rows, up_small):
        down_ref[...] = sum(
            lax.dot_general(a[...], b[...], CONTRACT_FIRST, preferred_element_type=F32)
            for a, b in zip(down_rows, down_small)
        )
        up_ref[...] = sum(
            lax.dot_general(a[...], b[...], CONTRACT_FIRST, preferred_element_type=F32)
            for a, b in zip(up_small, up_rows)
        )

    @pl.when(table[0] == 0)
    def _():
        products(early, small_late, late, small_early)

    @pl.when(table[0] == 1)
    def _():
        products(late, small_early, early, small_late)


def gradients(table, early, late, small_early, small_late):
    replicas = len(early)
    rows, width = early[0].shape
    rank = small_early[0].shape[1]
    tile = min(512, width)
    columns = pl.BlockSpec((rows, tile), lambda step, table: (0, step))
    small = pl.BlockSpec((rows, rank), lambda step, table: (0, 0))
    return pl.pallas_call(
        functools.partial(gradient_kernel, replicas=replicas),
        grid_spec=pltpu.PrefetchScalarGridSpec(
            num_scalar_prefetch=1,
            grid=(width // tile,),
            in_specs=[columns] * (2 * replicas) + [small] * (2 * replicas),
            out_specs=[
                pl.BlockSpec((tile, rank), lambda step, table: (step, 0)),
                pl.BlockSpec((rank, tile), lambda step, table: (0, step)),
            ],
        ),
        out_shape=[
            jax.ShapeDtypeStruct((width, rank), F32),
            jax.ShapeDtypeStruct((rank, width), F32),
        ],
        compiler_params=pltpu.CompilerParams(vmem_limit_bytes=24 * 1024 * 1024),
        cost_estimate=pl.CostEstimate(
            flops=4 * replicas * rows * width * rank,
            bytes_accessed=8 * width * rank + 4 * replicas * rows * width,
            transcendentals=0,
        ),
    )(table, *early, *late, *small_early, *small_late)


def orders(count):
    first, first_slots, second, second_slots = [], [], [], []
    for z in range(count):
        sends = [(slot, 0, count - slot + z) for slot in range(z + 1, count)]
        sends += [(slot, 1, slot - count + z) for slot in range(count - z, count)]
        sends.sort()
        first.append([block for _, _, block in sends] + [z])
        first_slots.append({(slot, side): at for at, (slot, side, _) in enumerate(sends)})
        arrivals = [(slot, 0, z - 1 - slot) for slot in range(z)]
        arrivals += [(slot, 1, z + 1 + slot) for slot in range(count - 1 - z)]
        arrivals.sort()
        second.append([z] + [block for _, _, block in arrivals])
        second_slots.append([None] + [(slot, side) for slot, side, _ in arrivals])
    return first, first_slots, second, second_slots


def pick(place_of, choice, cases):
    if len(cases) == 1:
        return cases[0]
    chosen = jnp.asarray(choice, jnp.int32)[place_of]
    return lax.select_n(chosen, *cases) if len(cases) > 2 else jnp.where(chosen == 0, *cases)


def sum_over_tensor(value, wire):
    count = lax.axis_size("tensor")
    if count & (count - 1):
        return lax.psum(value.astype(wire), "tensor").astype(F32)
    distance = 1
    while distance < count:
        other = lax.ppermute(
            value.astype(wire), "tensor", [(place, place ^ distance) for place in range(count)]
        )
        value = value + other.astype(F32)
        distance *= 2
    return value


def with_other_replicas(value):
    count = lax.axis_size("replica")
    return [value] + [
        lax.ppermute(value, "replica", [(place, (place + step) % count) for place in range(count)])
        for step in range(1, count)
    ]


def on_device(
    tokens,
    cotangent,
    gain,
    frozen_base_weight,
    adapter_down_factors,
    adapter_up_factors,
    tenant_adapter_scale,
    row_tenant_owner,
):
    section = lax.axis_index("section")
    place = lax.axis_index("tensor")
    count = lax.axis_size("tensor")
    is_first = section == 0
    weight = frozen_base_weight[0]
    gain_row = gain[0][None, :]
    down = adapter_down_factors[0]
    up = adapter_up_factors[0]
    rows, width = tokens.shape
    features = width * count
    ranks = down.shape[1]

    tenant_of_column = jnp.arange(ranks, dtype=jnp.int32) // (ranks // TENANT_COUNT)
    coefficients = jnp.where(
        row_tenant_owner[:, None] == tenant_of_column[None, :],
        jnp.repeat(tenant_adapter_scale, ranks // TENANT_COUNT)[None, :],
        0.0,
    )

    first_order, first_slots, second_order, second_slots = orders(count)
    place_of = section * count + place
    table = jnp.concatenate(
        [section[None].astype(jnp.int32), jnp.asarray(first_order + second_order, jnp.int32)[place_of]]
    )

    def small_product(value, first_factor, second_factor):
        return jnp.where(
            is_first,
            jnp.dot(value, first_factor, preferred_element_type=F32),
            lax.dot_general(value, second_factor, CONTRACT_LAST, preferred_element_type=F32),
        )

    def line(value, first_pairs, second_pairs, toward):
        pairs = [(2 * z, 2 * (z + toward)) for z in first_pairs] + [
            (2 * z + 1, 2 * (z + toward) + 1) for z in second_pairs
        ]
        return lax.ppermute(value, ("tensor", "section"), pairs)

    token_float = tokens.astype(F32)
    early = lax.optimization_barrier(
        jnp.where(is_first, (token_float * gain_row).astype(BF16), cotangent)
    )

    everyone = range(count)
    arrivals = [
        (
            line(cotangent, [], [z for z in everyone if z + 1 < count], 1),
            line(cotangent, [], [z for z in everyone if z > 0], -1),
        )
    ]
    early_all = with_other_replicas(early)

    parts = []
    small_sum = None
    for stage in range(count):
        wanted = [None if stage == 0 else second_slots[z][stage] for z in everyone]
        cases = sorted({slot for slot in wanted if slot is not None})
        here = [early] + [arrivals[slot][side] for slot, side in cases]
        if stage > 0:
            *here, _, _ = lax.optimization_barrier((*here, *arrivals[stage - 1]))
        value = pick(
            place_of,
            [0] * count + [0 if slot is None else 1 + cases.index(slot) for slot in wanted],
            here,
        )
        part = block_product(table, value, weight, stage)
        if stage == 0:
            after, part = lax.optimization_barrier((early, part))
            small_sum = small_product(after, down, up)
            squares = jnp.sum(token_float * token_float, axis=1, keepdims=True)
            small_sum = sum_over_tensor(
                jnp.concatenate([small_sum, jnp.broadcast_to(squares, (rows, 128))], axis=1), BF16
            )
        if stage == 1:
            part, *early_all = lax.optimization_barrier((part, *early_all))
        if stage == count - 2:
            part, small_sum = lax.optimization_barrier((part, small_sum))
        parts.append(part)
        slot = stage + 1
        if slot == count:
            break
        sent = []
        for side in (0, 1):
            needed = [first_slots[z].get((slot, side)) for z in everyone]
            stages = sorted({at for at in needed if at is not None})
            own = pick(
                place_of,
                [0 if at is None else stages.index(at) for at in needed] + [0] * count,
                [parts[at] for at in stages],
            )
            arrived = arrivals[-1][side].astype(F32)
            sent.append((arrived + jnp.where(is_first, own, 0.0)).astype(BF16))
        arrivals.append(
            (
                line(
                    sent[0],
                    [z for z in everyone if z < slot and z + 1 < count],
                    [z for z in everyone if slot + 1 < count and z >= slot and z + 1 < count],
                    1,
                ),
                line(
                    sent[1],
                    [z for z in everyone if z >= count - slot and z > 0],
                    [z for z in everyone if slot + 1 < count and z < count - slot and z > 0],
                    -1,
                ),
            )
        )
    from_left, from_right = arrivals[-1]

    inv_first = lax.rsqrt(small_sum[:, ranks:][:, :1] / features + EPSILON)
    small_early = (coefficients * small_sum[:, :ranks]).astype(BF16)
    low_product = jnp.where(
        is_first,
        jnp.dot(small_early, up, preferred_element_type=F32),
        lax.dot_general(small_early, down, CONTRACT_LAST, preferred_element_type=F32),
    )

    parts = lax.optimization_barrier(parts)
    pulled = (gain_row * (sum(parts) + low_product)).astype(BF16)
    pulled = lax.ppermute(pulled, "section", [(1, 0)]).astype(F32)

    projected = parts[-1] + from_left.astype(F32) + from_right.astype(F32) + low_product
    hidden = (token_float + inv_first * projected).astype(BF16)
    hidden_on_second = lax.ppermute(hidden, "section", [(0, 1)])
    hidden_float = hidden.astype(F32)
    row_sums = jnp.stack(
        [jnp.sum(hidden_float * hidden_float, axis=1), jnp.sum(hidden_float * pulled, axis=1)]
    )
    row_sums = sum_over_tensor(row_sums, F32)
    inv_second = lax.rsqrt(row_sums[0] / features + EPSILON)
    toward_hidden = row_sums[1] * inv_second * inv_second * inv_second / features
    inv_on_second = lax.ppermute(inv_second, "section", [(0, 1)])
    hidden_grad = (
        cotangent.astype(F32)
        + inv_second[:, None] * pulled
        - toward_hidden[:, None] * hidden_float
    ).astype(BF16)
    late = jnp.where(
        is_first, hidden_grad, (hidden_on_second.astype(F32) * gain_row).astype(BF16)
    )
    late_all = with_other_replicas(late)
    rank_late = sum_over_tensor(
        jnp.where(
            is_first,
            lax.dot_general(late, up, CONTRACT_LAST, preferred_element_type=F32),
            jnp.dot(late, down, preferred_element_type=F32),
        ),
        BF16,
    )
    row_scale = jnp.where(is_first, inv_first, inv_on_second[:, None])
    small_late = (coefficients * rank_late * row_scale).astype(BF16)
    small_early = (small_early.astype(F32) * row_scale).astype(BF16)
    smalls = with_other_replicas(jnp.concatenate([small_early, small_late], axis=1))
    grad_down, grad_up = gradients(
        table,
        early_all,
        late_all,
        [small[:, :ranks] for small in smalls],
        [small[:, ranks:] for small in smalls],
    )
    return (grad_down[None], grad_up[None])


def solution(mesh):
    return jax.shard_map(
        on_device,
        mesh=mesh,
        in_specs=(
            P(("groups", "replica"), "tensor"),
            P(("groups", "replica"), "tensor"),
            P("section", "tensor"),
            P("section", "tensor", None),
            P("section", "tensor", None),
            P("section", None, "tensor"),
            P(),
            P(("groups", "replica")),
        ),
        out_specs=(P("section", "tensor", "groups"), P("section", "groups", "tensor")),
        check_vma=False,
    )
```

```python
import functools

import jax
import jax.numpy as jnp
from jax import lax
from jax.experimental import pallas as pl
from jax.experimental.pallas import tpu as pltpu
from jax.sharding import PartitionSpec as P

TENANT_COUNT = 4
EPSILON = 1e-05
CONTRACT_LAST = (((1,), (1,)), ((), ()))
CONTRACT_FIRST = (((0,), (0,)), ((), ()))
BF16 = jnp.bfloat16
F32 = jnp.float32
AHEAD = 2


def is_one_of(number, members):
    return functools.reduce(jnp.logical_or, [number == member for member in members])


def look_up(number, values):
    found = values[0]
    for value in sorted(set(values) - {values[0]}):
        found = jnp.where(
            is_one_of(number, [at for at, other in enumerate(values) if other == value]), value, found
        )
    return found


def block_kernel(table, value_ref, weight_ref, out_ref, wide, tall, arrived, *, blocks, tile, tiles):
    section = table[0]
    block = look_up(table[1], blocks)
    step = pl.program_id(0)
    width = tile * tiles

    def copy_of(index, is_wide):
        whole = pl.ds(pl.multiple_of(block * width, width), width)
        part = pl.ds(pl.multiple_of(block * width + index * tile, tile), tile)
        if is_wide:
            return pltpu.make_async_copy(weight_ref.at[:, part], wide.at[index], arrived.at[index])
        rows = pl.ds(pl.multiple_of(index * tile, tile), tile)
        return pltpu.make_async_copy(weight_ref.at[rows, whole], tall.at[index], arrived.at[index])

    for number, is_wide in ((0, True), (1, False)):

        @pl.when(section == number)
        def _():
            @pl.when(step == 0)
            def _():
                for index in range(min(AHEAD, tiles)):
                    copy_of(index, is_wide).start()

            @pl.when(step + AHEAD < tiles)
            def _():
                copy_of(step + AHEAD, is_wide).start()

            copy_of(step, is_wide).wait()
            if is_wide:
                out_ref[...] = jnp.dot(value_ref[...], wide[step], preferred_element_type=F32)
            else:
                out_ref[...] = lax.dot_general(
                    value_ref[...], tall[step], CONTRACT_LAST, preferred_element_type=F32
                )


def block_product(table, value, weight, blocks):
    rows, width = value.shape
    tile = min(256, width)
    tiles = width // tile
    return pl.pallas_call(
        functools.partial(block_kernel, blocks=blocks, tile=tile, tiles=tiles),
        grid_spec=pltpu.PrefetchScalarGridSpec(
            num_scalar_prefetch=1,
            grid=(tiles,),
            in_specs=[
                pl.BlockSpec((rows, width), lambda step, table: (0, 0)),
                pl.BlockSpec(memory_space=pl.ANY),
            ],
            out_specs=pl.BlockSpec((rows, tile), lambda step, table: (0, step)),
            scratch_shapes=[
                pltpu.VMEM((tiles, width, tile), BF16),
                pltpu.VMEM((tiles, tile, width), BF16),
                pltpu.SemaphoreType.DMA((tiles,)),
            ],
        ),
        out_shape=jax.ShapeDtypeStruct((rows, width), F32),
        compiler_params=pltpu.CompilerParams(vmem_limit_bytes=24 * 1024 * 1024),
        cost_estimate=pl.CostEstimate(
            flops=8 * rows * width * width, bytes_accessed=2 * width * width, transcendentals=0
        ),
    )(table, value, weight)


def gradient_kernel(table, gain_ref, *refs, replicas):
    early, cotangent, pulled, hidden, smalls = (
        refs[kind * replicas : (kind + 1) * replicas] for kind in range(5)
    )
    down_ref, up_ref = refs[5 * replicas :]
    ranks = down_ref.shape[1]

    def products(down_rows, up_rows):
        down_ref[...] = sum(
            lax.dot_general(a, small[:, ranks : 2 * ranks], CONTRACT_FIRST, preferred_element_type=F32)
            for a, small in zip(down_rows, smalls)
        )
        up_ref[...] = sum(
            lax.dot_general(small[:, :ranks], a, CONTRACT_FIRST, preferred_element_type=F32)
            for a, small in zip(up_rows, smalls)
        )

    @pl.when(table[0] == 0)
    def _():
        grads = []
        for at in range(replicas):
            inverse = smalls[at][:, 2 * ranks : 2 * ranks + 1].astype(F32)
            toward = smalls[at][:, 2 * ranks + 64 : 2 * ranks + 65].astype(F32)
            grads.append(
                (
                    cotangent[at][...].astype(F32)
                    + inverse * pulled[at][...].astype(F32)
                    - toward * hidden[at][...].astype(F32)
                ).astype(BF16)
            )
        products([a[...] for a in early], grads)

    @pl.when(table[0] == 1)
    def _():
        scaled = [(a[...].astype(F32) * gain_ref[...]).astype(BF16) for a in hidden]
        products(scaled, [a[...] for a in early])


def gradients(table, gain_row, early, cotangent, pulled, hidden, smalls, ranks):
    replicas = len(early)
    rows, width = early[0].shape
    tile = min(512, width)
    columns = pl.BlockSpec((rows, tile), lambda step, table: (0, step))
    small = pl.BlockSpec(smalls[0].shape, lambda step, table: (0, 0))
    return pl.pallas_call(
        functools.partial(gradient_kernel, replicas=replicas),
        grid_spec=pltpu.PrefetchScalarGridSpec(
            num_scalar_prefetch=1,
            grid=(width // tile,),
            in_specs=[pl.BlockSpec((1, tile), lambda step, table: (0, step))]
            + [columns] * (4 * replicas)
            + [small] * replicas,
            out_specs=[
                pl.BlockSpec((tile, ranks), lambda step, table: (step, 0)),
                pl.BlockSpec((ranks, tile), lambda step, table: (0, step)),
            ],
        ),
        out_shape=[
            jax.ShapeDtypeStruct((width, ranks), F32),
            jax.ShapeDtypeStruct((ranks, width), F32),
        ],
        compiler_params=pltpu.CompilerParams(vmem_limit_bytes=24 * 1024 * 1024),
        cost_estimate=pl.CostEstimate(
            flops=4 * replicas * rows * width * ranks,
            bytes_accessed=8 * width * ranks + 8 * replicas * rows * width,
            transcendentals=0,
        ),
    )(table, gain_row, *early, *cotangent, *pulled, *hidden, *smalls)


def orders(count):
    first, first_slots, second, second_slots = [], [], [], []
    for z in range(count):
        sends = [(slot, 0, count - slot + z) for slot in range(z + 1, count)]
        sends += [(slot, 1, slot - count + z) for slot in range(count - z, count)]
        sends.sort()
        first.append([block for _, _, block in sends] + [z])
        first_slots.append({(slot, side): at for at, (slot, side, _) in enumerate(sends)})
        arrivals = [(slot, 0, z - 1 - slot) for slot in range(z)]
        arrivals += [(slot, 1, z + 1 + slot) for slot in range(count - 1 - z)]
        arrivals.sort()
        second.append([z] + [block for _, _, block in arrivals])
        second_slots.append([None] + [(slot, side) for slot, side, _ in arrivals])
    return first, first_slots, second, second_slots


def pick(number, choice, cases):
    chosen = cases[0]
    for at in range(1, len(cases)):
        members = [device for device, wanted in enumerate(choice) if wanted == at]
        chosen = jnp.where(is_one_of(number, members), cases[at], chosen)
    return chosen


def sum_steps():
    count = lax.axis_size("tensor")
    return [1 << bit for bit in range(count.bit_length() - 1)]


def add_neighbour(value, distance):
    count = lax.axis_size("tensor")
    other = lax.ppermute(
        value.astype(BF16), "tensor", [(place, place ^ distance) for place in range(count)]
    )
    return value + other.astype(F32)


def with_other_replicas(value, sections=(0, 1)):
    count = lax.axis_size("replica")
    return [value] + [
        lax.ppermute(
            value,
            ("section", "replica"),
            [(s * count + r, s * count + (r + step) % count) for s in sections for r in range(count)],
        )
        for step in range(1, count)
    ]


def to_other_core(value, source):
    return lax.ppermute(value, "section", [(source, 1 - source)])


def on_device(
    tokens,
    cotangent,
    gain,
    frozen_base_weight,
    adapter_down_factors,
    adapter_up_factors,
    tenant_adapter_scale,
    row_tenant_owner,
):
    section = lax.axis_index("section")
    place = lax.axis_index("tensor")
    count = lax.axis_size("tensor")
    is_first = section == 0
    weight = frozen_base_weight[0]
    gain_row = gain[0][None, :]
    down = adapter_down_factors[0]
    up = adapter_up_factors[0]
    rows, width = tokens.shape
    features = width * count
    ranks = down.shape[1]

    tenant_of_column = jnp.arange(ranks, dtype=jnp.int32) // (ranks // TENANT_COUNT)
    coefficients = jnp.where(
        row_tenant_owner[:, None] == tenant_of_column[None, :],
        jnp.repeat(tenant_adapter_scale, ranks // TENANT_COUNT)[None, :],
        0.0,
    )

    first_order, first_slots, second_order, second_slots = orders(count)
    place_of = section * count + place
    table = jnp.stack([section, place_of]).astype(jnp.int32)

    def times_down(value):
        return jnp.dot(value, down, preferred_element_type=F32)

    def times_up_transposed(value):
        return lax.dot_general(value, up, CONTRACT_LAST, preferred_element_type=F32)

    def line(value, first_pairs, second_pairs, toward):
        pairs = [(2 * z, 2 * (z + toward)) for z in first_pairs] + [
            (2 * z + 1, 2 * (z + toward) + 1) for z in second_pairs
        ]
        return lax.ppermute(value, ("tensor", "section"), pairs)

    token_float = tokens.astype(F32)
    early = lax.optimization_barrier(
        jnp.where(is_first, (token_float * gain_row).astype(BF16), cotangent)
    )

    everyone = range(count)
    arrivals = [
        (
            line(cotangent, [], [z for z in everyone if z + 1 < count], 1),
            line(cotangent, [], [z for z in everyone if z > 0], -1),
        )
    ]
    early_all = with_other_replicas(early)

    parts = []
    small_sum = None
    steps_left = sum_steps()
    for stage in range(count):
        wanted = [None if stage == 0 else second_slots[z][stage] for z in everyone]
        cases = sorted({slot for slot in wanted if slot is not None})
        here = [early] + [arrivals[slot][side] for slot, side in cases]
        if stage == 1:
            after, again, *_ = lax.optimization_barrier((cotangent, early, *sent))
            squares = jnp.sum(token_float * token_float, axis=1, keepdims=True)
            small_sum = jnp.concatenate(
                [
                    times_up_transposed(after),
                    times_down(again),
                    jnp.broadcast_to(squares, (rows, 128)),
                ],
                axis=1,
            )
        elif stage > 1 and steps_left:
            small_sum = add_neighbour(small_sum, steps_left.pop(0))
        if stage == 2:
            cotangent_all = [cotangent] + [to_other_core(other, 1) for other in early_all[1:]]
        if stage == 3:
            small_sum, *cotangent_all = lax.optimization_barrier((small_sum, *cotangent_all))
        if stage > 0:
            *here, small_sum = lax.optimization_barrier((*here, small_sum, *sent))[: len(here) + 1]
        value = pick(
            place_of,
            [0] * count + [0 if slot is None else 1 + cases.index(slot) for slot in wanted],
            here,
        )
        order = [blocks[stage] for blocks in first_order + second_order]
        part = block_product(table, value, weight, order)
        parts.append(part)
        slot = stage + 1
        if slot == count:
            break
        sent = []
        for side in (0, 1):
            needed = [first_slots[z].get((slot, side)) for z in everyone]
            stages = sorted({at for at in needed if at is not None})
            own = pick(
                place_of,
                [0 if at is None else stages.index(at) for at in needed] + [0] * count,
                [parts[at] for at in stages],
            )
            arrived = arrivals[-1][side].astype(F32)
            sent.append((arrived + jnp.where(is_first, own, 0.0)).astype(BF16))
        arrivals.append(
            (
                line(
                    sent[0],
                    [z for z in everyone if z < slot and z + 1 < count],
                    [z for z in everyone if slot + 1 < count and z >= slot and z + 1 < count],
                    1,
                ),
                line(
                    sent[1],
                    [z for z in everyone if z >= count - slot and z > 0],
                    [z for z in everyone if slot + 1 < count and z < count - slot and z > 0],
                    -1,
                ),
            )
        )
    from_left, from_right = arrivals[-1]

    while steps_left:
        small_sum = add_neighbour(small_sum, steps_left.pop(0))
    rank_up, rank_down = small_sum[:, :ranks], small_sum[:, ranks : 2 * ranks]
    inv_first = lax.rsqrt(small_sum[:, 2 * ranks : 2 * ranks + 1] / features + EPSILON)
    small_early = (coefficients * jnp.where(is_first, rank_down, rank_up)).astype(BF16)
    low_product = jnp.where(
        is_first,
        jnp.dot(small_early, up, preferred_element_type=F32),
        lax.dot_general(small_early, down, CONTRACT_LAST, preferred_element_type=F32),
    )

    pulled = (gain_row * (sum(parts) + low_product)).astype(BF16)
    from_left, from_right, _ = lax.optimization_barrier((from_left, from_right, pulled))
    pulled = to_other_core(pulled, 1)
    pulled_all = with_other_replicas(pulled, (0,))
    pulled_rank = times_up_transposed(pulled)

    projected = parts[-1] + from_left.astype(F32) + from_right.astype(F32) + low_product
    hidden = (token_float + inv_first * projected).astype(BF16)
    hidden_here = jnp.where(is_first, hidden, to_other_core(hidden, 0))
    hidden_others = with_other_replicas(hidden, (0,))[1:]
    hidden_float = hidden_here.astype(F32)
    row_sums = [
        jnp.broadcast_to(jnp.sum(terms, axis=1, keepdims=True), (rows, 64))
        for terms in (hidden_float * hidden_float, hidden_float * pulled.astype(F32))
    ]
    hidden_rank = jnp.where(
        is_first,
        times_up_transposed(hidden_here),
        times_down((hidden_float * gain_row).astype(BF16)),
    )
    late_sum = jnp.concatenate([hidden_rank, pulled_rank, *row_sums], axis=1)
    for at, distance in enumerate(sum_steps()):
        late_sum = add_neighbour(late_sum, distance)
        if at == 0:
            late_sum, *pulled_all = lax.optimization_barrier((late_sum, *pulled_all))
    late_sum, *hidden_others = lax.optimization_barrier((late_sum, *hidden_others))
    hidden_all = [hidden_here] + [
        jnp.where(is_first, other, to_other_core(other, 0)) for other in hidden_others
    ]

    inv_second = lax.rsqrt(late_sum[:, 2 * ranks : 2 * ranks + 1] / features + EPSILON)
    toward_hidden = (
        late_sum[:, 2 * ranks + 64 : 2 * ranks + 65]
        * inv_second * inv_second * inv_second / features
    )
    hidden_rank, pulled_rank = late_sum[:, :ranks], late_sum[:, ranks : 2 * ranks]
    rank_late = jnp.where(
        is_first, rank_up + inv_second * pulled_rank - toward_hidden * hidden_rank, hidden_rank
    )
    row_scale = jnp.where(is_first, inv_first, inv_second)
    small_late = coefficients * rank_late * row_scale
    small_early = small_early.astype(F32) * row_scale
    smalls = jnp.concatenate(
        [
            jnp.where(is_first, small_early, small_late),
            jnp.where(is_first, small_late, small_early),
            jnp.broadcast_to(inv_second, (rows, 64)),
            jnp.broadcast_to(toward_hidden, (rows, 64)),
        ],
        axis=1,
    ).astype(BF16)
    grad_down, grad_up = gradients(
        table,
        gain_row,
        early_all,
        cotangent_all,
        pulled_all,
        hidden_all,
        with_other_replicas(smalls),
        ranks,
    )
    return (grad_down[None], grad_up[None])


def solution(mesh):
    return jax.shard_map(
        on_device,
        mesh=mesh,
        in_specs=(
            P(("groups", "replica"), "tensor"),
            P(("groups", "replica"), "tensor"),
            P("section", "tensor"),
            P("section", "tensor", None),
            P("section", "tensor", None),
            P("section", None, "tensor"),
            P(),
            P(("groups", "replica")),
        ),
        out_specs=(P("section", "tensor", "groups"), P("section", "groups", "tensor")),
        check_vma=False,
    )
```

```python
import functools

import jax
import jax.numpy as jnp
from jax import lax
from jax.experimental import pallas as pl
from jax.experimental.pallas import tpu as pltpu
from jax.sharding import PartitionSpec as P

TENANT_COUNT = 4
EPSILON = 1e-05
CONTRACT_LAST = (((1,), (1,)), ((), ()))
CONTRACT_FIRST = (((0,), (0,)), ((), ()))
BF16 = jnp.bfloat16
F32 = jnp.float32
AHEAD = 2


def is_one_of(number, members):
    return functools.reduce(jnp.logical_or, [number == member for member in members])


def look_up(number, values):
    found = values[0]
    for value in sorted(set(values) - {values[0]}):
        found = jnp.where(
            is_one_of(number, [at for at, other in enumerate(values) if other == value]), value, found
        )
    return found


def block_kernel(table, value_ref, weight_ref, out_ref, wide, tall, arrived, *, blocks, tile, tiles):
    section = table[0]
    block = look_up(table[1], blocks)
    step = pl.program_id(0)
    width = tile * tiles

    def copy_of(index, is_wide):
        whole = pl.ds(pl.multiple_of(block * width, width), width)
        part = pl.ds(pl.multiple_of(block * width + index * tile, tile), tile)
        if is_wide:
            return pltpu.make_async_copy(weight_ref.at[:, part], wide.at[index], arrived.at[index])
        rows = pl.ds(pl.multiple_of(index * tile, tile), tile)
        return pltpu.make_async_copy(weight_ref.at[rows, whole], tall.at[index], arrived.at[index])

    for number, is_wide in ((0, True), (1, False)):

        @pl.when(section == number)
        def _():
            @pl.when(step == 0)
            def _():
                for index in range(min(AHEAD, tiles)):
                    copy_of(index, is_wide).start()

            @pl.when(step + AHEAD < tiles)
            def _():
                copy_of(step + AHEAD, is_wide).start()

            copy_of(step, is_wide).wait()
            if is_wide:
                out_ref[...] = jnp.dot(value_ref[...], wide[step], preferred_element_type=F32)
            else:
                out_ref[...] = lax.dot_general(
                    value_ref[...], tall[step], CONTRACT_LAST, preferred_element_type=F32
                )


def block_product(table, value, weight, blocks):
    rows, width = value.shape
    tile = min(256, width)
    tiles = width // tile
    return pl.pallas_call(
        functools.partial(block_kernel, blocks=blocks, tile=tile, tiles=tiles),
        grid_spec=pltpu.PrefetchScalarGridSpec(
            num_scalar_prefetch=1,
            grid=(tiles,),
            in_specs=[
                pl.BlockSpec((rows, width), lambda step, table: (0, 0)),
                pl.BlockSpec(memory_space=pl.ANY),
            ],
            out_specs=pl.BlockSpec((rows, tile), lambda step, table: (0, step)),
            scratch_shapes=[
                pltpu.VMEM((tiles, width, tile), BF16),
                pltpu.VMEM((tiles, tile, width), BF16),
                pltpu.SemaphoreType.DMA((tiles,)),
            ],
        ),
        out_shape=jax.ShapeDtypeStruct((rows, width), F32),
        compiler_params=pltpu.CompilerParams(vmem_limit_bytes=24 * 1024 * 1024),
        cost_estimate=pl.CostEstimate(
            flops=8 * rows * width * width, bytes_accessed=2 * width * width, transcendentals=0
        ),
    )(table, value, weight)


def gradient_kernel(table, gain_ref, *refs, replicas):
    early, cotangent, pulled, hidden, small_early, small_late = (
        refs[kind * replicas : (kind + 1) * replicas] for kind in range(6)
    )
    down_ref, up_ref = refs[6 * replicas :]
    ranks = down_ref.shape[1]

    def products(down_rows, down_small, up_rows, up_small):
        down_ref[...] = sum(
            lax.dot_general(a, b, CONTRACT_FIRST, preferred_element_type=F32)
            for a, b in zip(down_rows, down_small)
        )
        up_ref[...] = sum(
            lax.dot_general(a, b, CONTRACT_FIRST, preferred_element_type=F32)
            for a, b in zip(up_small, up_rows)
        )

    late = [small[:, :ranks] for small in small_late]
    inverse = [small[:, ranks : ranks + 1].astype(F32) for small in small_late]
    toward = [small[:, ranks + 64 : ranks + 65].astype(F32) for small in small_late]

    @pl.when(table[0] == 0)
    def _():
        grads = [
            (
                cotangent[at][...].astype(F32)
                + inverse[at] * pulled[at][...].astype(F32)
                - toward[at] * hidden[at][...].astype(F32)
            ).astype(BF16)
            for at in range(replicas)
        ]
        products([a[...] for a in early], late, grads, [a[...] for a in small_early])

    @pl.when(table[0] == 1)
    def _():
        scaled = [(a[...].astype(F32) * gain_ref[...]).astype(BF16) for a in hidden]
        weighed = [
            (a[...].astype(F32) * inverse[at]).astype(BF16) for at, a in enumerate(small_early)
        ]
        products(scaled, weighed, [a[...] for a in early], late)


def gradients(table, gain_row, early, cotangent, pulled, hidden, small_early, small_late, ranks):
    replicas = len(early)
    rows, width = early[0].shape
    tile = min(512, width)
    columns = pl.BlockSpec((rows, tile), lambda step, table: (0, step))
    smalls = [*small_early, *small_late]
    return pl.pallas_call(
        functools.partial(gradient_kernel, replicas=replicas),
        grid_spec=pltpu.PrefetchScalarGridSpec(
            num_scalar_prefetch=1,
            grid=(width // tile,),
            in_specs=[pl.BlockSpec((1, tile), lambda step, table: (0, step))]
            + [columns] * (4 * replicas)
            + [pl.BlockSpec(small.shape, lambda step, table: (0, 0)) for small in smalls],
            out_specs=[
                pl.BlockSpec((tile, ranks), lambda step, table: (step, 0)),
                pl.BlockSpec((ranks, tile), lambda step, table: (0, step)),
            ],
        ),
        out_shape=[
            jax.ShapeDtypeStruct((width, ranks), F32),
            jax.ShapeDtypeStruct((ranks, width), F32),
        ],
        compiler_params=pltpu.CompilerParams(vmem_limit_bytes=24 * 1024 * 1024),
        cost_estimate=pl.CostEstimate(
            flops=4 * replicas * rows * width * ranks,
            bytes_accessed=8 * width * ranks + 8 * replicas * rows * width,
            transcendentals=0,
        ),
    )(table, gain_row, *early, *cotangent, *pulled, *hidden, *smalls)


def orders(count):
    first, first_slots, second, second_slots = [], [], [], []
    for z in range(count):
        sends = [(slot, 0, count - slot + z) for slot in range(z + 1, count)]
        sends += [(slot, 1, slot - count + z) for slot in range(count - z, count)]
        sends.sort()
        first.append([block for _, _, block in sends] + [z])
        first_slots.append({(slot, side): at for at, (slot, side, _) in enumerate(sends)})
        arrivals = [(slot, 0, z - 1 - slot) for slot in range(z)]
        arrivals += [(slot, 1, z + 1 + slot) for slot in range(count - 1 - z)]
        arrivals.sort()
        second.append([z] + [block for _, _, block in arrivals])
        second_slots.append([None] + [(slot, side) for slot, side, _ in arrivals])
    return first, first_slots, second, second_slots


def pick(number, choice, cases):
    chosen = cases[0]
    for at in range(1, len(cases)):
        members = [device for device, wanted in enumerate(choice) if wanted == at]
        chosen = jnp.where(is_one_of(number, members), cases[at], chosen)
    return chosen


def doubling_steps():
    count = lax.axis_size("tensor")
    return [
        ([(place, place ^ (1 << bit)) for place in range(count)], True)
        for bit in range(count.bit_length() - 1)
    ]


def line_steps():
    if lax.axis_size("tensor") != 4:
        return doubling_steps()
    return [([(0, 1), (3, 2)], True), ([(1, 2), (2, 1)], True), ([(1, 0), (2, 3)], False)]


def sum_step(value, step, wire=BF16):
    pairs, adds = step
    other = lax.ppermute(value.astype(wire), "tensor", pairs).astype(F32)
    if adds:
        return value + other
    takes = is_one_of(lax.axis_index("tensor"), [target for _, target in pairs])
    return jnp.where(takes, other, value)


def with_other_replicas(value, sections=(0, 1)):
    count = lax.axis_size("replica")
    return [value] + [
        lax.ppermute(
            value,
            ("section", "replica"),
            [(s * count + r, s * count + (r + step) % count) for s in sections for r in range(count)],
        )
        for step in range(1, count)
    ]


def to_other_core(value, source):
    return lax.ppermute(value, "section", [(source, 1 - source)])


def on_device(
    tokens,
    cotangent,
    gain,
    frozen_base_weight,
    adapter_down_factors,
    adapter_up_factors,
    tenant_adapter_scale,
    row_tenant_owner,
):
    section = lax.axis_index("section")
    place = lax.axis_index("tensor")
    count = lax.axis_size("tensor")
    is_first = section == 0
    weight = frozen_base_weight[0]
    gain_row = gain[0][None, :]
    down = adapter_down_factors[0]
    up = adapter_up_factors[0]
    rows, width = tokens.shape
    features = width * count
    ranks = down.shape[1]

    tenant_of_column = jnp.arange(ranks, dtype=jnp.int32) // (ranks // TENANT_COUNT)
    coefficients = jnp.where(
        row_tenant_owner[:, None] == tenant_of_column[None, :],
        jnp.repeat(tenant_adapter_scale, ranks // TENANT_COUNT)[None, :],
        0.0,
    )

    first_order, first_slots, second_order, second_slots = orders(count)
    place_of = section * count + place
    table = jnp.stack([section, place_of]).astype(jnp.int32)

    def times_down(value):
        return jnp.dot(value, down, preferred_element_type=F32)

    def times_up_transposed(value):
        return lax.dot_general(value, up, CONTRACT_LAST, preferred_element_type=F32)

    def line(value, first_pairs, second_pairs, toward):
        pairs = [(2 * z, 2 * (z + toward)) for z in first_pairs] + [
            (2 * z + 1, 2 * (z + toward) + 1) for z in second_pairs
        ]
        return lax.ppermute(value, ("tensor", "section"), pairs)

    token_float = tokens.astype(F32)
    early = lax.optimization_barrier(
        jnp.where(is_first, (token_float * gain_row).astype(BF16), cotangent)
    )

    everyone = range(count)
    arrivals = [
        (
            line(cotangent, [], [z for z in everyone if z + 1 < count], 1),
            line(cotangent, [], [z for z in everyone if z > 0], -1),
        )
    ]
    parts = []
    small_sum = None
    steps_left = line_steps()
    for stage in range(count):
        wanted = [None if stage == 0 else second_slots[z][stage] for z in everyone]
        cases = sorted({slot for slot in wanted if slot is not None})
        here = [early] + [arrivals[slot][side] for slot, side in cases]
        if stage == 1:
            after, plain, *_ = lax.optimization_barrier((early, tokens, *sent))
            plain = plain.astype(F32)
            squares = jnp.sum(plain * plain, axis=1, keepdims=True)
            small_sum = jnp.concatenate(
                [
                    jnp.where(is_first, times_down(after), times_up_transposed(after)),
                    jnp.broadcast_to(squares, (rows, 128)),
                ],
                axis=1,
            )
        elif stage > 1 and steps_left:
            small_sum = sum_step(small_sum, steps_left.pop(0))
        if stage == 2:
            cotangent_all = [cotangent] + [to_other_core(other, 1) for other in early_all[1:]]
        if stage == 3:
            small_sum, *cotangent_all = lax.optimization_barrier((small_sum, *cotangent_all))
        if stage > 0:
            *here, small_sum = lax.optimization_barrier((*here, small_sum, *sent))[: len(here) + 1]
        value = pick(
            place_of,
            [0] * count + [0 if slot is None else 1 + cases.index(slot) for slot in wanted],
            here,
        )
        order = [blocks[stage] for blocks in first_order + second_order]
        part = block_product(table, value, weight, order)
        if stage == 0:
            part, after = lax.optimization_barrier((part, early))
            early_all = [early] + with_other_replicas(after)[1:]
        parts.append(part)
        slot = stage + 1
        if slot == count:
            break
        sent = []
        for side in (0, 1):
            needed = [first_slots[z].get((slot, side)) for z in everyone]
            stages = sorted({at for at in needed if at is not None})
            own = pick(
                place_of,
                [0 if at is None else stages.index(at) for at in needed] + [0] * count,
                [parts[at] for at in stages],
            )
            arrived = arrivals[-1][side].astype(F32)
            sent.append((arrived + jnp.where(is_first, own, 0.0)).astype(BF16))
        arrivals.append(
            (
                line(
                    sent[0],
                    [z for z in everyone if z < slot and z + 1 < count],
                    [z for z in everyone if slot + 1 < count and z >= slot and z + 1 < count],
                    1,
                ),
                line(
                    sent[1],
                    [z for z in everyone if z >= count - slot and z > 0],
                    [z for z in everyone if slot + 1 < count and z < count - slot and z > 0],
                    -1,
                ),
            )
        )
    from_left, from_right = arrivals[-1]

    while steps_left:
        small_sum = sum_step(small_sum, steps_left.pop(0))
    inv_first = lax.rsqrt(small_sum[:, ranks : ranks + 1] / features + EPSILON)
    small_early = (coefficients * small_sum[:, :ranks]).astype(BF16)
    low_product = jnp.where(
        is_first,
        jnp.dot(small_early, up, preferred_element_type=F32),
        lax.dot_general(small_early, down, CONTRACT_LAST, preferred_element_type=F32),
    )
    small_early_all = with_other_replicas(
        (small_early.astype(F32) * jnp.where(is_first, inv_first, 1.0)).astype(BF16)
    )

    pulled = (gain_row * (sum(parts) + low_product)).astype(BF16)
    from_left, from_right, *small_early_all, _ = lax.optimization_barrier(
        (from_left, from_right, *small_early_all, pulled)
    )
    pulled_others = with_other_replicas(pulled, (1,))[1:]
    pulled = to_other_core(pulled, 1)

    projected = parts[-1] + from_left.astype(F32) + from_right.astype(F32) + low_product
    hidden = (token_float + inv_first * projected).astype(BF16)
    hidden_here = jnp.where(is_first, hidden, to_other_core(hidden, 0))
    hidden_others = with_other_replicas(hidden, (0,))[1:]
    hidden_float = hidden_here.astype(F32)
    pulled_float = pulled.astype(F32)
    row_sums = jnp.stack(
        [jnp.sum(hidden_float * hidden_float, axis=1), jnp.sum(hidden_float * pulled_float, axis=1)]
    )
    for at, step in enumerate(doubling_steps()):
        row_sums = sum_step(row_sums, step, F32)
        if at == 0:
            row_sums, *pulled_others = lax.optimization_barrier((row_sums, *pulled_others))
    inv_second = lax.rsqrt(row_sums[0] / features + EPSILON)[:, None]
    toward_hidden = row_sums[1][:, None] * inv_second * inv_second * inv_second / features
    hidden_grad = cotangent.astype(F32) + inv_second * pulled_float - toward_hidden * hidden_float
    rank_late = jnp.where(
        is_first,
        times_up_transposed(hidden_grad.astype(BF16)),
        times_down((hidden_float * gain_row).astype(BF16)),
    )
    for step in doubling_steps():
        rank_late = sum_step(rank_late, step)

    rank_late, *swapped = lax.optimization_barrier(
        (
            rank_late,
            *[jnp.where(is_first, *pair) for pair in zip(hidden_others, pulled_others)],
        )
    )
    swapped = [lax.ppermute(other, "section", [(0, 1), (1, 0)]) for other in swapped]
    hidden_all = [hidden_here] + [
        jnp.where(is_first, *pair) for pair in zip(hidden_others, swapped)
    ]
    pulled_all = [pulled] + swapped

    small_late = coefficients * rank_late * jnp.where(is_first, inv_first, inv_second)
    smalls = jnp.concatenate(
        [
            small_late,
            jnp.broadcast_to(inv_second, (rows, 64)),
            jnp.broadcast_to(toward_hidden, (rows, 64)),
        ],
        axis=1,
    ).astype(BF16)
    grad_down, grad_up = gradients(
        table,
        gain_row,
        early_all,
        cotangent_all,
        pulled_all,
        hidden_all,
        small_early_all,
        with_other_replicas(smalls),
        ranks,
    )
    return (grad_down[None], grad_up[None])


def solution(mesh):
    return jax.shard_map(
        on_device,
        mesh=mesh,
        in_specs=(
            P(("groups", "replica"), "tensor"),
            P(("groups", "replica"), "tensor"),
            P("section", "tensor"),
            P("section", "tensor", None),
            P("section", "tensor", None),
            P("section", None, "tensor"),
            P(),
            P(("groups", "replica")),
        ),
        out_specs=(P("section", "tensor", "groups"), P("section", "groups", "tensor")),
        check_vma=False,
    )
```

```python
import functools

import jax
import jax.numpy as jnp
from jax import lax
from jax.experimental import pallas as pl
from jax.experimental.pallas import tpu as pltpu
from jax.sharding import PartitionSpec as P

TENANT_COUNT = 4
EPSILON = 1e-05
CONTRACT_LAST = (((1,), (1,)), ((), ()))
CONTRACT_FIRST = (((0,), (0,)), ((), ()))
BF16 = jnp.bfloat16
F32 = jnp.float32
AHEAD = 2


def is_one_of(number, members):
    return functools.reduce(jnp.logical_or, [number == member for member in members])


def look_up(number, values):
    found = values[0]
    for value in sorted(set(values) - {values[0]}):
        found = jnp.where(
            is_one_of(number, [at for at, other in enumerate(values) if other == value]), value, found
        )
    return found


def block_kernel(
    table, value_ref, riding_ref, weight_ref, out_ref, wide, tall, arrived, *, blocks, tile, tiles
):
    section = table[0]
    block = look_up(table[1], blocks)
    step = pl.program_id(0)
    width = tile * tiles

    def copy_of(index, is_wide):
        whole = pl.ds(pl.multiple_of(block * width, width), width)
        part = pl.ds(pl.multiple_of(block * width + index * tile, tile), tile)
        if is_wide:
            return pltpu.make_async_copy(weight_ref.at[:, part], wide.at[index], arrived.at[index])
        rows = pl.ds(pl.multiple_of(index * tile, tile), tile)
        return pltpu.make_async_copy(weight_ref.at[rows, whole], tall.at[index], arrived.at[index])

    @pl.when(step == 0)
    def _():
        out_ref[:, width:] = riding_ref[...]

    columns = pl.ds(pl.multiple_of(step * tile, tile), tile)
    for number, is_wide in ((0, True), (1, False)):

        @pl.when(section == number)
        def _():
            @pl.when(step == 0)
            def _():
                for index in range(min(AHEAD, tiles)):
                    copy_of(index, is_wide).start()

            @pl.when(step + AHEAD < tiles)
            def _():
                copy_of(step + AHEAD, is_wide).start()

            copy_of(step, is_wide).wait()
            if is_wide:
                out_ref[:, columns] = jnp.dot(
                    value_ref[:, :width], wide[step], preferred_element_type=F32
                )
            else:
                out_ref[:, columns] = lax.dot_general(
                    value_ref[:, :width], tall[step], CONTRACT_LAST, preferred_element_type=F32
                )


def block_product(table, value, riding, weight, blocks):
    rows, columns = value.shape
    width = columns - riding.shape[1]
    tile = min(256, width)
    tiles = width // tile
    return pl.pallas_call(
        functools.partial(block_kernel, blocks=blocks, tile=tile, tiles=tiles),
        grid_spec=pltpu.PrefetchScalarGridSpec(
            num_scalar_prefetch=1,
            grid=(tiles,),
            in_specs=[
                pl.BlockSpec(value.shape, lambda step, table: (0, 0)),
                pl.BlockSpec(riding.shape, lambda step, table: (0, 0)),
                pl.BlockSpec(memory_space=pl.ANY),
            ],
            out_specs=pl.BlockSpec(value.shape, lambda step, table: (0, 0)),
            scratch_shapes=[
                pltpu.VMEM((tiles, width, tile), BF16),
                pltpu.VMEM((tiles, tile, width), BF16),
                pltpu.SemaphoreType.DMA((tiles,)),
            ],
        ),
        out_shape=jax.ShapeDtypeStruct(value.shape, F32),
        compiler_params=pltpu.CompilerParams(vmem_limit_bytes=28 * 1024 * 1024),
        cost_estimate=pl.CostEstimate(
            flops=8 * rows * width * width, bytes_accessed=2 * width * width, transcendentals=0
        ),
    )(table, value, riding, weight)


def gradient_kernel(table, gain_ref, *refs, replicas):
    early, cotangent, pulled, hidden, smalls = (
        refs[kind * replicas : (kind + 1) * replicas] for kind in range(5)
    )
    down_ref, up_ref = refs[5 * replicas :]
    ranks = down_ref.shape[1]

    def products(down_rows, up_rows):
        down_ref[...] = sum(
            lax.dot_general(a, small[:, ranks : 2 * ranks], CONTRACT_FIRST, preferred_element_type=F32)
            for a, small in zip(down_rows, smalls)
        )
        up_ref[...] = sum(
            lax.dot_general(small[:, :ranks], a, CONTRACT_FIRST, preferred_element_type=F32)
            for a, small in zip(up_rows, smalls)
        )

    @pl.when(table[0] == 0)
    def _():
        grads = []
        for at in range(replicas):
            inverse = smalls[at][:, 2 * ranks : 2 * ranks + 1].astype(F32)
            toward = smalls[at][:, 2 * ranks + 64 : 2 * ranks + 65].astype(F32)
            grads.append(
                (
                    cotangent[at][...].astype(F32)
                    + inverse * pulled[at][...].astype(F32)
                    - toward * hidden[at][...].astype(F32)
                ).astype(BF16)
            )
        products([a[...] for a in early], grads)

    @pl.when(table[0] == 1)
    def _():
        scaled = [(a[...].astype(F32) * gain_ref[...]).astype(BF16) for a in hidden]
        products(scaled, [a[...] for a in early])


def gradients(table, gain_row, early, cotangent, pulled, hidden, smalls, ranks):
    replicas = len(early)
    rows, width = early[0].shape
    tile = min(512, width)
    columns = pl.BlockSpec((rows, tile), lambda step, table: (0, step))
    small = pl.BlockSpec(smalls[0].shape, lambda step, table: (0, 0))
    return pl.pallas_call(
        functools.partial(gradient_kernel, replicas=replicas),
        grid_spec=pltpu.PrefetchScalarGridSpec(
            num_scalar_prefetch=1,
            grid=(width // tile,),
            in_specs=[pl.BlockSpec((1, tile), lambda step, table: (0, step))]
            + [columns] * (4 * replicas)
            + [small] * replicas,
            out_specs=[
                pl.BlockSpec((tile, ranks), lambda step, table: (step, 0)),
                pl.BlockSpec((ranks, tile), lambda step, table: (0, step)),
            ],
        ),
        out_shape=[
            jax.ShapeDtypeStruct((width, ranks), F32),
            jax.ShapeDtypeStruct((ranks, width), F32),
        ],
        compiler_params=pltpu.CompilerParams(vmem_limit_bytes=24 * 1024 * 1024),
        cost_estimate=pl.CostEstimate(
            flops=4 * replicas * rows * width * ranks,
            bytes_accessed=8 * width * ranks + 8 * replicas * rows * width,
            transcendentals=0,
        ),
    )(table, gain_row, *early, *cotangent, *pulled, *hidden, *smalls)


def orders(count):
    first, first_slots, second, second_slots = [], [], [], []
    for z in range(count):
        sends = [(slot, 0, count - slot + z) for slot in range(z + 1, count)]
        sends += [(slot, 1, slot - count + z) for slot in range(count - z, count)]
        sends.sort()
        first.append([block for _, _, block in sends] + [z])
        first_slots.append({(slot, side): at for at, (slot, side, _) in enumerate(sends)})
        arrivals = [(slot, 0, z - 1 - slot) for slot in range(z)]
        arrivals += [(slot, 1, z + 1 + slot) for slot in range(count - 1 - z)]
        arrivals.sort()
        second.append([z] + [block for _, _, block in arrivals])
        second_slots.append([None] + [(slot, side) for slot, side, _ in arrivals])
    return first, first_slots, second, second_slots


def pick(number, choice, cases):
    chosen = cases[0]
    for at in range(1, len(cases)):
        members = [device for device, wanted in enumerate(choice) if wanted == at]
        chosen = jnp.where(is_one_of(number, members), cases[at], chosen)
    return chosen


def doubling_steps():
    count = lax.axis_size("tensor")
    return [
        [(place, place ^ (1 << bit)) for place in range(count)]
        for bit in range(count.bit_length() - 1)
    ]


def sum_step(value, pairs, wire=BF16):
    return value + lax.ppermute(value.astype(wire), "tensor", pairs).astype(F32)


def with_other_replicas(value, sections=(0, 1)):
    count = lax.axis_size("replica")
    return [value] + [
        lax.ppermute(
            value,
            ("section", "replica"),
            [(s * count + r, s * count + (r + step) % count) for s in sections for r in range(count)],
        )
        for step in range(1, count)
    ]


def to_other_core(value, source):
    return lax.ppermute(value, "section", [(source, 1 - source)])


def on_device(
    tokens,
    cotangent,
    gain,
    frozen_base_weight,
    adapter_down_factors,
    adapter_up_factors,
    tenant_adapter_scale,
    row_tenant_owner,
):
    section = lax.axis_index("section")
    place = lax.axis_index("tensor")
    count = lax.axis_size("tensor")
    is_first = section == 0
    weight = frozen_base_weight[0]
    gain_row = gain[0][None, :]
    down = adapter_down_factors[0]
    up = adapter_up_factors[0]
    rows, width = tokens.shape
    features = width * count
    ranks = down.shape[1]

    tenant_of_column = jnp.arange(ranks, dtype=jnp.int32) // (ranks // TENANT_COUNT)
    coefficients = jnp.where(
        row_tenant_owner[:, None] == tenant_of_column[None, :],
        jnp.repeat(tenant_adapter_scale, ranks // TENANT_COUNT)[None, :],
        0.0,
    )

    first_order, first_slots, second_order, second_slots = orders(count)
    place_of = section * count + place
    table = jnp.stack([section, place_of]).astype(jnp.int32)

    def times_down(value):
        return jnp.dot(value, down, preferred_element_type=F32)

    def times_up_transposed(value):
        return lax.dot_general(value, up, CONTRACT_LAST, preferred_element_type=F32)

    def line(value, first_pairs, second_pairs, toward):
        pairs = [(2 * z, 2 * (z + toward)) for z in first_pairs] + [
            (2 * z + 1, 2 * (z + toward) + 1) for z in second_pairs
        ]
        return lax.ppermute(value, ("tensor", "section"), pairs)

    token_float = tokens.astype(F32)
    early = jnp.where(is_first, (token_float * gain_row).astype(BF16), cotangent)
    riding = jnp.concatenate(
        [
            jnp.where(is_first, times_down(early), times_up_transposed(early)),
            jnp.broadcast_to(jnp.sum(token_float * token_float, axis=1, keepdims=True), (rows, 128)),
        ],
        axis=1,
    )
    first = jnp.concatenate([early, riding.astype(BF16)], axis=1)
    early, riding, first = lax.optimization_barrier((early, riding, first))

    everyone = range(count)
    arrivals = [
        (
            line(first, [], [z for z in everyone if z + 1 < count], 1),
            line(first, [], [z for z in everyone if z > 0], -1),
        )
    ]
    parts = []
    for stage in range(count):
        wanted = [None if stage == 0 else second_slots[z][stage] for z in everyone]
        cases = sorted({slot for slot in wanted if slot is not None})
        here = [first] + [arrivals[slot][side] for slot, side in cases]
        if stage > 0:
            here = lax.optimization_barrier((*here, *sent))[: len(here)]
        value = pick(
            place_of,
            [0] * count + [0 if slot is None else 1 + cases.index(slot) for slot in wanted],
            here,
        )
        order = [blocks[stage] for blocks in first_order + second_order]
        part = block_product(table, value, riding, weight, order)
        if stage == 0:
            part, after = lax.optimization_barrier((part, early))
            early_all = [early] + with_other_replicas(after)[1:]
        if stage == 2:
            part, *early_all = lax.optimization_barrier((part, *early_all))
        parts.append(part)
        slot = stage + 1
        if slot == count:
            break
        sent = []
        for side in (0, 1):
            needed = [first_slots[z].get((slot, side)) for z in everyone]
            stages = sorted({at for at in needed if at is not None})
            own = pick(
                place_of,
                [0 if at is None else stages.index(at) for at in needed] + [0] * count,
                [parts[at] for at in stages],
            )
            arrived = arrivals[-1][side].astype(F32)
            sent.append((arrived + jnp.where(is_first, own, 0.0)).astype(BF16))
        arrivals.append(
            (
                line(
                    sent[0],
                    [z for z in everyone if z < slot and z + 1 < count],
                    [z for z in everyone if slot + 1 < count and z >= slot and z + 1 < count],
                    1,
                ),
                line(
                    sent[1],
                    [z for z in everyone if z >= count - slot and z > 0],
                    [z for z in everyone if slot + 1 < count and z < count - slot and z > 0],
                    -1,
                ),
            )
        )
    from_left, from_right = arrivals[-1]

    passed = sum(
        (arrived[:, width:].astype(F32) for pair in arrivals[:-1] for arrived in pair), riding
    )

    def small_factor(rank_sum):
        return (coefficients * rank_sum).astype(BF16)

    small_second = small_factor(passed[:, :ranks])

    pulled = sum(part[:, :width] for part in parts) + lax.dot_general(
        small_second, down, CONTRACT_LAST, preferred_element_type=F32
    )
    pulled = (gain_row * pulled).astype(BF16)
    pulled_others = with_other_replicas(pulled, (1,))[1:]
    pulled = to_other_core(pulled, 1)
    from_left, from_right, pulled = lax.optimization_barrier((from_left, from_right, pulled))

    summed = parts[-1] + from_left.astype(F32) + from_right.astype(F32)
    small_first = small_factor(summed[:, width : width + ranks])
    inv_first = lax.rsqrt(summed[:, width + ranks : width + ranks + 1] / features + EPSILON)
    projected = summed[:, :width] + jnp.dot(small_first, up, preferred_element_type=F32)
    hidden = (token_float + inv_first * projected).astype(BF16)
    swap = [(0, 1), (1, 0)]
    swapped = [
        lax.ppermute(jnp.where(is_first, hidden, other), "section", swap) for other in early_all[1:]
    ]
    hidden_on_second = swapped[0] if swapped else to_other_core(hidden, 0)
    cotangent_all = [cotangent] + swapped
    hidden_here = jnp.where(is_first, hidden, hidden_on_second)
    small_early = jnp.where(is_first, small_first, small_second)
    hidden_others = with_other_replicas(hidden, (0,))[1:]
    hidden_float = hidden_here.astype(F32)
    pulled_float = pulled.astype(F32)
    row_sums = jnp.stack(
        [jnp.sum(hidden_float * hidden_float, axis=1), jnp.sum(hidden_float * pulled_float, axis=1)]
    )
    for step in doubling_steps():
        row_sums = sum_step(row_sums, step, F32)
    inv_second = lax.rsqrt(row_sums[0] / features + EPSILON)[:, None]
    toward_hidden = row_sums[1][:, None] * inv_second * inv_second * inv_second / features
    hidden_grad = cotangent.astype(F32) + inv_second * pulled_float - toward_hidden * hidden_float
    rank_late = jnp.where(
        is_first,
        times_up_transposed(hidden_grad.astype(BF16)),
        times_down((hidden_float * gain_row).astype(BF16)),
    )
    for at, step in enumerate(doubling_steps()):
        rank_late = sum_step(rank_late, step)
        if at == 0:
            rank_late, *pulled_others = lax.optimization_barrier((rank_late, *pulled_others))

    rank_late, *swapped = lax.optimization_barrier(
        (
            rank_late,
            *[jnp.where(is_first, *pair) for pair in zip(hidden_others, pulled_others)],
        )
    )
    swapped = [lax.ppermute(other, "section", swap) for other in swapped]
    hidden_all = [hidden_here] + [
        jnp.where(is_first, *pair) for pair in zip(hidden_others, swapped)
    ]
    pulled_all = [pulled] + swapped

    row_scale = jnp.where(is_first, inv_first, inv_second)
    small_late = coefficients * rank_late * row_scale
    small_early = small_early.astype(F32) * row_scale
    smalls = jnp.concatenate(
        [
            jnp.where(is_first, small_early, small_late),
            jnp.where(is_first, small_late, small_early),
            jnp.broadcast_to(inv_second, (rows, 64)),
            jnp.broadcast_to(toward_hidden, (rows, 64)),
        ],
        axis=1,
    ).astype(BF16)
    grad_down, grad_up = gradients(
        table,
        gain_row,
        early_all,
        cotangent_all,
        pulled_all,
        hidden_all,
        with_other_replicas(smalls),
        ranks,
    )
    return (grad_down[None], grad_up[None])


def solution(mesh):
    return jax.shard_map(
        on_device,
        mesh=mesh,
        in_specs=(
            P(("groups", "replica"), "tensor"),
            P(("groups", "replica"), "tensor"),
            P("section", "tensor"),
            P("section", "tensor", None),
            P("section", "tensor", None),
            P("section", None, "tensor"),
            P(),
            P(("groups", "replica")),
        ),
        out_specs=(P("section", "tensor", "groups"), P("section", "groups", "tensor")),
        check_vma=False,
    )
```

```python
import functools

import jax
import jax.numpy as jnp
from jax import lax
from jax.experimental import pallas as pl
from jax.experimental.pallas import tpu as pltpu
from jax.sharding import PartitionSpec as P

TENANT_COUNT = 4
EPSILON = 1e-05
CONTRACT_LAST = (((1,), (1,)), ((), ()))
CONTRACT_FIRST = (((0,), (0,)), ((), ()))
BF16 = jnp.bfloat16
F32 = jnp.float32
AHEAD = 2


def is_one_of(number, members):
    return functools.reduce(jnp.logical_or, [number == member for member in members])


def look_up(number, values):
    found = values[0]
    for value in sorted(set(values) - {values[0]}):
        found = jnp.where(
            is_one_of(number, [at for at, other in enumerate(values) if other == value]), value, found
        )
    return found


def block_kernel(table, value_ref, weight_ref, out_ref, wide, tall, arrived, *, blocks, tile, tiles):
    section = table[0]
    block = look_up(table[1], blocks)
    step = pl.program_id(0)
    width = tile * tiles

    def copy_of(index, is_wide):
        whole = pl.ds(pl.multiple_of(block * width, width), width)
        part = pl.ds(pl.multiple_of(block * width + index * tile, tile), tile)
        if is_wide:
            return pltpu.make_async_copy(weight_ref.at[:, part], wide.at[index], arrived.at[index])
        rows = pl.ds(pl.multiple_of(index * tile, tile), tile)
        return pltpu.make_async_copy(weight_ref.at[rows, whole], tall.at[index], arrived.at[index])

    for number, is_wide in ((0, True), (1, False)):

        @pl.when(section == number)
        def _():
            @pl.when(step == 0)
            def _():
                for index in range(min(AHEAD, tiles)):
                    copy_of(index, is_wide).start()

            @pl.when(step + AHEAD < tiles)
            def _():
                copy_of(step + AHEAD, is_wide).start()

            copy_of(step, is_wide).wait()
            if is_wide:
                out_ref[...] = jnp.dot(value_ref[...], wide[step], preferred_element_type=F32)
            else:
                out_ref[...] = lax.dot_general(
                    value_ref[...], tall[step], CONTRACT_LAST, preferred_element_type=F32
                )


def block_product(table, value, weight, blocks):
    rows, width = value.shape
    tile = min(256, width)
    tiles = width // tile
    return pl.pallas_call(
        functools.partial(block_kernel, blocks=blocks, tile=tile, tiles=tiles),
        grid_spec=pltpu.PrefetchScalarGridSpec(
            num_scalar_prefetch=1,
            grid=(tiles,),
            in_specs=[
                pl.BlockSpec((rows, width), lambda step, table: (0, 0)),
                pl.BlockSpec(memory_space=pl.ANY),
            ],
            out_specs=pl.BlockSpec((rows, tile), lambda step, table: (0, step)),
            scratch_shapes=[
                pltpu.VMEM((tiles, width, tile), BF16),
                pltpu.VMEM((tiles, tile, width), BF16),
                pltpu.SemaphoreType.DMA((tiles,)),
            ],
        ),
        out_shape=jax.ShapeDtypeStruct((rows, width), F32),
        compiler_params=pltpu.CompilerParams(vmem_limit_bytes=24 * 1024 * 1024),
        cost_estimate=pl.CostEstimate(
            flops=8 * rows * width * width, bytes_accessed=2 * width * width, transcendentals=0
        ),
    )(table, value, weight)


def gradient_kernel(table, gain_ref, *refs, replicas):
    early, cotangent, pulled, hidden, smalls = (
        refs[kind * replicas : (kind + 1) * replicas] for kind in range(5)
    )
    down_ref, up_ref = refs[5 * replicas :]
    ranks = down_ref.shape[1]

    def products(down_rows, up_rows):
        down_ref[...] = sum(
            lax.dot_general(a, small[:, ranks : 2 * ranks], CONTRACT_FIRST, preferred_element_type=F32)
            for a, small in zip(down_rows, smalls)
        )
        up_ref[...] = sum(
            lax.dot_general(small[:, :ranks], a, CONTRACT_FIRST, preferred_element_type=F32)
            for a, small in zip(up_rows, smalls)
        )

    @pl.when(table[0] == 0)
    def _():
        grads = []
        for at in range(replicas):
            inverse = smalls[at][:, 2 * ranks : 2 * ranks + 1].astype(F32)
            toward = smalls[at][:, 2 * ranks + 64 : 2 * ranks + 65].astype(F32)
            grads.append(
                (
                    cotangent[at][...].astype(F32)
                    + inverse * pulled[at][...].astype(F32)
                    - toward * hidden[at][...].astype(F32)
                ).astype(BF16)
            )
        products([a[...] for a in early], grads)

    @pl.when(table[0] == 1)
    def _():
        scaled = [(a[...].astype(F32) * gain_ref[...]).astype(BF16) for a in hidden]
        products(scaled, [a[...] for a in early])


def gradients(table, gain_row, early, cotangent, pulled, hidden, smalls, ranks):
    replicas = len(early)
    rows, width = early[0].shape
    tile = min(512, width)
    columns = pl.BlockSpec((rows, tile), lambda step, table: (0, step))
    small = pl.BlockSpec(smalls[0].shape, lambda step, table: (0, 0))
    return pl.pallas_call(
        functools.partial(gradient_kernel, replicas=replicas),
        grid_spec=pltpu.PrefetchScalarGridSpec(
            num_scalar_prefetch=1,
            grid=(width // tile,),
            in_specs=[pl.BlockSpec((1, tile), lambda step, table: (0, step))]
            + [columns] * (4 * replicas)
            + [small] * replicas,
            out_specs=[
                pl.BlockSpec((tile, ranks), lambda step, table: (step, 0)),
                pl.BlockSpec((ranks, tile), lambda step, table: (0, step)),
            ],
        ),
        out_shape=[
            jax.ShapeDtypeStruct((width, ranks), F32),
            jax.ShapeDtypeStruct((ranks, width), F32),
        ],
        compiler_params=pltpu.CompilerParams(vmem_limit_bytes=24 * 1024 * 1024),
        cost_estimate=pl.CostEstimate(
            flops=4 * replicas * rows * width * ranks,
            bytes_accessed=8 * width * ranks + 8 * replicas * rows * width,
            transcendentals=0,
        ),
    )(table, gain_row, *early, *cotangent, *pulled, *hidden, *smalls)


def orders(count):
    first, first_slots, second, second_slots = [], [], [], []
    for z in range(count):
        sends = [(slot, 0, count - slot + z) for slot in range(z + 1, count)]
        sends += [(slot, 1, slot - count + z) for slot in range(count - z, count)]
        sends.sort()
        first.append([block for _, _, block in sends] + [z])
        first_slots.append({(slot, side): at for at, (slot, side, _) in enumerate(sends)})
        arrivals = [(slot, 0, z - 1 - slot) for slot in range(z)]
        arrivals += [(slot, 1, z + 1 + slot) for slot in range(count - 1 - z)]
        arrivals.sort()
        second.append([z] + [block for _, _, block in arrivals])
        second_slots.append([None] + [(slot, side) for slot, side, _ in arrivals])
    return first, first_slots, second, second_slots


def pick(number, choice, cases):
    chosen = cases[0]
    for at in range(1, len(cases)):
        members = [device for device, wanted in enumerate(choice) if wanted == at]
        chosen = jnp.where(is_one_of(number, members), cases[at], chosen)
    return chosen


def doubling_steps():
    count = lax.axis_size("tensor")
    return [
        [(place, place ^ (1 << bit)) for place in range(count)]
        for bit in range(count.bit_length() - 1)
    ]


def sum_step(value, pairs, wire=BF16):
    return value + lax.ppermute(value.astype(wire), "tensor", pairs).astype(F32)


def with_other_replicas(value, sections=(0, 1)):
    count = lax.axis_size("replica")
    return [value] + [
        lax.ppermute(
            value,
            ("section", "replica"),
            [(s * count + r, s * count + (r + step) % count) for s in sections for r in range(count)],
        )
        for step in range(1, count)
    ]


def to_other_core(value, source):
    return lax.ppermute(value, "section", [(source, 1 - source)])


def on_device(
    tokens,
    cotangent,
    gain,
    frozen_base_weight,
    adapter_down_factors,
    adapter_up_factors,
    tenant_adapter_scale,
    row_tenant_owner,
):
    section = lax.axis_index("section")
    place = lax.axis_index("tensor")
    count = lax.axis_size("tensor")
    is_first = section == 0
    weight = frozen_base_weight[0]
    gain_row = gain[0][None, :]
    down = adapter_down_factors[0]
    up = adapter_up_factors[0]
    rows, width = tokens.shape
    features = width * count
    ranks = down.shape[1]

    tenant_of_column = jnp.arange(ranks, dtype=jnp.int32) // (ranks // TENANT_COUNT)
    coefficients = jnp.where(
        row_tenant_owner[:, None] == tenant_of_column[None, :],
        jnp.repeat(tenant_adapter_scale, ranks // TENANT_COUNT)[None, :],
        0.0,
    )

    first_order, first_slots, second_order, second_slots = orders(count)
    place_of = section * count + place
    table = jnp.stack([section, place_of]).astype(jnp.int32)

    def times_down(value):
        return jnp.dot(value, down, preferred_element_type=F32)

    def times_up_transposed(value):
        return lax.dot_general(value, up, CONTRACT_LAST, preferred_element_type=F32)

    def line(value, first_pairs, second_pairs, toward):
        pairs = [(2 * z, 2 * (z + toward)) for z in first_pairs] + [
            (2 * z + 1, 2 * (z + toward) + 1) for z in second_pairs
        ]
        return lax.ppermute(value, ("tensor", "section"), pairs)

    token_float = tokens.astype(F32)
    early = jnp.where(is_first, (token_float * gain_row).astype(BF16), cotangent)
    early = lax.optimization_barrier(early)
    small = jnp.where(is_first, times_down(early), times_up_transposed(early)).astype(BF16)
    squares = jnp.sum(token_float * token_float, axis=1).astype(BF16)
    squares = jnp.pad(squares, (0, -rows % ranks)).reshape(-1, ranks)
    small = jnp.concatenate([small, jnp.pad(squares, ((0, 15), (0, 0)))], axis=0)
    small_all = lax.all_gather(small, "tensor")
    early_all = lax.all_gather(early, "replica")

    everyone = range(count)
    arrivals = [
        (
            line(cotangent, [], [z for z in everyone if z + 1 < count], 1),
            line(cotangent, [], [z for z in everyone if z > 0], -1),
        )
    ]
    parts = []
    for stage in range(count):
        wanted = [None if stage == 0 else second_slots[z][stage] for z in everyone]
        cases = sorted({slot for slot in wanted if slot is not None})
        here = [early] + [arrivals[slot][side] for slot, side in cases]
        if stage > 0:
            here = lax.optimization_barrier((*here, *sent))[: len(here)]
        value = pick(
            place_of,
            [0] * count + [0 if slot is None else 1 + cases.index(slot) for slot in wanted],
            here,
        )
        order = [blocks[stage] for blocks in first_order + second_order]
        part = block_product(table, value, weight, order)
        parts.append(part)
        slot = stage + 1
        if slot == count:
            break
        sent = []
        for side in (0, 1):
            needed = [first_slots[z].get((slot, side)) for z in everyone]
            stages = sorted({at for at in needed if at is not None})
            own = pick(
                place_of,
                [0 if at is None else stages.index(at) for at in needed] + [0] * count,
                [parts[at] for at in stages],
            )
            arrived = arrivals[-1][side].astype(F32)
            sent.append((arrived + jnp.where(is_first, own, 0.0)).astype(BF16))
        arrivals.append(
            (
                line(
                    sent[0],
                    [z for z in everyone if z < slot and z + 1 < count],
                    [z for z in everyone if slot + 1 < count and z >= slot and z + 1 < count],
                    1,
                ),
                line(
                    sent[1],
                    [z for z in everyone if z >= count - slot and z > 0],
                    [z for z in everyone if slot + 1 < count and z < count - slot and z > 0],
                    -1,
                ),
            )
        )
    from_left, from_right = arrivals[-1]

    small_all, early_all, _ = lax.optimization_barrier(
        (small_all, early_all, arrivals[max(count - 2, 0)])
    )
    replica, replicas = lax.axis_index("replica"), lax.axis_size("replica")
    early_all = [early] + [
        lax.dynamic_index_in_dim(early_all, lax.rem(replica + replicas - step, replicas), 0, False)
        for step in range(1, replicas)
    ]
    small_sum = jnp.sum(small_all.astype(F32), axis=0)
    inv_first = lax.rsqrt(
        small_sum[rows:].reshape(-1)[:rows][:, None] / features + EPSILON
    )
    small_early = (coefficients * small_sum[:rows]).astype(BF16)
    low_product = jnp.where(
        is_first,
        jnp.dot(small_early, up, preferred_element_type=F32),
        lax.dot_general(small_early, down, CONTRACT_LAST, preferred_element_type=F32),
    )

    pulled_here = (gain_row * (sum(parts) + low_product)).astype(BF16)
    pulled = to_other_core(pulled_here, 1)
    from_left, from_right, _ = lax.optimization_barrier((from_left, from_right, pulled_here))

    projected = parts[-1] + from_left.astype(F32) + from_right.astype(F32) + low_product
    hidden = (token_float + inv_first * projected).astype(BF16)
    late_others = with_other_replicas(jnp.where(is_first, hidden, pulled_here))[1:]
    swap = [(0, 1), (1, 0)]
    swapped = [
        lax.ppermute(jnp.where(is_first, hidden, other), "section", swap) for other in early_all[1:]
    ]
    hidden_on_second = swapped[0] if swapped else to_other_core(hidden, 0)
    cotangent_all = [cotangent] + swapped
    hidden_here = jnp.where(is_first, hidden, hidden_on_second)
    hidden_float = hidden_here.astype(F32)
    pulled_float = pulled.astype(F32)
    row_sums = jnp.stack(
        [jnp.sum(hidden_float * hidden_float, axis=1), jnp.sum(hidden_float * pulled_float, axis=1)]
    )
    for step in doubling_steps():
        row_sums = sum_step(row_sums, step, F32)
    inv_second = lax.rsqrt(row_sums[0] / features + EPSILON)[:, None]
    toward_hidden = row_sums[1][:, None] * inv_second * inv_second * inv_second / features
    hidden_grad = cotangent.astype(F32) + inv_second * pulled_float - toward_hidden * hidden_float
    rank_late = jnp.where(
        is_first,
        times_up_transposed(hidden_grad.astype(BF16)),
        times_down((hidden_float * gain_row).astype(BF16)),
    )
    for step in doubling_steps():
        rank_late = sum_step(rank_late, step)

    swapped = [lax.ppermute(other, "section", swap) for other in late_others]
    hidden_all = [hidden_here] + [
        jnp.where(is_first, *pair) for pair in zip(late_others, swapped)
    ]
    pulled_all = [pulled] + swapped

    row_scale = jnp.where(is_first, inv_first, inv_second)
    small_late = coefficients * rank_late * row_scale
    small_early = small_early.astype(F32) * row_scale
    smalls = jnp.concatenate(
        [
            jnp.where(is_first, small_early, small_late),
            jnp.where(is_first, small_late, small_early),
            jnp.broadcast_to(inv_second, (rows, 64)),
            jnp.broadcast_to(toward_hidden, (rows, 64)),
        ],
        axis=1,
    ).astype(BF16)
    grad_down, grad_up = gradients(
        table,
        gain_row,
        early_all,
        cotangent_all,
        pulled_all,
        hidden_all,
        with_other_replicas(smalls),
        ranks,
    )
    return (grad_down[None], grad_up[None])


def solution(mesh):
    return jax.shard_map(
        on_device,
        mesh=mesh,
        in_specs=(
            P(("groups", "replica"), "tensor"),
            P(("groups", "replica"), "tensor"),
            P("section", "tensor"),
            P("section", "tensor", None),
            P("section", "tensor", None),
            P("section", None, "tensor"),
            P(),
            P(("groups", "replica")),
        ),
        out_specs=(P("section", "tensor", "groups"), P("section", "groups", "tensor")),
        check_vma=False,
    )
```

```python
import functools

import jax
import jax.numpy as jnp
from jax import lax
from jax.experimental import pallas as pl
from jax.experimental.pallas import tpu as pltpu
from jax.sharding import PartitionSpec as P

TENANT_COUNT = 4
EPSILON = 1e-05
CONTRACT_LAST = (((1,), (1,)), ((), ()))
CONTRACT_FIRST = (((0,), (0,)), ((), ()))
BF16 = jnp.bfloat16
F32 = jnp.float32
AHEAD = 2


def is_one_of(number, members):
    return functools.reduce(jnp.logical_or, [number == member for member in members])


def look_up(number, values):
    found = values[0]
    for value in sorted(set(values) - {values[0]}):
        found = jnp.where(
            is_one_of(number, [at for at, other in enumerate(values) if other == value]), value, found
        )
    return found


def block_kernel(table, value_ref, weight_ref, out_ref, wide, tall, arrived, *, blocks, tile, tiles):
    section = table[0]
    block = look_up(table[1], blocks)
    step = pl.program_id(0)
    width = tile * tiles

    def copy_of(index, is_wide):
        whole = pl.ds(pl.multiple_of(block * width, width), width)
        part = pl.ds(pl.multiple_of(block * width + index * tile, tile), tile)
        if is_wide:
            return pltpu.make_async_copy(weight_ref.at[:, part], wide.at[index], arrived.at[index])
        rows = pl.ds(pl.multiple_of(index * tile, tile), tile)
        return pltpu.make_async_copy(weight_ref.at[rows, whole], tall.at[index], arrived.at[index])

    for number, is_wide in ((0, True), (1, False)):

        @pl.when(section == number)
        def _():
            @pl.when(step == 0)
            def _():
                for index in range(min(AHEAD, tiles)):
                    copy_of(index, is_wide).start()

            @pl.when(step + AHEAD < tiles)
            def _():
                copy_of(step + AHEAD, is_wide).start()

            copy_of(step, is_wide).wait()
            if is_wide:
                out_ref[...] = jnp.dot(value_ref[...], wide[step], preferred_element_type=F32)
            else:
                out_ref[...] = lax.dot_general(
                    value_ref[...], tall[step], CONTRACT_LAST, preferred_element_type=F32
                )


def block_product(table, value, weight, blocks):
    rows, width = value.shape
    tile = min(512, width)
    tiles = width // tile
    return pl.pallas_call(
        functools.partial(block_kernel, blocks=blocks, tile=tile, tiles=tiles),
        grid_spec=pltpu.PrefetchScalarGridSpec(
            num_scalar_prefetch=1,
            grid=(tiles,),
            in_specs=[
                pl.BlockSpec((rows, width), lambda step, table: (0, 0)),
                pl.BlockSpec(memory_space=pl.ANY),
            ],
            out_specs=pl.BlockSpec((rows, tile), lambda step, table: (0, step)),
            scratch_shapes=[
                pltpu.VMEM((tiles, width, tile), BF16),
                pltpu.VMEM((tiles, tile, width), BF16),
                pltpu.SemaphoreType.DMA((tiles,)),
            ],
        ),
        out_shape=jax.ShapeDtypeStruct((rows, width), F32),
        compiler_params=pltpu.CompilerParams(vmem_limit_bytes=24 * 1024 * 1024),
        cost_estimate=pl.CostEstimate(
            flops=8 * rows * width * width, bytes_accessed=2 * width * width, transcendentals=0
        ),
    )(table, value, weight)


def gradient_kernel(table, gain_ref, *refs, replicas):
    early, cotangent, pulled, hidden, smalls = (
        refs[kind * replicas : (kind + 1) * replicas] for kind in range(5)
    )
    down_ref, up_ref = refs[5 * replicas :]
    ranks = down_ref.shape[1]

    def products(down_rows, up_rows):
        down_ref[...] = sum(
            lax.dot_general(a, small[:, ranks : 2 * ranks], CONTRACT_FIRST, preferred_element_type=F32)
            for a, small in zip(down_rows, smalls)
        )
        up_ref[...] = sum(
            lax.dot_general(small[:, :ranks], a, CONTRACT_FIRST, preferred_element_type=F32)
            for a, small in zip(up_rows, smalls)
        )

    @pl.when(table[0] == 0)
    def _():
        grads = []
        for at in range(replicas):
            inverse = smalls[at][:, 2 * ranks : 2 * ranks + 1].astype(F32)
            toward = smalls[at][:, 2 * ranks + 64 : 2 * ranks + 65].astype(F32)
            grads.append(
                (
                    cotangent[at][...].astype(F32)
                    + inverse * pulled[at][...].astype(F32)
                    - toward * hidden[at][...].astype(F32)
                ).astype(BF16)
            )
        products([a[...] for a in early], grads)

    @pl.when(table[0] == 1)
    def _():
        scaled = [(a[...].astype(F32) * gain_ref[...]).astype(BF16) for a in hidden]
        products(scaled, [a[...] for a in early])


def gradients(table, gain_row, early, cotangent, pulled, hidden, smalls, ranks):
    replicas = len(early)
    rows, width = early[0].shape
    tile = min(512, width)
    columns = pl.BlockSpec((rows, tile), lambda step, table: (0, step))
    small = pl.BlockSpec(smalls[0].shape, lambda step, table: (0, 0))
    return pl.pallas_call(
        functools.partial(gradient_kernel, replicas=replicas),
        grid_spec=pltpu.PrefetchScalarGridSpec(
            num_scalar_prefetch=1,
            grid=(width // tile,),
            in_specs=[pl.BlockSpec((1, tile), lambda step, table: (0, step))]
            + [columns] * (4 * replicas)
            + [small] * replicas,
            out_specs=[
                pl.BlockSpec((tile, ranks), lambda step, table: (step, 0)),
                pl.BlockSpec((ranks, tile), lambda step, table: (0, step)),
            ],
        ),
        out_shape=[
            jax.ShapeDtypeStruct((width, ranks), F32),
            jax.ShapeDtypeStruct((ranks, width), F32),
        ],
        compiler_params=pltpu.CompilerParams(vmem_limit_bytes=24 * 1024 * 1024),
        cost_estimate=pl.CostEstimate(
            flops=4 * replicas * rows * width * ranks,
            bytes_accessed=8 * width * ranks + 8 * replicas * rows * width,
            transcendentals=0,
        ),
    )(table, gain_row, *early, *cotangent, *pulled, *hidden, *smalls)


def orders(count):
    first, first_slots, second, second_slots = [], [], [], []
    for z in range(count):
        sends = [(slot, 0, count - slot + z) for slot in range(z + 1, count)]
        sends += [(slot, 1, slot - count + z) for slot in range(count - z, count)]
        sends.sort()
        first.append([block for _, _, block in sends] + [z])
        first_slots.append({(slot, side): at for at, (slot, side, _) in enumerate(sends)})
        arrivals = [(slot, 0, z - 1 - slot) for slot in range(z)]
        arrivals += [(slot, 1, z + 1 + slot) for slot in range(count - 1 - z)]
        arrivals.sort()
        second.append([z] + [block for _, _, block in arrivals])
        second_slots.append([None] + [(slot, side) for slot, side, _ in arrivals])
    return first, first_slots, second, second_slots


def pick(number, choice, cases):
    chosen = cases[0]
    for at in range(1, len(cases)):
        members = [device for device, wanted in enumerate(choice) if wanted == at]
        chosen = jnp.where(is_one_of(number, members), cases[at], chosen)
    return chosen


def doubling_steps():
    count = lax.axis_size("tensor")
    return [
        [(place, place ^ (1 << bit)) for place in range(count)]
        for bit in range(count.bit_length() - 1)
    ]


def sum_step(value, pairs, wire=BF16):
    return value + lax.ppermute(value.astype(wire), "tensor", pairs).astype(F32)


def with_other_replicas(value, sections=(0, 1)):
    count = lax.axis_size("replica")
    return [value] + [
        lax.ppermute(
            value,
            ("section", "replica"),
            [(s * count + r, s * count + (r + step) % count) for s in sections for r in range(count)],
        )
        for step in range(1, count)
    ]


def to_other_core(value, source):
    return lax.ppermute(value, "section", [(source, 1 - source)])


def on_device(
    tokens,
    cotangent,
    gain,
    frozen_base_weight,
    adapter_down_factors,
    adapter_up_factors,
    tenant_adapter_scale,
    row_tenant_owner,
):
    section = lax.axis_index("section")
    place = lax.axis_index("tensor")
    count = lax.axis_size("tensor")
    is_first = section == 0
    weight = frozen_base_weight[0]
    gain_row = gain[0][None, :]
    down = adapter_down_factors[0]
    up = adapter_up_factors[0]
    rows, width = tokens.shape
    features = width * count
    ranks = down.shape[1]

    tenant_of_column = jnp.arange(ranks, dtype=jnp.int32) // (ranks // TENANT_COUNT)
    coefficients = jnp.where(
        row_tenant_owner[:, None] == tenant_of_column[None, :],
        jnp.repeat(tenant_adapter_scale, ranks // TENANT_COUNT)[None, :],
        0.0,
    )

    first_order, first_slots, second_order, second_slots = orders(count)
    place_of = section * count + place
    table = jnp.stack([section, place_of]).astype(jnp.int32)

    def times_down(value):
        return jnp.dot(value, down, preferred_element_type=F32)

    def times_up_transposed(value):
        return lax.dot_general(value, up, CONTRACT_LAST, preferred_element_type=F32)

    def line(value, first_pairs, second_pairs, toward):
        pairs = [(2 * z, 2 * (z + toward)) for z in first_pairs] + [
            (2 * z + 1, 2 * (z + toward) + 1) for z in second_pairs
        ]
        return lax.ppermute(value, ("tensor", "section"), pairs)

    token_float = tokens.astype(F32)
    early = jnp.where(is_first, (token_float * gain_row).astype(BF16), cotangent)
    early = lax.optimization_barrier(early)

    def small_columns(value, plain):
        small = jnp.where(is_first, times_down(value), times_up_transposed(value))
        squares = jnp.sum(plain.astype(F32) ** 2, axis=1)
        squares = jnp.pad(squares, (0, -rows % ranks)).reshape(-1, ranks)
        return jnp.concatenate([small, jnp.pad(squares, ((0, -len(squares) % 16), (0, 0)))], axis=0)

    everyone = range(count)
    arrivals = [
        (
            line(cotangent, [], [z for z in everyone if z + 1 < count], 1),
            line(cotangent, [], [z for z in everyone if z > 0], -1),
        )
    ]
    parts = []
    small_sum = None
    steps_left = doubling_steps()
    for stage in range(count):
        wanted = [None if stage == 0 else second_slots[z][stage] for z in everyone]
        cases = sorted({slot for slot in wanted if slot is not None})
        here = [early] + [arrivals[slot][side] for slot, side in cases]
        if stage == 1:
            small_sum = small_columns(*lax.optimization_barrier((early, tokens, *sent))[:2])
        elif stage > 1 and steps_left:
            small_sum = sum_step(small_sum, steps_left.pop(0))
        if stage > 0:
            *here, small_sum = lax.optimization_barrier((*here, small_sum, *sent))[: len(here) + 1]
        value = pick(
            place_of,
            [0] * count + [0 if slot is None else 1 + cases.index(slot) for slot in wanted],
            here,
        )
        order = [blocks[stage] for blocks in first_order + second_order]
        part = block_product(table, value, weight, order)
        if stage == 0:
            part, after = lax.optimization_barrier((part, early))
            early_all = [early] + with_other_replicas(after)[1:]
        if stage == 2:
            part, *early_all = lax.optimization_barrier((part, *early_all))
        parts.append(part)
        slot = stage + 1
        if slot == count:
            break
        sent = []
        for side in (0, 1):
            needed = [first_slots[z].get((slot, side)) for z in everyone]
            stages = sorted({at for at in needed if at is not None})
            own = pick(
                place_of,
                [0 if at is None else stages.index(at) for at in needed] + [0] * count,
                [parts[at] for at in stages],
            )
            arrived = arrivals[-1][side]
            if side == 1:
                arrived, _ = lax.optimization_barrier((arrived, sent[0]))
            arrived = arrived.astype(F32)
            sent.append((arrived + jnp.where(is_first, own, 0.0)).astype(BF16))
        arrivals.append(
            (
                line(
                    sent[0],
                    [z for z in everyone if z < slot and z + 1 < count],
                    [z for z in everyone if slot + 1 < count and z >= slot and z + 1 < count],
                    1,
                ),
                line(
                    sent[1],
                    [z for z in everyone if z >= count - slot and z > 0],
                    [z for z in everyone if slot + 1 < count and z < count - slot and z > 0],
                    -1,
                ),
            )
        )
    from_left, from_right = arrivals[-1]

    while steps_left:
        small_sum = sum_step(small_sum, steps_left.pop(0))
    inv_first = lax.rsqrt(
        small_sum[rows:].reshape(-1)[:rows][:, None] / features + EPSILON
    )
    small_early = (coefficients * small_sum[:rows]).astype(BF16)
    low_product = jnp.where(
        is_first,
        jnp.dot(small_early, up, preferred_element_type=F32),
        lax.dot_general(small_early, down, CONTRACT_LAST, preferred_element_type=F32),
    )

    pulled_here = (gain_row * (sum(parts) + low_product)).astype(BF16)
    pulled = to_other_core(pulled_here, 1)
    from_left, from_right, _ = lax.optimization_barrier((from_left, from_right, pulled_here))

    projected = parts[-1] + from_left.astype(F32) + from_right.astype(F32) + low_product
    hidden = (token_float + inv_first * projected).astype(BF16)
    late_others = with_other_replicas(jnp.where(is_first, hidden, pulled_here))[1:]
    swap = [(0, 1), (1, 0)]
    swapped = [
        lax.ppermute(jnp.where(is_first, hidden, other), "section", swap) for other in early_all[1:]
    ]
    hidden_on_second = swapped[0] if swapped else to_other_core(hidden, 0)
    cotangent_all = [cotangent] + swapped
    hidden_here = jnp.where(is_first, hidden, hidden_on_second)
    hidden_float = hidden_here.astype(F32)
    pulled_float = pulled.astype(F32)
    row_sums = jnp.stack(
        [jnp.sum(hidden_float * hidden_float, axis=1), jnp.sum(hidden_float * pulled_float, axis=1)]
    )
    for step in doubling_steps():
        row_sums = sum_step(row_sums, step, F32)
    inv_second = lax.rsqrt(row_sums[0] / features + EPSILON)[:, None]
    toward_hidden = row_sums[1][:, None] * inv_second * inv_second * inv_second / features
    hidden_grad = cotangent.astype(F32) + inv_second * pulled_float - toward_hidden * hidden_float
    rank_late = jnp.where(
        is_first,
        times_up_transposed(hidden_grad.astype(BF16)),
        times_down((hidden_float * gain_row).astype(BF16)),
    )
    for step in doubling_steps():
        rank_late = sum_step(rank_late, step)

    swapped = [
        lax.ppermute(lax.optimization_barrier((other, rank_late))[0], "section", swap)
        for other in late_others
    ]
    hidden_all = [hidden_here] + [
        jnp.where(is_first, *pair) for pair in zip(late_others, swapped)
    ]
    pulled_all = [pulled] + swapped

    row_scale = jnp.where(is_first, inv_first, inv_second)
    small_late = coefficients * rank_late * row_scale
    small_early = small_early.astype(F32) * row_scale
    smalls = jnp.concatenate(
        [
            jnp.where(is_first, small_early, small_late),
            jnp.where(is_first, small_late, small_early),
            jnp.broadcast_to(inv_second, (rows, 64)),
            jnp.broadcast_to(toward_hidden, (rows, 64)),
        ],
        axis=1,
    ).astype(BF16)
    grad_down, grad_up = gradients(
        table,
        gain_row,
        early_all,
        cotangent_all,
        pulled_all,
        hidden_all,
        with_other_replicas(smalls),
        ranks,
    )
    return (grad_down[None], grad_up[None])


def solution(mesh):
    return jax.shard_map(
        on_device,
        mesh=mesh,
        in_specs=(
            P(("groups", "replica"), "tensor"),
            P(("groups", "replica"), "tensor"),
            P("section", "tensor"),
            P("section", "tensor", None),
            P("section", "tensor", None),
            P("section", None, "tensor"),
            P(),
            P(("groups", "replica")),
        ),
        out_specs=(P("section", "tensor", "groups"), P("section", "groups", "tensor")),
        check_vma=False,
    )
```

```python
import functools

import jax
import jax.numpy as jnp
from jax import lax
from jax.experimental import pallas as pl
from jax.experimental.pallas import tpu as pltpu
from jax.sharding import PartitionSpec as P

TENANT_COUNT = 4
EPSILON = 1e-05
CONTRACT_LAST = (((1,), (1,)), ((), ()))
CONTRACT_FIRST = (((0,), (0,)), ((), ()))
BF16 = jnp.bfloat16
F32 = jnp.float32
AHEAD = 2


def is_one_of(number, members):
    return functools.reduce(jnp.logical_or, [number == member for member in members])


def look_up(number, values):
    found = values[0]
    for value in sorted(set(values) - {values[0]}):
        found = jnp.where(
            is_one_of(number, [at for at, other in enumerate(values) if other == value]), value, found
        )
    return found


def block_kernel(table, value_ref, weight_ref, out_ref, wide, tall, arrived, *, blocks, tile, tiles):
    section = table[0]
    block = look_up(table[1], blocks)
    step = pl.program_id(0)
    width = tile * tiles

    def copy_of(index, is_wide):
        whole = pl.ds(pl.multiple_of(block * width, width), width)
        part = pl.ds(pl.multiple_of(block * width + index * tile, tile), tile)
        if is_wide:
            return pltpu.make_async_copy(weight_ref.at[:, part], wide.at[index], arrived.at[index])
        rows = pl.ds(pl.multiple_of(index * tile, tile), tile)
        return pltpu.make_async_copy(weight_ref.at[rows, whole], tall.at[index], arrived.at[index])

    for number, is_wide in ((0, True), (1, False)):

        @pl.when(section == number)
        def _():
            @pl.when(step == 0)
            def _():
                for index in range(min(AHEAD, tiles)):
                    copy_of(index, is_wide).start()

            @pl.when(step + AHEAD < tiles)
            def _():
                copy_of(step + AHEAD, is_wide).start()

            copy_of(step, is_wide).wait()
            if is_wide:
                out_ref[...] = jnp.dot(value_ref[...], wide[step], preferred_element_type=F32)
            else:
                out_ref[...] = lax.dot_general(
                    value_ref[...], tall[step], CONTRACT_LAST, preferred_element_type=F32
                )


def block_product(table, value, weight, blocks):
    rows, width = value.shape
    tile = min(512, width)
    tiles = width // tile
    return pl.pallas_call(
        functools.partial(block_kernel, blocks=blocks, tile=tile, tiles=tiles),
        grid_spec=pltpu.PrefetchScalarGridSpec(
            num_scalar_prefetch=1,
            grid=(tiles,),
            in_specs=[
                pl.BlockSpec((rows, width), lambda step, table: (0, 0)),
                pl.BlockSpec(memory_space=pl.ANY),
            ],
            out_specs=pl.BlockSpec((rows, tile), lambda step, table: (0, step)),
            scratch_shapes=[
                pltpu.VMEM((tiles, width, tile), BF16),
                pltpu.VMEM((tiles, tile, width), BF16),
                pltpu.SemaphoreType.DMA((tiles,)),
            ],
        ),
        out_shape=jax.ShapeDtypeStruct((rows, width), F32),
        compiler_params=pltpu.CompilerParams(vmem_limit_bytes=24 * 1024 * 1024),
        cost_estimate=pl.CostEstimate(
            flops=8 * rows * width * width, bytes_accessed=2 * width * width, transcendentals=0
        ),
    )(table, value, weight)


def transposed_times(left, right):
    return lax.dot_general(left, right, CONTRACT_FIRST, preferred_element_type=F32)


def own_gradient_kernel(table, early, late, small_early, small_late, down_ref, up_ref):
    @pl.when(table[0] == 0)
    def _():
        down_ref[...] = transposed_times(early[...], small_late[...])
        up_ref[...] = transposed_times(small_early[...], late[...])

    @pl.when(table[0] == 1)
    def _():
        down_ref[...] = transposed_times(late[...], small_early[...])
        up_ref[...] = transposed_times(small_late[...], early[...])


def other_gradient_kernel(
    table, gain_ref, down_sum, up_sum, early, cotangent, pulled, hidden, small_early, small_late,
    down_ref, up_ref,
):
    ranks = down_ref.shape[1]
    late = small_late[:, :ranks]
    inverse = small_late[:, ranks : ranks + 1].astype(F32)
    toward = small_late[:, ranks + 64 : ranks + 65].astype(F32)

    @pl.when(table[0] == 0)
    def _():
        grad = (
            cotangent[...].astype(F32)
            + inverse * pulled[...].astype(F32)
            - toward * hidden[...].astype(F32)
        ).astype(BF16)
        down_ref[...] = down_sum[...] + transposed_times(early[...], late)
        up_ref[...] = up_sum[...] + transposed_times(small_early[...], grad)

    @pl.when(table[0] == 1)
    def _():
        scaled = (hidden[...].astype(F32) * gain_ref[...]).astype(BF16)
        weighed = (small_early[...].astype(F32) * inverse).astype(BF16)
        down_ref[...] = down_sum[...] + transposed_times(scaled, weighed)
        up_ref[...] = up_sum[...] + transposed_times(late, early[...])


def gradient_call(kernel, table, sums, by_column, whole, width, ranks, rows):
    tile = min(512, width)
    down_spec = pl.BlockSpec((tile, ranks), lambda step, table: (step, 0))
    up_spec = pl.BlockSpec((ranks, tile), lambda step, table: (0, step))
    leading = [array for array in by_column if array.shape[0] == 1]
    columns = [array for array in by_column if array.shape[0] != 1]
    return pl.pallas_call(
        kernel,
        grid_spec=pltpu.PrefetchScalarGridSpec(
            num_scalar_prefetch=1,
            grid=(width // tile,),
            in_specs=[pl.BlockSpec((1, tile), lambda step, table: (0, step)) for _ in leading]
            + [down_spec, up_spec][: len(sums)]
            + [pl.BlockSpec((rows, tile), lambda step, table: (0, step)) for _ in columns]
            + [pl.BlockSpec(array.shape, lambda step, table: (0, 0)) for array in whole],
            out_specs=[down_spec, up_spec],
        ),
        out_shape=[
            jax.ShapeDtypeStruct((width, ranks), F32),
            jax.ShapeDtypeStruct((ranks, width), F32),
        ],
        compiler_params=pltpu.CompilerParams(vmem_limit_bytes=20 * 1024 * 1024),
        cost_estimate=pl.CostEstimate(
            flops=4 * rows * width * ranks,
            bytes_accessed=8 * width * ranks * (1 + len(sums) // 2) + 2 * rows * width * len(columns),
            transcendentals=0,
        ),
    )(table, *leading, *sums, *columns, *whole)


def orders(count):
    first, first_slots, second, second_slots = [], [], [], []
    for z in range(count):
        sends = [(slot, 0, count - slot + z) for slot in range(z + 1, count)]
        sends += [(slot, 1, slot - count + z) for slot in range(count - z, count)]
        sends.sort()
        first.append([block for _, _, block in sends] + [z])
        first_slots.append({(slot, side): at for at, (slot, side, _) in enumerate(sends)})
        arrivals = [(slot, 0, z - 1 - slot) for slot in range(z)]
        arrivals += [(slot, 1, z + 1 + slot) for slot in range(count - 1 - z)]
        arrivals.sort()
        second.append([z] + [block for _, _, block in arrivals])
        second_slots.append([None] + [(slot, side) for slot, side, _ in arrivals])
    return first, first_slots, second, second_slots


def pick(number, choice, cases):
    chosen = cases[0]
    for at in range(1, len(cases)):
        members = [device for device, wanted in enumerate(choice) if wanted == at]
        chosen = jnp.where(is_one_of(number, members), cases[at], chosen)
    return chosen


def doubling_steps():
    count = lax.axis_size("tensor")
    return [
        [(place, place ^ (1 << bit)) for place in range(count)]
        for bit in range(count.bit_length() - 1)
    ]


def sum_step(value, pairs, wire=BF16):
    return value + lax.ppermute(value.astype(wire), "tensor", pairs).astype(F32)


def with_other_replicas(value, sections=(0, 1)):
    count = lax.axis_size("replica")
    return [value] + [
        lax.ppermute(
            value,
            ("section", "replica"),
            [(s * count + r, s * count + (r + step) % count) for s in sections for r in range(count)],
        )
        for step in range(1, count)
    ]


def to_other_core(value, source):
    return lax.ppermute(value, "section", [(source, 1 - source)])


def on_device(
    tokens,
    cotangent,
    gain,
    frozen_base_weight,
    adapter_down_factors,
    adapter_up_factors,
    tenant_adapter_scale,
    row_tenant_owner,
):
    section = lax.axis_index("section")
    place = lax.axis_index("tensor")
    count = lax.axis_size("tensor")
    is_first = section == 0
    weight = frozen_base_weight[0]
    gain_row = gain[0][None, :]
    down = adapter_down_factors[0]
    up = adapter_up_factors[0]
    rows, width = tokens.shape
    features = width * count
    replicas = lax.axis_size("replica")
    ranks = down.shape[1]

    tenant_of_column = jnp.arange(ranks, dtype=jnp.int32) // (ranks // TENANT_COUNT)
    coefficients = jnp.where(
        row_tenant_owner[:, None] == tenant_of_column[None, :],
        jnp.repeat(tenant_adapter_scale, ranks // TENANT_COUNT)[None, :],
        0.0,
    )

    first_order, first_slots, second_order, second_slots = orders(count)
    place_of = section * count + place
    table = jnp.stack([section, place_of]).astype(jnp.int32)

    def times_down(value):
        return jnp.dot(value, down, preferred_element_type=F32)

    def times_up_transposed(value):
        return lax.dot_general(value, up, CONTRACT_LAST, preferred_element_type=F32)

    def line(value, first_pairs, second_pairs, toward):
        pairs = [(2 * z, 2 * (z + toward)) for z in first_pairs] + [
            (2 * z + 1, 2 * (z + toward) + 1) for z in second_pairs
        ]
        return lax.ppermute(value, ("tensor", "section"), pairs)

    token_float = tokens.astype(F32)
    early = jnp.where(is_first, (token_float * gain_row).astype(BF16), cotangent)
    early = lax.optimization_barrier(early)

    def small_columns(value, plain):
        small = jnp.where(is_first, times_down(value), times_up_transposed(value))
        squares = jnp.sum(plain.astype(F32) ** 2, axis=1)
        squares = jnp.pad(squares, (0, -rows % ranks)).reshape(-1, ranks)
        return jnp.concatenate([small, jnp.pad(squares, ((0, -len(squares) % 16), (0, 0)))], axis=0)

    steps_left = doubling_steps()
    small_sum = small_columns(early, tokens)
    sent_first, small_sum = lax.optimization_barrier((cotangent, small_sum))
    if steps_left:
        small_sum = sum_step(small_sum, steps_left.pop(0))

    everyone = range(count)
    arrivals = [
        (
            line(sent_first, [], [z for z in everyone if z + 1 < count], 1),
            line(sent_first, [], [z for z in everyone if z > 0], -1),
        )
    ]
    parts = []
    for stage in range(count):
        wanted = [None if stage == 0 else second_slots[z][stage] for z in everyone]
        cases = sorted({slot for slot in wanted if slot is not None})
        here = [early] + [arrivals[slot][side] for slot, side in cases]
        if stage == 2:
            *here, small_sum = lax.optimization_barrier((*here, small_sum, *sent))[: len(here) + 1]
        elif stage > 0:
            here = lax.optimization_barrier((*here, *sent))[: len(here)]
        value = pick(
            place_of,
            [0] * count + [0 if slot is None else 1 + cases.index(slot) for slot in wanted],
            here,
        )
        order = [blocks[stage] for blocks in first_order + second_order]
        part = block_product(table, value, weight, order)
        if steps_left:
            part, small_sum = lax.optimization_barrier((part, small_sum))
            small_sum = sum_step(small_sum, steps_left.pop(0))
        if stage == 1:
            part, after = lax.optimization_barrier((part, early))
            early_all = [early] + with_other_replicas(after)[1:]
        if stage == count - 1:
            part, *early_all = lax.optimization_barrier((part, *early_all))
        parts.append(part)
        slot = stage + 1
        if slot == count:
            break
        sent = []
        for side in (0, 1):
            needed = [first_slots[z].get((slot, side)) for z in everyone]
            stages = sorted({at for at in needed if at is not None})
            own = pick(
                place_of,
                [0 if at is None else stages.index(at) for at in needed] + [0] * count,
                [parts[at] for at in stages],
            )
            arrived = arrivals[-1][side]
            if side == 1:
                arrived, _ = lax.optimization_barrier((arrived, sent[0]))
            arrived = arrived.astype(F32)
            sent.append((arrived + jnp.where(is_first, own, 0.0)).astype(BF16))
        arrivals.append(
            (
                line(
                    sent[0],
                    [z for z in everyone if z < slot and z + 1 < count],
                    [z for z in everyone if slot + 1 < count and z >= slot and z + 1 < count],
                    1,
                ),
                line(
                    sent[1],
                    [z for z in everyone if z >= count - slot and z > 0],
                    [z for z in everyone if slot + 1 < count and z < count - slot and z > 0],
                    -1,
                ),
            )
        )
    from_left, from_right = arrivals[-1]

    while steps_left:
        small_sum = sum_step(small_sum, steps_left.pop(0))
    inv_first = lax.rsqrt(
        small_sum[rows:].reshape(-1)[:rows][:, None] / features + EPSILON
    )
    small_early = (coefficients * small_sum[:rows]).astype(BF16)
    small_early_all = with_other_replicas(
        (small_early.astype(F32) * jnp.where(is_first, inv_first, 1.0)).astype(BF16)
    )
    low_product = jnp.where(
        is_first,
        jnp.dot(small_early, up, preferred_element_type=F32),
        lax.dot_general(small_early, down, CONTRACT_LAST, preferred_element_type=F32),
    )

    pulled_here = (gain_row * (sum(parts) + low_product)).astype(BF16)
    pulled = to_other_core(pulled_here, 1)
    from_left, from_right, *small_early_all, _ = lax.optimization_barrier(
        (from_left, from_right, *small_early_all, pulled_here)
    )

    projected = parts[-1] + from_left.astype(F32) + from_right.astype(F32) + low_product
    hidden = (token_float + inv_first * projected).astype(BF16)
    late_others = with_other_replicas(jnp.where(is_first, hidden, pulled_here))[1:]
    swap = [(0, 1), (1, 0)]
    swapped = [
        lax.ppermute(jnp.where(is_first, hidden, other), "section", swap) for other in early_all[1:]
    ]
    hidden_on_second = swapped[0] if swapped else to_other_core(hidden, 0)
    cotangent_all = [cotangent] + swapped
    hidden_here = jnp.where(is_first, hidden, hidden_on_second)
    hidden_float = hidden_here.astype(F32)
    pulled_float = pulled.astype(F32)
    row_sums = jnp.stack(
        [jnp.sum(hidden_float * hidden_float, axis=1), jnp.sum(hidden_float * pulled_float, axis=1)]
    )
    if count <= 4:
        row_sums = row_sums + sum(
            lax.ppermute(row_sums, "tensor", [(z, (z + step) % count) for z in everyone])
            for step in range(1, count)
        )
    else:
        for step in doubling_steps():
            row_sums = sum_step(row_sums, step, F32)
    inv_second = lax.rsqrt(row_sums[0] / features + EPSILON)[:, None]
    toward_hidden = row_sums[1][:, None] * inv_second * inv_second * inv_second / features
    hidden_grad = cotangent.astype(F32) + inv_second * pulled_float - toward_hidden * hidden_float
    late = jnp.where(
        is_first, hidden_grad.astype(BF16), (hidden_float * gain_row).astype(BF16)
    )
    rank_late = jnp.where(is_first, times_up_transposed(late), times_down(late))
    for step in doubling_steps():
        rank_late = sum_step(rank_late, step)

    swapped = [
        lax.ppermute(lax.optimization_barrier((other, rank_late))[0], "section", swap)
        for other in late_others
    ]
    hidden_all = [hidden_here] + [
        jnp.where(is_first, *pair) for pair in zip(late_others, swapped)
    ]
    pulled_all = [pulled] + swapped

    small_late = (coefficients * rank_late * jnp.where(is_first, inv_first, inv_second)).astype(BF16)
    small_late_all = with_other_replicas(
        jnp.concatenate(
            [
                small_late,
                jnp.broadcast_to(inv_second, (rows, 64)).astype(BF16),
                jnp.broadcast_to(toward_hidden, (rows, 64)).astype(BF16),
            ],
            axis=1,
        )
    )
    small_early_own = (
        small_early.astype(F32) * jnp.where(is_first, inv_first, inv_second)
    ).astype(BF16)
    sums = gradient_call(
        own_gradient_kernel,
        table, [], [early, late], [small_early_own, small_late], width, ranks, rows,
    )
    for at in range(1, replicas):
        sums = gradient_call(
            other_gradient_kernel,
            table,
            sums,
            [gain_row, early_all[at], cotangent_all[at], pulled_all[at], hidden_all[at]],
            [small_early_all[at], small_late_all[at]],
            width,
            ranks,
            rows,
        )
    grad_down, grad_up = sums
    return (grad_down[None], grad_up[None])


def solution(mesh):
    return jax.shard_map(
        on_device,
        mesh=mesh,
        in_specs=(
            P(("groups", "replica"), "tensor"),
            P(("groups", "replica"), "tensor"),
            P("section", "tensor"),
            P("section", "tensor", None),
            P("section", "tensor", None),
            P("section", None, "tensor"),
            P(),
            P(("groups", "replica")),
        ),
        out_specs=(P("section", "tensor", "groups"), P("section", "groups", "tensor")),
        check_vma=False,
    )
```

```python
import functools

import jax
import jax.numpy as jnp
from jax import lax
from jax.experimental import pallas as pl
from jax.experimental.pallas import tpu as pltpu
from jax.sharding import PartitionSpec as P

TENANT_COUNT = 4
EPSILON = 1e-05
CONTRACT_LAST = (((1,), (1,)), ((), ()))
CONTRACT_FIRST = (((0,), (0,)), ((), ()))
BF16 = jnp.bfloat16
F32 = jnp.float32
AHEAD = 2


def is_one_of(number, members):
    return functools.reduce(jnp.logical_or, [number == member for member in members])


def look_up(number, values):
    found = values[0]
    for value in sorted(set(values) - {values[0]}):
        found = jnp.where(
            is_one_of(number, [at for at, other in enumerate(values) if other == value]), value, found
        )
    return found


def block_kernel(table, value_ref, weight_ref, out_ref, wide, tall, arrived, *, blocks, tile, tiles):
    section = table[0]
    block = look_up(table[1], blocks)
    step = pl.program_id(0)
    width = tile * tiles

    def copy_of(index, is_wide):
        whole = pl.ds(pl.multiple_of(block * width, width), width)
        part = pl.ds(pl.multiple_of(block * width + index * tile, tile), tile)
        if is_wide:
            return pltpu.make_async_copy(weight_ref.at[:, part], wide.at[index], arrived.at[index])
        rows = pl.ds(pl.multiple_of(index * tile, tile), tile)
        return pltpu.make_async_copy(weight_ref.at[rows, whole], tall.at[index], arrived.at[index])

    for number, is_wide in ((0, True), (1, False)):

        @pl.when(section == number)
        def _():
            @pl.when(step == 0)
            def _():
                for index in range(min(AHEAD, tiles)):
                    copy_of(index, is_wide).start()

            @pl.when(step + AHEAD < tiles)
            def _():
                copy_of(step + AHEAD, is_wide).start()

            copy_of(step, is_wide).wait()
            if is_wide:
                out_ref[...] = jnp.dot(value_ref[...], wide[step], preferred_element_type=F32)
            else:
                out_ref[...] = lax.dot_general(
                    value_ref[...], tall[step], CONTRACT_LAST, preferred_element_type=F32
                )


def block_product(table, value, weight, blocks):
    rows, width = value.shape
    tile = min(512, width)
    tiles = width // tile
    return pl.pallas_call(
        functools.partial(block_kernel, blocks=blocks, tile=tile, tiles=tiles),
        grid_spec=pltpu.PrefetchScalarGridSpec(
            num_scalar_prefetch=1,
            grid=(tiles,),
            in_specs=[
                pl.BlockSpec((rows, width), lambda step, table: (0, 0)),
                pl.BlockSpec(memory_space=pl.ANY),
            ],
            out_specs=pl.BlockSpec((rows, tile), lambda step, table: (0, step)),
            scratch_shapes=[
                pltpu.VMEM((tiles, width, tile), BF16),
                pltpu.VMEM((tiles, tile, width), BF16),
                pltpu.SemaphoreType.DMA((tiles,)),
            ],
        ),
        out_shape=jax.ShapeDtypeStruct((rows, width), F32),
        compiler_params=pltpu.CompilerParams(vmem_limit_bytes=24 * 1024 * 1024),
        cost_estimate=pl.CostEstimate(
            flops=8 * rows * width * width, bytes_accessed=2 * width * width, transcendentals=0
        ),
    )(table, value, weight)


def transposed_times(left, right):
    return lax.dot_general(left, right, CONTRACT_FIRST, preferred_element_type=F32)


def own_gradient_kernel(table, early, late, small_early, small_late, down_ref, up_ref):
    @pl.when(table[0] == 0)
    def _():
        down_ref[...] = transposed_times(early[...], small_late[...])
        up_ref[...] = transposed_times(small_early[...], late[...])

    @pl.when(table[0] == 1)
    def _():
        down_ref[...] = transposed_times(late[...], small_early[...])
        up_ref[...] = transposed_times(small_late[...], early[...])


def other_gradient_kernel(
    table, gain_ref, down_sum, up_sum, early, cotangent, pulled, hidden, small_early, small_late,
    down_ref, up_ref,
):
    ranks = down_ref.shape[1]
    late = small_late[:, :ranks]
    inverse = small_late[:, ranks : ranks + 1].astype(F32)
    toward = small_late[:, ranks + 64 : ranks + 65].astype(F32)

    @pl.when(table[0] == 0)
    def _():
        grad = (
            cotangent[...].astype(F32)
            + inverse * pulled[...].astype(F32)
            - toward * hidden[...].astype(F32)
        ).astype(BF16)
        down_ref[...] = down_sum[...] + transposed_times(early[...], late)
        up_ref[...] = up_sum[...] + transposed_times(small_early[...], grad)

    @pl.when(table[0] == 1)
    def _():
        scaled = (hidden[...].astype(F32) * gain_ref[...]).astype(BF16)
        weighed = (small_early[...].astype(F32) * inverse).astype(BF16)
        down_ref[...] = down_sum[...] + transposed_times(scaled, weighed)
        up_ref[...] = up_sum[...] + transposed_times(late, early[...])


def gradient_call(kernel, table, sums, by_column, whole, width, ranks, rows):
    tile = min(512, width)
    down_spec = pl.BlockSpec((tile, ranks), lambda step, table: (step, 0))
    up_spec = pl.BlockSpec((ranks, tile), lambda step, table: (0, step))
    leading = [array for array in by_column if array.shape[0] == 1]
    columns = [array for array in by_column if array.shape[0] != 1]
    return pl.pallas_call(
        kernel,
        grid_spec=pltpu.PrefetchScalarGridSpec(
            num_scalar_prefetch=1,
            grid=(width // tile,),
            in_specs=[pl.BlockSpec((1, tile), lambda step, table: (0, step)) for _ in leading]
            + [down_spec, up_spec][: len(sums)]
            + [pl.BlockSpec((rows, tile), lambda step, table: (0, step)) for _ in columns]
            + [pl.BlockSpec(array.shape, lambda step, table: (0, 0)) for array in whole],
            out_specs=[down_spec, up_spec],
        ),
        out_shape=[
            jax.ShapeDtypeStruct((width, ranks), F32),
            jax.ShapeDtypeStruct((ranks, width), F32),
        ],
        compiler_params=pltpu.CompilerParams(vmem_limit_bytes=20 * 1024 * 1024),
        cost_estimate=pl.CostEstimate(
            flops=4 * rows * width * ranks,
            bytes_accessed=8 * width * ranks * (1 + len(sums) // 2) + 2 * rows * width * len(columns),
            transcendentals=0,
        ),
    )(table, *leading, *sums, *columns, *whole)


def orders(count):
    first, first_slots, second, second_slots = [], [], [], []
    for z in range(count):
        sends = [(slot, 0, count - slot + z) for slot in range(z + 1, count)]
        sends += [(slot, 1, slot - count + z) for slot in range(count - z, count)]
        sends.sort()
        first.append([block for _, _, block in sends] + [z])
        first_slots.append({(slot, side): at for at, (slot, side, _) in enumerate(sends)})
        arrivals = [(slot, 0, z - 1 - slot) for slot in range(z)]
        arrivals += [(slot, 1, z + 1 + slot) for slot in range(count - 1 - z)]
        arrivals.sort()
        second.append([z] + [block for _, _, block in arrivals])
        second_slots.append([None] + [(slot, side) for slot, side, _ in arrivals])
    return first, first_slots, second, second_slots


def pick(number, choice, cases):
    chosen = cases[0]
    for at in range(1, len(cases)):
        members = [device for device, wanted in enumerate(choice) if wanted == at]
        chosen = jnp.where(is_one_of(number, members), cases[at], chosen)
    return chosen


def doubling_steps():
    count = lax.axis_size("tensor")
    return [
        [(place, place ^ (1 << bit)) for place in range(count)]
        for bit in range(count.bit_length() - 1)
    ]


def sum_step(value, pairs, wire=BF16, after=()):
    other = lax.ppermute(value.astype(wire), "tensor", pairs)
    if after:
        other = lax.optimization_barrier((other, *after))[0]
    return value + other.astype(F32)


def with_other_replicas(value, sections=(0, 1)):
    count = lax.axis_size("replica")
    return [value] + [
        lax.ppermute(
            value,
            ("section", "replica"),
            [(s * count + r, s * count + (r + step) % count) for s in sections for r in range(count)],
        )
        for step in range(1, count)
    ]


def to_other_core(value, source):
    return lax.ppermute(value, "section", [(source, 1 - source)])


def on_device(
    tokens,
    cotangent,
    gain,
    frozen_base_weight,
    adapter_down_factors,
    adapter_up_factors,
    tenant_adapter_scale,
    row_tenant_owner,
):
    section = lax.axis_index("section")
    place = lax.axis_index("tensor")
    count = lax.axis_size("tensor")
    is_first = section == 0
    weight = frozen_base_weight[0]
    gain_row = gain[0][None, :]
    down = adapter_down_factors[0]
    up = adapter_up_factors[0]
    rows, width = tokens.shape
    features = width * count
    replicas = lax.axis_size("replica")
    ranks = down.shape[1]

    tenant_of_column = jnp.arange(ranks, dtype=jnp.int32) // (ranks // TENANT_COUNT)
    coefficients = jnp.where(
        row_tenant_owner[:, None] == tenant_of_column[None, :],
        jnp.repeat(tenant_adapter_scale, ranks // TENANT_COUNT)[None, :],
        0.0,
    )

    first_order, first_slots, second_order, second_slots = orders(count)
    place_of = section * count + place
    table = jnp.stack([section, place_of]).astype(jnp.int32)

    def times_down(value):
        return jnp.dot(value, down, preferred_element_type=F32)

    def times_up_transposed(value):
        return lax.dot_general(value, up, CONTRACT_LAST, preferred_element_type=F32)

    def line(value, first_pairs, second_pairs, toward):
        pairs = [(2 * z, 2 * (z + toward)) for z in first_pairs] + [
            (2 * z + 1, 2 * (z + toward) + 1) for z in second_pairs
        ]
        return lax.ppermute(value, ("tensor", "section"), pairs)

    token_float = tokens.astype(F32)
    early = jnp.where(is_first, (token_float * gain_row).astype(BF16), cotangent)
    early = lax.optimization_barrier(early)

    def small_columns(value, plain):
        small = jnp.where(is_first, times_down(value), times_up_transposed(value))
        squares = jnp.sum(plain.astype(F32) ** 2, axis=1)
        squares = jnp.pad(squares, (0, -rows % ranks)).reshape(-1, ranks)
        return jnp.concatenate([small, jnp.pad(squares, ((0, -len(squares) % 16), (0, 0)))], axis=0)

    everyone = range(count)
    steps_left = doubling_steps()
    arrivals = [
        (
            lax.ppermute(
                cotangent,
                ("tensor", "section"),
                [(2 * z, 2 * (z + 1) + 1) for z in everyone if z + 1 < count],
            ),
            line(cotangent, [], [z for z in everyone if z > 0], -1),
        )
    ]
    parts = []
    for stage in range(count):
        wanted = [None if stage == 0 else second_slots[z][stage] for z in everyone]
        cases = sorted({slot for slot in wanted if slot is not None})
        here = [early] + [arrivals[slot][side] for slot, side in cases]
        if stage == 1:
            small_sum = small_columns(*lax.optimization_barrier((early, tokens, *sent))[:2])
        elif stage > 1 and steps_left:
            small_sum = sum_step(small_sum, steps_left.pop(0), after=sent)
        if stage > 0:
            *here, small_sum = lax.optimization_barrier((*here, small_sum, *sent))[: len(here) + 1]
        value = pick(
            place_of,
            [0] * count + [0 if slot is None else 1 + cases.index(slot) for slot in wanted],
            here,
        )
        order = [blocks[stage] for blocks in first_order + second_order]
        part = block_product(table, value, weight, order)
        if stage == 1:
            part, after = lax.optimization_barrier((part, early))
            early_all = [early] + with_other_replicas(after)[1:]
        if stage == count - 1:
            part, *early_all = lax.optimization_barrier((part, *early_all))
        parts.append(part)
        slot = stage + 1
        if slot == count:
            break
        sent = []
        for side in (0, 1):
            needed = [first_slots[z].get((slot, side)) for z in everyone]
            stages = sorted({at for at in needed if at is not None})
            own = pick(
                place_of,
                [0 if at is None else stages.index(at) for at in needed] + [0] * count,
                [parts[at] for at in stages],
            )
            arrived = arrivals[-1][side]
            if side == 1:
                arrived, _ = lax.optimization_barrier((arrived, sent[0]))
            arrived = arrived.astype(F32)
            sent.append((arrived + jnp.where(is_first, own, 0.0)).astype(BF16))
        arrivals.append(
            (
                line(
                    sent[0],
                    [z for z in everyone if z < slot and z + 1 < count],
                    [z for z in everyone if slot + 1 < count and z >= slot and z + 1 < count],
                    1,
                ),
                line(
                    sent[1],
                    [z for z in everyone if z >= count - slot and z > 0],
                    [z for z in everyone if slot + 1 < count and z < count - slot and z > 0],
                    -1,
                ),
            )
        )
    from_left, from_right = arrivals[-1]

    while steps_left:
        small_sum = sum_step(small_sum, steps_left.pop(0))
    inv_first = lax.rsqrt(
        small_sum[rows:].reshape(-1)[:rows][:, None] / features + EPSILON
    )
    small_early = (coefficients * small_sum[:rows]).astype(BF16)
    small_early_all = with_other_replicas(
        (small_early.astype(F32) * jnp.where(is_first, inv_first, 1.0)).astype(BF16)
    )
    low_product = jnp.where(
        is_first,
        jnp.dot(small_early, up, preferred_element_type=F32),
        lax.dot_general(small_early, down, CONTRACT_LAST, preferred_element_type=F32),
    )

    pulled_here = (gain_row * (sum(parts) + low_product)).astype(BF16)
    pulled = to_other_core(pulled_here, 1)
    from_left, from_right, *small_early_all, _ = lax.optimization_barrier(
        (from_left, from_right, *small_early_all, pulled_here)
    )

    projected = parts[-1] + from_left.astype(F32) + from_right.astype(F32) + low_product
    hidden = (token_float + inv_first * projected).astype(BF16)
    late_others = with_other_replicas(jnp.where(is_first, hidden, pulled_here))[1:]
    swap = [(0, 1), (1, 0)]
    swapped = [
        lax.ppermute(jnp.where(is_first, hidden, other), "section", swap) for other in early_all[1:]
    ]
    hidden_on_second = swapped[0] if swapped else to_other_core(hidden, 0)
    cotangent_all = [cotangent] + swapped
    hidden_here = jnp.where(is_first, hidden, hidden_on_second)
    hidden_float = hidden_here.astype(F32)
    pulled_float = pulled.astype(F32)
    row_sums = jnp.stack(
        [jnp.sum(hidden_float * hidden_float, axis=1), jnp.sum(hidden_float * pulled_float, axis=1)]
    )
    if count <= 4:
        row_sums = row_sums + sum(
            lax.ppermute(row_sums, "tensor", [(z, (z + step) % count) for z in everyone])
            for step in range(1, count)
        )
    else:
        for step in doubling_steps():
            row_sums = sum_step(row_sums, step, F32)
    inv_second = lax.rsqrt(row_sums[0] / features + EPSILON)[:, None]
    toward_hidden = row_sums[1][:, None] * inv_second * inv_second * inv_second / features
    hidden_grad = cotangent.astype(F32) + inv_second * pulled_float - toward_hidden * hidden_float
    late = jnp.where(
        is_first, hidden_grad.astype(BF16), (hidden_float * gain_row).astype(BF16)
    )
    rank_late = jnp.where(is_first, times_up_transposed(late), times_down(late))
    for step in doubling_steps():
        rank_late = sum_step(rank_late, step)

    swapped = [
        lax.ppermute(lax.optimization_barrier((other, rank_late))[0], "section", swap)
        for other in late_others
    ]
    hidden_all = [hidden_here] + [
        jnp.where(is_first, *pair) for pair in zip(late_others, swapped)
    ]
    pulled_all = [pulled] + swapped

    small_late = (coefficients * rank_late * jnp.where(is_first, inv_first, inv_second)).astype(BF16)
    small_late_all = with_other_replicas(
        jnp.concatenate(
            [
                small_late,
                jnp.broadcast_to(inv_second, (rows, 64)).astype(BF16),
                jnp.broadcast_to(toward_hidden, (rows, 64)).astype(BF16),
            ],
            axis=1,
        )
    )
    small_early_own = (
        small_early.astype(F32) * jnp.where(is_first, inv_first, inv_second)
    ).astype(BF16)
    sums = gradient_call(
        own_gradient_kernel,
        table, [], [early, late], [small_early_own, small_late], width, ranks, rows,
    )
    for at in range(1, replicas):
        sums = gradient_call(
            other_gradient_kernel,
            table,
            sums,
            [gain_row, early_all[at], cotangent_all[at], pulled_all[at], hidden_all[at]],
            [small_early_all[at], small_late_all[at]],
            width,
            ranks,
            rows,
        )
    grad_down, grad_up = sums
    return (grad_down[None], grad_up[None])


def solution(mesh):
    return jax.shard_map(
        on_device,
        mesh=mesh,
        in_specs=(
            P(("groups", "replica"), "tensor"),
            P(("groups", "replica"), "tensor"),
            P("section", "tensor"),
            P("section", "tensor", None),
            P("section", "tensor", None),
            P("section", None, "tensor"),
            P(),
            P(("groups", "replica")),
        ),
        out_specs=(P("section", "tensor", "groups"), P("section", "groups", "tensor")),
        check_vma=False,
    )
```

```python
import functools

import jax
import jax.numpy as jnp
from jax import lax
from jax.experimental import pallas as pl
from jax.experimental.pallas import tpu as pltpu
from jax.sharding import PartitionSpec as P

TENANT_COUNT = 4
EPSILON = 1e-05
CONTRACT_LAST = (((1,), (1,)), ((), ()))
CONTRACT_FIRST = (((0,), (0,)), ((), ()))
BF16 = jnp.bfloat16
F32 = jnp.float32
AHEAD = 2


def is_one_of(number, members):
    return functools.reduce(jnp.logical_or, [number == member for member in members])


def look_up(number, values):
    found = values[0]
    for value in sorted(set(values) - {values[0]}):
        found = jnp.where(
            is_one_of(number, [at for at, other in enumerate(values) if other == value]), value, found
        )
    return found


def block_kernel(table, value_ref, weight_ref, out_ref, wide, tall, arrived, *, blocks, tile, tiles):
    section = table[0]
    block = look_up(table[1], blocks)
    step = pl.program_id(0)
    width = tile * tiles

    def copy_of(index, is_wide):
        whole = pl.ds(pl.multiple_of(block * width, width), width)
        part = pl.ds(pl.multiple_of(block * width + index * tile, tile), tile)
        if is_wide:
            return pltpu.make_async_copy(weight_ref.at[:, part], wide.at[index], arrived.at[index])
        rows = pl.ds(pl.multiple_of(index * tile, tile), tile)
        return pltpu.make_async_copy(weight_ref.at[rows, whole], tall.at[index], arrived.at[index])

    for number, is_wide in ((0, True), (1, False)):

        @pl.when(section == number)
        def _():
            @pl.when(step == 0)
            def _():
                for index in range(min(AHEAD, tiles)):
                    copy_of(index, is_wide).start()

            @pl.when(step + AHEAD < tiles)
            def _():
                copy_of(step + AHEAD, is_wide).start()

            copy_of(step, is_wide).wait()
            if is_wide:
                out_ref[...] = jnp.dot(value_ref[...], wide[step], preferred_element_type=F32)
            else:
                out_ref[...] = lax.dot_general(
                    value_ref[...], tall[step], CONTRACT_LAST, preferred_element_type=F32
                )


def block_product(table, value, weight, blocks):
    rows, width = value.shape
    tile = min(512, width)
    tiles = width // tile
    return pl.pallas_call(
        functools.partial(block_kernel, blocks=blocks, tile=tile, tiles=tiles),
        grid_spec=pltpu.PrefetchScalarGridSpec(
            num_scalar_prefetch=1,
            grid=(tiles,),
            in_specs=[
                pl.BlockSpec((rows, width), lambda step, table: (0, 0)),
                pl.BlockSpec(memory_space=pl.ANY),
            ],
            out_specs=pl.BlockSpec((rows, tile), lambda step, table: (0, step)),
            scratch_shapes=[
                pltpu.VMEM((tiles, width, tile), BF16),
                pltpu.VMEM((tiles, tile, width), BF16),
                pltpu.SemaphoreType.DMA((tiles,)),
            ],
        ),
        out_shape=jax.ShapeDtypeStruct((rows, width), F32),
        compiler_params=pltpu.CompilerParams(vmem_limit_bytes=24 * 1024 * 1024),
        cost_estimate=pl.CostEstimate(
            flops=8 * rows * width * width, bytes_accessed=2 * width * width, transcendentals=0
        ),
    )(table, value, weight)


def transposed_times(left, right):
    return lax.dot_general(left, right, CONTRACT_FIRST, preferred_element_type=F32)


def own_gradient_kernel(table, early, late, small_early, small_late, down_ref, up_ref):
    @pl.when(table[0] == 0)
    def _():
        down_ref[...] = transposed_times(early[...], small_late[...])
        up_ref[...] = transposed_times(small_early[...], late[...])

    @pl.when(table[0] == 1)
    def _():
        down_ref[...] = transposed_times(late[...], small_early[...])
        up_ref[...] = transposed_times(small_late[...], early[...])


def other_gradient_kernel(
    table, down_sum, up_sum, early, late, small_early, beside, down_ref, up_ref
):
    ranks = down_ref.shape[1]
    small_late = beside[:, :ranks]

    @pl.when(table[0] == 0)
    def _():
        down_ref[...] = down_sum[...] + transposed_times(early[...], small_late)
        up_ref[...] = up_sum[...] + transposed_times(small_early[...], late[...])

    @pl.when(table[0] == 1)
    def _():
        scale = beside[:, ranks : ranks + 1].astype(F32)
        weighed = (small_early[...].astype(F32) * scale).astype(BF16)
        down_ref[...] = down_sum[...] + transposed_times(late[...], weighed)
        up_ref[...] = up_sum[...] + transposed_times(small_late, early[...])


def gradient_call(kernel, table, sums, by_column, whole, width, ranks, rows):
    tile = min(512, width)
    down_spec = pl.BlockSpec((tile, ranks), lambda step, table: (step, 0))
    up_spec = pl.BlockSpec((ranks, tile), lambda step, table: (0, step))
    return pl.pallas_call(
        kernel,
        grid_spec=pltpu.PrefetchScalarGridSpec(
            num_scalar_prefetch=1,
            grid=(width // tile,),
            in_specs=[down_spec, up_spec][: len(sums)]
            + [pl.BlockSpec((rows, tile), lambda step, table: (0, step)) for _ in by_column]
            + [pl.BlockSpec(array.shape, lambda step, table: (0, 0)) for array in whole],
            out_specs=[down_spec, up_spec],
        ),
        out_shape=[
            jax.ShapeDtypeStruct((width, ranks), F32),
            jax.ShapeDtypeStruct((ranks, width), F32),
        ],
        compiler_params=pltpu.CompilerParams(vmem_limit_bytes=20 * 1024 * 1024),
        cost_estimate=pl.CostEstimate(
            flops=4 * rows * width * ranks,
            bytes_accessed=8 * width * ranks * (1 + len(sums) // 2) + 2 * rows * width * len(by_column),
            transcendentals=0,
        ),
    )(table, *sums, *by_column, *whole)


def orders(count):
    first, first_slots, second, second_slots = [], [], [], []
    for z in range(count):
        sends = [(slot, 0, count - slot + z) for slot in range(z + 1, count)]
        sends += [(slot, 1, slot - count + z) for slot in range(count - z, count)]
        sends.sort()
        first.append([block for _, _, block in sends] + [z])
        first_slots.append({(slot, side): at for at, (slot, side, _) in enumerate(sends)})
        arrivals = [(slot, 0, z - 1 - slot) for slot in range(z)]
        arrivals += [(slot, 1, z + 1 + slot) for slot in range(count - 1 - z)]
        arrivals.sort()
        second.append([z] + [block for _, _, block in arrivals])
        second_slots.append([None] + [(slot, side) for slot, side, _ in arrivals])
    return first, first_slots, second, second_slots


def pick(number, choice, cases):
    chosen = cases[0]
    for at in range(1, len(cases)):
        members = [device for device, wanted in enumerate(choice) if wanted == at]
        chosen = jnp.where(is_one_of(number, members), cases[at], chosen)
    return chosen


def doubling_steps():
    count = lax.axis_size("tensor")
    return [
        [(place, place ^ (1 << bit)) for place in range(count)]
        for bit in range(count.bit_length() - 1)
    ]


def sum_step(value, pairs, wire=BF16, after=()):
    other = lax.ppermute(value.astype(wire), "tensor", pairs)
    if after:
        other = lax.optimization_barrier((other, *after))[0]
    return value + other.astype(F32)


def with_other_replicas(value, sections=(0, 1)):
    count = lax.axis_size("replica")
    return [value] + [
        lax.ppermute(
            value,
            ("section", "replica"),
            [(s * count + r, s * count + (r + step) % count) for s in sections for r in range(count)],
        )
        for step in range(1, count)
    ]


def to_other_core(value, source):
    return lax.ppermute(value, "section", [(source, 1 - source)])


def on_device(
    tokens,
    cotangent,
    gain,
    frozen_base_weight,
    adapter_down_factors,
    adapter_up_factors,
    tenant_adapter_scale,
    row_tenant_owner,
):
    section = lax.axis_index("section")
    place = lax.axis_index("tensor")
    count = lax.axis_size("tensor")
    is_first = section == 0
    weight = frozen_base_weight[0]
    gain_row = gain[0][None, :]
    down = adapter_down_factors[0]
    up = adapter_up_factors[0]
    rows, width = tokens.shape
    features = width * count
    ranks = down.shape[1]

    tenant_of_column = jnp.arange(ranks, dtype=jnp.int32) // (ranks // TENANT_COUNT)
    coefficients = jnp.where(
        row_tenant_owner[:, None] == tenant_of_column[None, :],
        jnp.repeat(tenant_adapter_scale, ranks // TENANT_COUNT)[None, :],
        0.0,
    )

    first_order, first_slots, second_order, second_slots = orders(count)
    place_of = section * count + place
    table = jnp.stack([section, place_of]).astype(jnp.int32)

    def times_down(value):
        return jnp.dot(value, down, preferred_element_type=F32)

    def times_up_transposed(value):
        return lax.dot_general(value, up, CONTRACT_LAST, preferred_element_type=F32)

    def line(value, first_pairs, second_pairs, toward):
        pairs = [(2 * z, 2 * (z + toward)) for z in first_pairs] + [
            (2 * z + 1, 2 * (z + toward) + 1) for z in second_pairs
        ]
        return lax.ppermute(value, ("tensor", "section"), pairs)

    token_float = tokens.astype(F32)
    early = jnp.where(is_first, (token_float * gain_row).astype(BF16), cotangent)
    early = lax.optimization_barrier(early)

    def small_columns(value, plain):
        small = jnp.where(is_first, times_down(value), times_up_transposed(value))
        squares = jnp.sum(plain.astype(F32) ** 2, axis=1)
        squares = jnp.pad(squares, (0, -rows % ranks)).reshape(-1, ranks)
        return jnp.concatenate([small, jnp.pad(squares, ((0, -len(squares) % 16), (0, 0)))], axis=0)

    everyone = range(count)
    steps_left = doubling_steps()
    arrivals = [
        (
            lax.ppermute(
                cotangent,
                ("tensor", "section"),
                [(2 * z, 2 * (z + 1) + 1) for z in everyone if z + 1 < count],
            ),
            line(cotangent, [], [z for z in everyone if z > 0], -1),
        )
    ]
    token_others = with_other_replicas(tokens, (0,))[1:]

    parts = []
    for stage in range(count):
        wanted = [None if stage == 0 else second_slots[z][stage] for z in everyone]
        cases = sorted({slot for slot in wanted if slot is not None})
        here = [early] + [arrivals[slot][side] for slot, side in cases]
        if stage == 1:
            small_sum = small_columns(*lax.optimization_barrier((early, tokens, *sent))[:2])
        elif stage > 1 and steps_left:
            small_sum = sum_step(small_sum, steps_left.pop(0), after=sent)
        if stage == 1:
            small_sum, *token_others = lax.optimization_barrier((small_sum, *token_others))
        if stage > 0:
            *here, small_sum = lax.optimization_barrier((*here, small_sum, *sent))[: len(here) + 1]
        value = pick(
            place_of,
            [0] * count + [0 if slot is None else 1 + cases.index(slot) for slot in wanted],
            here,
        )
        order = [blocks[stage] for blocks in first_order + second_order]
        part = block_product(table, value, weight, order)
        parts.append(part)
        slot = stage + 1
        if slot == count:
            break
        sent = []
        for side in (0, 1):
            needed = [first_slots[z].get((slot, side)) for z in everyone]
            stages = sorted({at for at in needed if at is not None})
            own = pick(
                place_of,
                [0 if at is None else stages.index(at) for at in needed] + [0] * count,
                [parts[at] for at in stages],
            )
            arrived = arrivals[-1][side]
            if side == 1:
                arrived, _ = lax.optimization_barrier((arrived, sent[0]))
            arrived = arrived.astype(F32)
            sent.append((arrived + jnp.where(is_first, own, 0.0)).astype(BF16))
        arrivals.append(
            (
                line(
                    sent[0],
                    [z for z in everyone if z < slot and z + 1 < count],
                    [z for z in everyone if slot + 1 < count and z >= slot and z + 1 < count],
                    1,
                ),
                line(
                    sent[1],
                    [z for z in everyone if z >= count - slot and z > 0],
                    [z for z in everyone if slot + 1 < count and z < count - slot and z > 0],
                    -1,
                ),
            )
        )
    from_left, from_right = arrivals[-1]

    while steps_left:
        small_sum = sum_step(small_sum, steps_left.pop(0))
    cotangent_others = with_other_replicas(
        lax.optimization_barrier((cotangent, *sent))[0], (1,)
    )[1:]
    inv_first = lax.rsqrt(
        small_sum[rows:].reshape(-1)[:rows][:, None] / features + EPSILON
    )
    small_early = (coefficients * small_sum[:rows]).astype(BF16)
    small_early_all = with_other_replicas(
        (small_early.astype(F32) * jnp.where(is_first, inv_first, 1.0)).astype(BF16)
    )
    low_product = jnp.where(
        is_first,
        jnp.dot(small_early, up, preferred_element_type=F32),
        lax.dot_general(small_early, down, CONTRACT_LAST, preferred_element_type=F32),
    )

    pulled_here = (gain_row * (sum(parts) + low_product)).astype(BF16)
    pulled = to_other_core(pulled_here, 1)
    from_left, from_right, _, *cotangent_others = lax.optimization_barrier(
        (from_left, from_right, pulled_here, *cotangent_others)
    )

    projected = parts[-1] + from_left.astype(F32) + from_right.astype(F32) + low_product
    hidden = (token_float + inv_first * projected).astype(BF16)
    hidden_on_second = to_other_core(hidden, 0)
    scaled_second = lax.optimization_barrier(
        (hidden_on_second.astype(F32) * gain_row).astype(BF16)
    )
    scaled_others = with_other_replicas(scaled_second, (1,))[1:]
    early_others = [
        jnp.where(is_first, (other.astype(F32) * gain_row).astype(BF16), same)
        for other, same in zip(token_others, cotangent_others)
    ]

    hidden_float = hidden.astype(F32)
    pulled_float = pulled.astype(F32)
    row_sums = jnp.stack(
        [jnp.sum(hidden_float * hidden_float, axis=1), jnp.sum(hidden_float * pulled_float, axis=1)]
    )

    def on_first(value, pairs):
        return lax.ppermute(value, ("tensor", "section"), [(2 * z, 2 * to) for z, to in pairs])

    if count <= 4:
        row_sums = row_sums + sum(
            on_first(row_sums, [(z, (z + step) % count) for z in everyone])
            for step in range(1, count)
        )
    else:
        for step in doubling_steps():
            row_sums = row_sums + on_first(row_sums, step)
    row_sums, *small_early_all = lax.optimization_barrier((row_sums, *small_early_all))
    inv_second = lax.rsqrt(row_sums[0] / features + EPSILON)
    inv_on_second = to_other_core(inv_second, 0)[:, None]
    inv_second = inv_second[:, None]
    toward_hidden = row_sums[1][:, None] * inv_second * inv_second * inv_second / features
    hidden_grad = cotangent.astype(F32) + inv_second * pulled_float - toward_hidden * hidden_float
    late = jnp.where(is_first, hidden_grad.astype(BF16), scaled_second)
    grad_others = with_other_replicas(late, (0,))[1:]
    rank_late = jnp.where(is_first, times_up_transposed(late), times_down(late))
    for at, step in enumerate(doubling_steps()):
        rank_late = sum_step(rank_late, step)
        if at == 0:
            rank_late, *scaled_others = lax.optimization_barrier((rank_late, *scaled_others))
    row_scale = jnp.where(is_first, inv_first, inv_on_second)
    small_late = (coefficients * rank_late * row_scale).astype(BF16)
    beside = jnp.concatenate(
        [small_late, jnp.broadcast_to(inv_on_second, (rows, 128)).astype(BF16)], axis=1
    )
    beside, *grad_others = lax.optimization_barrier((beside, *grad_others))
    small_late_others = with_other_replicas(beside)[1:]
    late_others = [jnp.where(is_first, *pair) for pair in zip(grad_others, scaled_others)]
    small_early_own = (small_early.astype(F32) * row_scale).astype(BF16)
    sums = gradient_call(
        own_gradient_kernel,
        table, [], [early, late], [small_early_own, small_late], width, ranks, rows,
    )
    for early_other, late_other, small_other, beside_other in zip(
        early_others, late_others, small_early_all[1:], small_late_others
    ):
        sums = gradient_call(
            other_gradient_kernel,
            table, sums, [early_other, late_other], [small_other, beside_other], width, ranks, rows,
        )
    grad_down, grad_up = sums
    return (grad_down[None], grad_up[None])


def solution(mesh):
    return jax.shard_map(
        on_device,
        mesh=mesh,
        in_specs=(
            P(("groups", "replica"), "tensor"),
            P(("groups", "replica"), "tensor"),
            P("section", "tensor"),
            P("section", "tensor", None),
            P("section", "tensor", None),
            P("section", None, "tensor"),
            P(),
            P(("groups", "replica")),
        ),
        out_specs=(P("section", "tensor", "groups"), P("section", "groups", "tensor")),
        check_vma=False,
    )
```

```python
import functools

import jax
import jax.numpy as jnp
from jax import lax
from jax.experimental import pallas as pl
from jax.experimental.pallas import tpu as pltpu
from jax.sharding import PartitionSpec as P

TENANT_COUNT = 4
EPSILON = 1e-05
CONTRACT_LAST = (((1,), (1,)), ((), ()))
CONTRACT_FIRST = (((0,), (0,)), ((), ()))
BF16 = jnp.bfloat16
F32 = jnp.float32
AHEAD = 2


def is_one_of(number, members):
    return functools.reduce(jnp.logical_or, [number == member for member in members])


def look_up(number, values):
    found = values[0]
    for value in sorted(set(values) - {values[0]}):
        found = jnp.where(
            is_one_of(number, [at for at, other in enumerate(values) if other == value]), value, found
        )
    return found


def block_kernel(table, value_ref, weight_ref, out_ref, wide, tall, arrived, *, blocks, tile, tiles):
    section = table[0]
    block = look_up(table[1], blocks)
    step = pl.program_id(0)
    width = tile * tiles

    def copy_of(index, is_wide):
        whole = pl.ds(pl.multiple_of(block * width, width), width)
        part = pl.ds(pl.multiple_of(block * width + index * tile, tile), tile)
        if is_wide:
            return pltpu.make_async_copy(weight_ref.at[:, part], wide.at[index], arrived.at[index])
        rows = pl.ds(pl.multiple_of(index * tile, tile), tile)
        return pltpu.make_async_copy(weight_ref.at[rows, whole], tall.at[index], arrived.at[index])

    for number, is_wide in ((0, True), (1, False)):

        @pl.when(section == number)
        def _():
            @pl.when(step == 0)
            def _():
                for index in range(min(AHEAD, tiles)):
                    copy_of(index, is_wide).start()

            @pl.when(step + AHEAD < tiles)
            def _():
                copy_of(step + AHEAD, is_wide).start()

            copy_of(step, is_wide).wait()
            if is_wide:
                out_ref[...] = jnp.dot(value_ref[...], wide[step], preferred_element_type=F32)
            else:
                out_ref[...] = lax.dot_general(
                    value_ref[...], tall[step], CONTRACT_LAST, preferred_element_type=F32
                )


def block_product(table, value, weight, blocks):
    rows, width = value.shape
    tile = min(512, width)
    tiles = width // tile
    return pl.pallas_call(
        functools.partial(block_kernel, blocks=blocks, tile=tile, tiles=tiles),
        grid_spec=pltpu.PrefetchScalarGridSpec(
            num_scalar_prefetch=1,
            grid=(tiles,),
            in_specs=[
                pl.BlockSpec((rows, width), lambda step, table: (0, 0)),
                pl.BlockSpec(memory_space=pl.ANY),
            ],
            out_specs=pl.BlockSpec((rows, tile), lambda step, table: (0, step)),
            scratch_shapes=[
                pltpu.VMEM((tiles, width, tile), BF16),
                pltpu.VMEM((tiles, tile, width), BF16),
                pltpu.SemaphoreType.DMA((tiles,)),
            ],
        ),
        out_shape=jax.ShapeDtypeStruct((rows, width), F32),
        compiler_params=pltpu.CompilerParams(vmem_limit_bytes=24 * 1024 * 1024),
        cost_estimate=pl.CostEstimate(
            flops=8 * rows * width * width, bytes_accessed=2 * width * width, transcendentals=0
        ),
    )(table, value, weight)


def transposed_times(left, right):
    return lax.dot_general(left, right, CONTRACT_FIRST, preferred_element_type=F32)


def own_gradient_kernel(table, early, late, small_early, small_late, down_ref, up_ref):
    @pl.when(table[0] == 0)
    def _():
        down_ref[...] = transposed_times(early[...], small_late[...])
        up_ref[...] = transposed_times(small_early[...], late[...])

    @pl.when(table[0] == 1)
    def _():
        down_ref[...] = transposed_times(late[...], small_early[...])
        up_ref[...] = transposed_times(small_late[...], early[...])


def other_gradient_kernel(
    table, gain_ref, down_sum, up_sum, early, cotangent, pulled, hidden, small_early, small_late,
    down_ref, up_ref,
):
    ranks = down_ref.shape[1]
    late = small_late[:, :ranks]
    inverse = small_late[:, ranks : ranks + 1].astype(F32)
    toward = small_late[:, ranks + 64 : ranks + 65].astype(F32)

    @pl.when(table[0] == 0)
    def _():
        grad = (
            cotangent[...].astype(F32)
            + inverse * pulled[...].astype(F32)
            - toward * hidden[...].astype(F32)
        ).astype(BF16)
        down_ref[...] = down_sum[...] + transposed_times(early[...], late)
        up_ref[...] = up_sum[...] + transposed_times(small_early[...], grad)

    @pl.when(table[0] == 1)
    def _():
        scaled = (hidden[...].astype(F32) * gain_ref[...]).astype(BF16)
        weighed = (small_early[...].astype(F32) * inverse).astype(BF16)
        down_ref[...] = down_sum[...] + transposed_times(scaled, weighed)
        up_ref[...] = up_sum[...] + transposed_times(late, early[...])


def gradient_call(kernel, table, sums, by_column, whole, width, ranks, rows):
    tile = min(512, width)
    down_spec = pl.BlockSpec((tile, ranks), lambda step, table: (step, 0))
    up_spec = pl.BlockSpec((ranks, tile), lambda step, table: (0, step))
    leading = [array for array in by_column if array.shape[0] == 1]
    columns = [array for array in by_column if array.shape[0] != 1]
    return pl.pallas_call(
        kernel,
        grid_spec=pltpu.PrefetchScalarGridSpec(
            num_scalar_prefetch=1,
            grid=(width // tile,),
            in_specs=[pl.BlockSpec((1, tile), lambda step, table: (0, step)) for _ in leading]
            + [down_spec, up_spec][: len(sums)]
            + [pl.BlockSpec((rows, tile), lambda step, table: (0, step)) for _ in columns]
            + [pl.BlockSpec(array.shape, lambda step, table: (0, 0)) for array in whole],
            out_specs=[down_spec, up_spec],
        ),
        out_shape=[
            jax.ShapeDtypeStruct((width, ranks), F32),
            jax.ShapeDtypeStruct((ranks, width), F32),
        ],
        compiler_params=pltpu.CompilerParams(vmem_limit_bytes=20 * 1024 * 1024),
        cost_estimate=pl.CostEstimate(
            flops=4 * rows * width * ranks,
            bytes_accessed=8 * width * ranks * (1 + len(sums) // 2) + 2 * rows * width * len(columns),
            transcendentals=0,
        ),
    )(table, *leading, *sums, *columns, *whole)


def orders(count):
    first, first_slots, second, second_slots = [], [], [], []
    for z in range(count):
        sends = [(slot, 0, count - slot + z) for slot in range(z + 1, count)]
        sends += [(slot, 1, slot - count + z) for slot in range(count - z, count)]
        sends.sort()
        first.append([block for _, _, block in sends] + [z])
        first_slots.append({(slot, side): at for at, (slot, side, _) in enumerate(sends)})
        arrivals = [(slot, 0, z - 1 - slot) for slot in range(z)]
        arrivals += [(slot, 1, z + 1 + slot) for slot in range(count - 1 - z)]
        arrivals.sort()
        second.append([z] + [block for _, _, block in arrivals])
        second_slots.append([None] + [(slot, side) for slot, side, _ in arrivals])
    return first, first_slots, second, second_slots


def pick(number, choice, cases):
    chosen = cases[0]
    for at in range(1, len(cases)):
        members = [device for device, wanted in enumerate(choice) if wanted == at]
        chosen = jnp.where(is_one_of(number, members), cases[at], chosen)
    return chosen


def doubling_steps():
    count = lax.axis_size("tensor")
    return [
        [(place, place ^ (1 << bit)) for place in range(count)]
        for bit in range(count.bit_length() - 1)
    ]


def sum_step(value, pairs, wire=BF16, after=()):
    other = lax.ppermute(value.astype(wire), "tensor", pairs)
    if after:
        other = lax.optimization_barrier((other, *after))[0]
    return value + other.astype(F32)


def with_other_replicas(value, sections=(0, 1)):
    count = lax.axis_size("replica")
    return [value] + [
        lax.ppermute(
            value,
            ("section", "replica"),
            [(s * count + r, s * count + (r + step) % count) for s in sections for r in range(count)],
        )
        for step in range(1, count)
    ]


def on_device(
    tokens,
    cotangent,
    gain,
    frozen_base_weight,
    adapter_down_factors,
    adapter_up_factors,
    tenant_adapter_scale,
    row_tenant_owner,
):
    section = lax.axis_index("section")
    place = lax.axis_index("tensor")
    count = lax.axis_size("tensor")
    is_first = section == 0
    weight = frozen_base_weight[0]
    gain_row = gain[0][None, :]
    down = adapter_down_factors[0]
    up = adapter_up_factors[0]
    rows, width = tokens.shape
    features = width * count
    replicas = lax.axis_size("replica")
    ranks = down.shape[1]

    tenant_of_column = jnp.arange(ranks, dtype=jnp.int32) // (ranks // TENANT_COUNT)
    coefficients = jnp.where(
        row_tenant_owner[:, None] == tenant_of_column[None, :],
        jnp.repeat(tenant_adapter_scale, ranks // TENANT_COUNT)[None, :],
        0.0,
    )

    first_order, first_slots, second_order, second_slots = orders(count)
    place_of = section * count + place
    table = jnp.stack([section, place_of]).astype(jnp.int32)

    def times_down(value):
        return jnp.dot(value, down, preferred_element_type=F32)

    def times_up_transposed(value):
        return lax.dot_general(value, up, CONTRACT_LAST, preferred_element_type=F32)

    def line(value, first_pairs, second_pairs, toward):
        pairs = [(2 * z, 2 * (z + toward)) for z in first_pairs] + [
            (2 * z + 1, 2 * (z + toward) + 1) for z in second_pairs
        ]
        return lax.ppermute(value, ("tensor", "section"), pairs)

    token_float = tokens.astype(F32)
    early = jnp.where(is_first, (token_float * gain_row).astype(BF16), cotangent)
    early = lax.optimization_barrier(early)

    def small_columns(value, plain):
        small = jnp.where(is_first, times_down(value), times_up_transposed(value))
        squares = jnp.sum(plain.astype(F32) ** 2, axis=1)
        squares = jnp.pad(squares, (0, -rows % ranks)).reshape(-1, ranks)
        return jnp.concatenate([small, jnp.pad(squares, ((0, -len(squares) % 16), (0, 0)))], axis=0)

    everyone = range(count)
    steps_left = doubling_steps()
    arrivals = [
        (
            lax.ppermute(
                cotangent,
                ("tensor", "section"),
                [(2 * z, 2 * (z + 1) + 1) for z in everyone if z + 1 < count],
            ),
            line(cotangent, [], [z for z in everyone if z > 0], -1),
        )
    ]
    parts = []
    for stage in range(count):
        wanted = [None if stage == 0 else second_slots[z][stage] for z in everyone]
        cases = sorted({slot for slot in wanted if slot is not None})
        here = [early] + [arrivals[slot][side] for slot, side in cases]
        if stage == 1:
            small_sum = small_columns(*lax.optimization_barrier((early, tokens, *sent))[:2])
        elif stage > 1 and steps_left:
            small_sum = sum_step(small_sum, steps_left.pop(0), after=sent)
        if stage > 0:
            *here, small_sum = lax.optimization_barrier((*here, small_sum, *sent))[: len(here) + 1]
        value = pick(
            place_of,
            [0] * count + [0 if slot is None else 1 + cases.index(slot) for slot in wanted],
            here,
        )
        order = [blocks[stage] for blocks in first_order + second_order]
        part = block_product(table, value, weight, order)
        if stage == 1:
            part, after = lax.optimization_barrier((part, early))
            early_all = [early] + with_other_replicas(after)[1:]
        if stage == count - 1:
            part, *early_all = lax.optimization_barrier((part, *early_all))
        parts.append(part)
        slot = stage + 1
        if slot == count:
            break
        sent = []
        for side in (0, 1):
            needed = [first_slots[z].get((slot, side)) for z in everyone]
            stages = sorted({at for at in needed if at is not None})
            own = pick(
                place_of,
                [0 if at is None else stages.index(at) for at in needed] + [0] * count,
                [parts[at] for at in stages],
            )
            arrived = arrivals[-1][side]
            if side == 1:
                arrived, _ = lax.optimization_barrier((arrived, sent[0]))
            arrived = arrived.astype(F32)
            sent.append((arrived + jnp.where(is_first, own, 0.0)).astype(BF16))
        arrivals.append(
            (
                line(
                    sent[0],
                    [z for z in everyone if z < slot and z + 1 < count],
                    [z for z in everyone if slot + 1 < count and z >= slot and z + 1 < count],
                    1,
                ),
                line(
                    sent[1],
                    [z for z in everyone if z >= count - slot and z > 0],
                    [z for z in everyone if slot + 1 < count and z < count - slot and z > 0],
                    -1,
                ),
            )
        )
    from_left, from_right = arrivals[-1]

    while steps_left:
        small_sum = sum_step(small_sum, steps_left.pop(0))
    inv_first = lax.rsqrt(
        small_sum[rows:].reshape(-1)[:rows][:, None] / features + EPSILON
    )
    small_early = (coefficients * small_sum[:rows]).astype(BF16)
    small_early_all = with_other_replicas(
        (small_early.astype(F32) * jnp.where(is_first, inv_first, 1.0)).astype(BF16)
    )
    low_product = jnp.where(
        is_first,
        jnp.dot(small_early, up, preferred_element_type=F32),
        lax.dot_general(small_early, down, CONTRACT_LAST, preferred_element_type=F32),
    )

    pulled_here = (gain_row * (sum(parts) + low_product)).astype(BF16)
    swap = [(0, 1), (1, 0)]
    pulled = lax.ppermute(pulled_here, "section", swap)
    pulled_others = with_other_replicas(pulled_here, (1,))[1:]
    from_left, from_right, _, *pulled_others = lax.optimization_barrier(
        (from_left, from_right, pulled_here, *pulled_others)
    )

    projected = parts[-1] + from_left.astype(F32) + from_right.astype(F32) + low_product
    hidden = (token_float + inv_first * projected).astype(BF16)
    hidden_others = with_other_replicas(hidden, (0,))[1:]
    swapped = [
        lax.ppermute(jnp.where(is_first, hidden, other), "section", swap) for other in early_all[1:]
    ]
    hidden_on_second = swapped[0] if swapped else lax.ppermute(hidden, "section", swap)
    cotangent_all = [cotangent] + swapped
    hidden_float = hidden.astype(F32)
    pulled_float = pulled.astype(F32)
    row_sums = jnp.stack(
        [jnp.sum(hidden_float * hidden_float, axis=1), jnp.sum(hidden_float * pulled_float, axis=1)]
    )
    if count <= 4:
        row_sums = row_sums + sum(
            lax.ppermute(row_sums, "tensor", [(z, (z + step) % count) for z in everyone])
            for step in range(1, count)
        )
    else:
        for step in doubling_steps():
            row_sums = sum_step(row_sums, step, F32)
    row_sums, *small_early_all = lax.optimization_barrier((row_sums, *small_early_all))
    inv_second = lax.rsqrt(row_sums[0] / features + EPSILON)
    inv_on_second = lax.ppermute(inv_second, "section", swap)[:, None]
    inv_second = inv_second[:, None]
    toward_hidden = row_sums[1][:, None] * inv_second * inv_second * inv_second / features
    hidden_grad = cotangent.astype(F32) + inv_second * pulled_float - toward_hidden * hidden_float
    late = jnp.where(
        is_first,
        hidden_grad.astype(BF16),
        (hidden_on_second.astype(F32) * gain_row).astype(BF16),
    )
    rank_late = jnp.where(is_first, times_up_transposed(late), times_down(late))
    for step in doubling_steps():
        rank_late = sum_step(rank_late, step)

    inv_second = jnp.where(is_first, inv_second, inv_on_second)
    row_scale = jnp.where(is_first, inv_first, inv_second)
    small_late = (coefficients * rank_late * row_scale).astype(BF16)
    beside = jnp.concatenate(
        [
            small_late,
            jnp.broadcast_to(inv_second, (rows, 64)).astype(BF16),
            jnp.broadcast_to(toward_hidden, (rows, 64)).astype(BF16),
        ],
        axis=1,
    )
    small_late_all = with_other_replicas(beside)
    swapped = [
        lax.ppermute(
            lax.optimization_barrier((jnp.where(is_first, *pair), beside))[0], "section", swap
        )
        for pair in zip(hidden_others, pulled_others)
    ]
    hidden_all = [hidden] + [jnp.where(is_first, *pair) for pair in zip(hidden_others, swapped)]
    pulled_all = [pulled] + swapped
    small_early_own = (small_early.astype(F32) * row_scale).astype(BF16)
    sums = gradient_call(
        own_gradient_kernel,
        table, [], [early, late], [small_early_own, small_late], width, ranks, rows,
    )
    for at in range(1, replicas):
        sums = gradient_call(
            other_gradient_kernel,
            table,
            sums,
            [gain_row, early_all[at], cotangent_all[at], pulled_all[at], hidden_all[at]],
            [small_early_all[at], small_late_all[at]],
            width,
            ranks,
            rows,
        )
    grad_down, grad_up = sums
    return (grad_down[None], grad_up[None])


def solution(mesh):
    return jax.shard_map(
        on_device,
        mesh=mesh,
        in_specs=(
            P(("groups", "replica"), "tensor"),
            P(("groups", "replica"), "tensor"),
            P("section", "tensor"),
            P("section", "tensor", None),
            P("section", "tensor", None),
            P("section", None, "tensor"),
            P(),
            P(("groups", "replica")),
        ),
        out_specs=(P("section", "tensor", "groups"), P("section", "groups", "tensor")),
        check_vma=False,
    )
```

```python
import functools

import jax
import jax.numpy as jnp
from jax import lax
from jax.experimental import pallas as pl
from jax.experimental.pallas import tpu as pltpu
from jax.sharding import PartitionSpec as P

TENANT_COUNT = 4
EPSILON = 1e-05
CONTRACT_LAST = (((1,), (1,)), ((), ()))
CONTRACT_FIRST = (((0,), (0,)), ((), ()))
BF16 = jnp.bfloat16
F32 = jnp.float32
AHEAD = 2


def is_one_of(number, members):
    return functools.reduce(jnp.logical_or, [number == member for member in members])


def look_up(number, values):
    found = values[0]
    for value in sorted(set(values) - {values[0]}):
        found = jnp.where(
            is_one_of(number, [at for at, other in enumerate(values) if other == value]), value, found
        )
    return found


def block_kernel(table, value_ref, weight_ref, out_ref, wide, tall, arrived, *, blocks, tile, tiles):
    section = table[0]
    block = look_up(table[1], blocks)
    step = pl.program_id(0)
    width = tile * tiles

    def copy_of(index, is_wide):
        whole = pl.ds(pl.multiple_of(block * width, width), width)
        part = pl.ds(pl.multiple_of(block * width + index * tile, tile), tile)
        if is_wide:
            return pltpu.make_async_copy(weight_ref.at[:, part], wide.at[index], arrived.at[index])
        rows = pl.ds(pl.multiple_of(index * tile, tile), tile)
        return pltpu.make_async_copy(weight_ref.at[rows, whole], tall.at[index], arrived.at[index])

    for number, is_wide in ((0, True), (1, False)):

        @pl.when(section == number)
        def _():
            @pl.when(step == 0)
            def _():
                for index in range(min(AHEAD, tiles)):
                    copy_of(index, is_wide).start()

            @pl.when(step + AHEAD < tiles)
            def _():
                copy_of(step + AHEAD, is_wide).start()

            copy_of(step, is_wide).wait()
            if is_wide:
                out_ref[...] = jnp.dot(value_ref[...], wide[step], preferred_element_type=F32)
            else:
                out_ref[...] = lax.dot_general(
                    value_ref[...], tall[step], CONTRACT_LAST, preferred_element_type=F32
                )


def block_product(table, value, weight, blocks):
    rows, width = value.shape
    tile = min(512, width)
    tiles = width // tile
    return pl.pallas_call(
        functools.partial(block_kernel, blocks=blocks, tile=tile, tiles=tiles),
        grid_spec=pltpu.PrefetchScalarGridSpec(
            num_scalar_prefetch=1,
            grid=(tiles,),
            in_specs=[
                pl.BlockSpec((rows, width), lambda step, table: (0, 0)),
                pl.BlockSpec(memory_space=pl.ANY),
            ],
            out_specs=pl.BlockSpec((rows, tile), lambda step, table: (0, step)),
            scratch_shapes=[
                pltpu.VMEM((tiles, width, tile), BF16),
                pltpu.VMEM((tiles, tile, width), BF16),
                pltpu.SemaphoreType.DMA((tiles,)),
            ],
        ),
        out_shape=jax.ShapeDtypeStruct((rows, width), F32),
        compiler_params=pltpu.CompilerParams(vmem_limit_bytes=24 * 1024 * 1024),
        cost_estimate=pl.CostEstimate(
            flops=8 * rows * width * width, bytes_accessed=2 * width * width, transcendentals=0
        ),
    )(table, value, weight)


def transposed_times(left, right):
    return lax.dot_general(left, right, CONTRACT_FIRST, preferred_element_type=F32)


def own_gradient_kernel(table, early, late, small_early, small_late, down_ref, up_ref):
    @pl.when(table[0] == 0)
    def _():
        down_ref[...] = transposed_times(early[...], small_late[...])
        up_ref[...] = transposed_times(small_early[...], late[...])

    @pl.when(table[0] == 1)
    def _():
        down_ref[...] = transposed_times(late[...], small_early[...])
        up_ref[...] = transposed_times(small_late[...], early[...])


def other_gradient_kernel(
    table, gain_ref, down_sum, up_sum, early, cotangent, pulled, hidden, small_early, small_late,
    down_ref, up_ref,
):
    ranks = down_ref.shape[1]
    late = small_late[:, :ranks]
    inverse = small_late[:, ranks : ranks + 1].astype(F32)
    toward = small_late[:, ranks + 64 : ranks + 65].astype(F32)

    @pl.when(table[0] == 0)
    def _():
        grad = (
            cotangent[...].astype(F32)
            + inverse * pulled[...].astype(F32)
            - toward * hidden[...].astype(F32)
        ).astype(BF16)
        down_ref[...] = down_sum[...] + transposed_times(early[...], late)
        up_ref[...] = up_sum[...] + transposed_times(small_early[...], grad)

    @pl.when(table[0] == 1)
    def _():
        scaled = (hidden[...].astype(F32) * gain_ref[...]).astype(BF16)
        weighed = (small_early[...].astype(F32) * inverse).astype(BF16)
        down_ref[...] = down_sum[...] + transposed_times(scaled, weighed)
        up_ref[...] = up_sum[...] + transposed_times(late, early[...])


def gradient_call(kernel, table, sums, by_column, whole, width, ranks, rows):
    tile = min(512, width)
    down_spec = pl.BlockSpec((tile, ranks), lambda step, table: (step, 0))
    up_spec = pl.BlockSpec((ranks, tile), lambda step, table: (0, step))
    leading = [array for array in by_column if array.shape[0] == 1]
    columns = [array for array in by_column if array.shape[0] != 1]
    return pl.pallas_call(
        kernel,
        grid_spec=pltpu.PrefetchScalarGridSpec(
            num_scalar_prefetch=1,
            grid=(width // tile,),
            in_specs=[pl.BlockSpec((1, tile), lambda step, table: (0, step)) for _ in leading]
            + [down_spec, up_spec][: len(sums)]
            + [pl.BlockSpec((rows, tile), lambda step, table: (0, step)) for _ in columns]
            + [pl.BlockSpec(array.shape, lambda step, table: (0, 0)) for array in whole],
            out_specs=[down_spec, up_spec],
        ),
        out_shape=[
            jax.ShapeDtypeStruct((width, ranks), F32),
            jax.ShapeDtypeStruct((ranks, width), F32),
        ],
        compiler_params=pltpu.CompilerParams(vmem_limit_bytes=20 * 1024 * 1024),
        cost_estimate=pl.CostEstimate(
            flops=4 * rows * width * ranks,
            bytes_accessed=8 * width * ranks * (1 + len(sums) // 2) + 2 * rows * width * len(columns),
            transcendentals=0,
        ),
    )(table, *leading, *sums, *columns, *whole)


def orders(count):
    first, first_slots, second, second_slots = [], [], [], []
    for z in range(count):
        sends = [(slot, 0, count - slot + z) for slot in range(z + 1, count)]
        sends += [(slot, 1, slot - count + z) for slot in range(count - z, count)]
        sends.sort()
        first.append([block for _, _, block in sends] + [z])
        first_slots.append({(slot, side): at for at, (slot, side, _) in enumerate(sends)})
        arrivals = [(slot, 0, z - 1 - slot) for slot in range(z)]
        arrivals += [(slot, 1, z + 1 + slot) for slot in range(count - 1 - z)]
        arrivals.sort()
        second.append([z] + [block for _, _, block in arrivals])
        second_slots.append([None] + [(slot, side) for slot, side, _ in arrivals])
    return first, first_slots, second, second_slots


def pick(number, choice, cases):
    chosen = cases[0]
    for at in range(1, len(cases)):
        members = [device for device, wanted in enumerate(choice) if wanted == at]
        chosen = jnp.where(is_one_of(number, members), cases[at], chosen)
    return chosen


def doubling_steps():
    count = lax.axis_size("tensor")
    return [
        [(place, place ^ (1 << bit)) for place in range(count)]
        for bit in range(count.bit_length() - 1)
    ]


def sum_step(value, pairs, wire=BF16, after=()):
    other = lax.ppermute(value.astype(wire), "tensor", pairs)
    if after:
        other = lax.optimization_barrier((other, *after))[0]
    return value + other.astype(F32)


def with_other_replicas(value, sections=(0, 1)):
    count = lax.axis_size("replica")
    return [value] + [
        lax.ppermute(
            value,
            ("section", "replica"),
            [(s * count + r, s * count + (r + step) % count) for s in sections for r in range(count)],
        )
        for step in range(1, count)
    ]


def on_device(
    tokens,
    cotangent,
    gain,
    frozen_base_weight,
    adapter_down_factors,
    adapter_up_factors,
    tenant_adapter_scale,
    row_tenant_owner,
):
    section = lax.axis_index("section")
    place = lax.axis_index("tensor")
    count = lax.axis_size("tensor")
    is_first = section == 0
    weight = frozen_base_weight[0]
    gain_row = gain[0][None, :]
    down = adapter_down_factors[0]
    up = adapter_up_factors[0]
    rows, width = tokens.shape
    features = width * count
    replicas = lax.axis_size("replica")
    ranks = down.shape[1]

    tenant_of_column = jnp.arange(ranks, dtype=jnp.int32) // (ranks // TENANT_COUNT)
    coefficients = jnp.where(
        row_tenant_owner[:, None] == tenant_of_column[None, :],
        jnp.repeat(tenant_adapter_scale, ranks // TENANT_COUNT)[None, :],
        0.0,
    )

    first_order, first_slots, second_order, second_slots = orders(count)
    place_of = section * count + place
    table = jnp.stack([section, place_of]).astype(jnp.int32)

    def times_down(value):
        return jnp.dot(value, down, preferred_element_type=F32)

    def times_up_transposed(value):
        return lax.dot_general(value, up, CONTRACT_LAST, preferred_element_type=F32)

    def line(value, first_pairs, second_pairs, toward):
        pairs = [(2 * z, 2 * (z + toward)) for z in first_pairs] + [
            (2 * z + 1, 2 * (z + toward) + 1) for z in second_pairs
        ]
        return lax.ppermute(value, ("tensor", "section"), pairs)

    token_float = tokens.astype(F32)
    early = jnp.where(is_first, (token_float * gain_row).astype(BF16), cotangent)
    early = lax.optimization_barrier(early)

    def small_columns(value, plain):
        small = jnp.where(is_first, times_down(value), times_up_transposed(value))
        squares = jnp.sum(plain.astype(F32) ** 2, axis=1)
        squares = jnp.pad(squares, (0, -rows % ranks)).reshape(-1, ranks)
        return jnp.concatenate([small, jnp.pad(squares, ((0, -len(squares) % 16), (0, 0)))], axis=0)

    everyone = range(count)
    steps_left = doubling_steps()
    arrivals = [
        (
            line(early, [], [z for z in everyone if z + 1 < count], 1),
            line(early, [], [z for z in everyone if z > 0], -1),
        )
    ]
    parts = []
    for stage in range(count):
        wanted = [None if stage == 0 else second_slots[z][stage] for z in everyone]
        cases = sorted({slot for slot in wanted if slot is not None})
        here = [early] + [arrivals[slot][side] for slot, side in cases]
        if stage == 1:
            small_sum = small_columns(*lax.optimization_barrier((early, tokens, *sent))[:2])
        elif stage > 1 and steps_left:
            small_sum = sum_step(small_sum, steps_left.pop(0), after=sent)
        if stage > 0:
            *here, small_sum = lax.optimization_barrier((*here, small_sum, *sent))[: len(here) + 1]
        value = pick(
            place_of,
            [0] * count + [0 if slot is None else 1 + cases.index(slot) for slot in wanted],
            here,
        )
        order = [blocks[stage] for blocks in first_order + second_order]
        part = block_product(table, value, weight, order)
        if stage == 1:
            part, after = lax.optimization_barrier((part, early))
            early_all = [early] + with_other_replicas(after)[1:]
        if stage == count - 1:
            part, *early_all = lax.optimization_barrier((part, *early_all))
        parts.append(part)
        slot = stage + 1
        if slot == count:
            break
        sent = []
        for side in (0, 1):
            needed = [first_slots[z].get((slot, side)) for z in everyone]
            stages = sorted({at for at in needed if at is not None})
            own = pick(
                place_of,
                [0 if at is None else stages.index(at) for at in needed] + [0] * count,
                [parts[at] for at in stages],
            )
            arrived = arrivals[-1][side]
            if side == 1:
                arrived, _ = lax.optimization_barrier((arrived, sent[0]))
            arrived = arrived.astype(F32)
            sent.append((arrived + jnp.where(is_first, own, 0.0)).astype(BF16))
        arrivals.append(
            (
                line(
                    sent[0],
                    [z for z in everyone if z < slot and z + 1 < count],
                    [z for z in everyone if slot + 1 < count and z >= slot and z + 1 < count],
                    1,
                ),
                line(
                    sent[1],
                    [z for z in everyone if z >= count - slot and z > 0],
                    [z for z in everyone if slot + 1 < count and z < count - slot and z > 0],
                    -1,
                ),
            )
        )
    from_left, from_right = arrivals[-1]

    while steps_left:
        small_sum = sum_step(small_sum, steps_left.pop(0))
    inv_first = lax.rsqrt(
        small_sum[rows:].reshape(-1)[:rows][:, None] / features + EPSILON
    )
    small_early = (coefficients * small_sum[:rows]).astype(BF16)
    small_early_all = with_other_replicas(
        (small_early.astype(F32) * jnp.where(is_first, inv_first, 1.0)).astype(BF16)
    )
    low_product = jnp.where(
        is_first,
        jnp.dot(small_early, up, preferred_element_type=F32),
        lax.dot_general(small_early, down, CONTRACT_LAST, preferred_element_type=F32),
    )

    pulled_here = (gain_row * (sum(parts) + low_product)).astype(BF16)
    swap = [(0, 1), (1, 0)]
    pulled = lax.ppermute(pulled_here, "section", swap)
    pulled_others = with_other_replicas(pulled_here, (1,))[1:]
    from_left, from_right, _ = lax.optimization_barrier((from_left, from_right, pulled_here))

    projected = parts[-1] + from_left.astype(F32) + from_right.astype(F32) + low_product
    hidden = (token_float + inv_first * projected).astype(BF16)
    swapped = [
        lax.ppermute(jnp.where(is_first, hidden, other), "section", swap) for other in early_all[1:]
    ]
    hidden_on_second = swapped[0] if swapped else lax.ppermute(hidden, "section", swap)
    cotangent_all = [cotangent] + swapped
    hidden_float = hidden.astype(F32)
    pulled_float = pulled.astype(F32)
    row_sums = jnp.stack(
        [jnp.sum(hidden_float * hidden_float, axis=1), jnp.sum(hidden_float * pulled_float, axis=1)]
    )
    if count <= 4:
        row_sums = row_sums + sum(
            lax.ppermute(row_sums, "tensor", [(z, (z + step) % count) for z in everyone])
            for step in range(1, count)
        )
    else:
        for step in doubling_steps():
            row_sums = sum_step(row_sums, step, F32)
    row_sums, *pulled_others = lax.optimization_barrier((row_sums, *pulled_others))
    inv_second = lax.rsqrt(row_sums[0] / features + EPSILON)
    inv_on_second = lax.ppermute(inv_second, "section", swap)[:, None]
    inv_second = inv_second[:, None]
    toward_hidden = row_sums[1][:, None] * inv_second * inv_second * inv_second / features
    hidden_grad = cotangent.astype(F32) + inv_second * pulled_float - toward_hidden * hidden_float
    late = jnp.where(
        is_first,
        hidden_grad.astype(BF16),
        (hidden_on_second.astype(F32) * gain_row).astype(BF16),
    )
    rank_late = jnp.where(is_first, times_up_transposed(late), times_down(late))
    hidden_others = with_other_replicas(
        lax.optimization_barrier((hidden, rank_late))[0], (0,)
    )[1:]
    for at, step in enumerate(doubling_steps()):
        rank_late = sum_step(rank_late, step)
        if at == 0:
            rank_late, *small_early_all = lax.optimization_barrier((rank_late, *small_early_all))

    inv_second = jnp.where(is_first, inv_second, inv_on_second)
    row_scale = jnp.where(is_first, inv_first, inv_second)
    small_late = (coefficients * rank_late * row_scale).astype(BF16)
    beside = jnp.concatenate(
        [
            small_late,
            jnp.broadcast_to(inv_second, (rows, 64)).astype(BF16),
            jnp.broadcast_to(toward_hidden, (rows, 64)).astype(BF16),
        ],
        axis=1,
    )
    small_late_all = with_other_replicas(beside)
    swapped = [
        lax.ppermute(
            lax.optimization_barrier((jnp.where(is_first, *pair), beside))[0], "section", swap
        )
        for pair in zip(hidden_others, pulled_others)
    ]
    hidden_all = [hidden] + [jnp.where(is_first, *pair) for pair in zip(hidden_others, swapped)]
    pulled_all = [pulled] + swapped
    small_early_own = (small_early.astype(F32) * row_scale).astype(BF16)
    sums = gradient_call(
        own_gradient_kernel,
        table, [], [early, late], [small_early_own, small_late], width, ranks, rows,
    )
    for at in range(1, replicas):
        sums = gradient_call(
            other_gradient_kernel,
            table,
            sums,
            [gain_row, early_all[at], cotangent_all[at], pulled_all[at], hidden_all[at]],
            [small_early_all[at], small_late_all[at]],
            width,
            ranks,
            rows,
        )
    grad_down, grad_up = sums
    return (grad_down[None], grad_up[None])


def solution(mesh):
    return jax.shard_map(
        on_device,
        mesh=mesh,
        in_specs=(
            P(("groups", "replica"), "tensor"),
            P(("groups", "replica"), "tensor"),
            P("section", "tensor"),
            P("section", "tensor", None),
            P("section", "tensor", None),
            P("section", None, "tensor"),
            P(),
            P(("groups", "replica")),
        ),
        out_specs=(P("section", "tensor", "groups"), P("section", "groups", "tensor")),
        check_vma=False,
    )
```

```python
import functools

import jax
import jax.numpy as jnp
from jax import lax
from jax.experimental import pallas as pl
from jax.experimental.pallas import tpu as pltpu
from jax.sharding import PartitionSpec as P

TENANT_COUNT = 4
EPSILON = 1e-05
CONTRACT_LAST = (((1,), (1,)), ((), ()))
CONTRACT_FIRST = (((0,), (0,)), ((), ()))
BF16 = jnp.bfloat16
F32 = jnp.float32
AHEAD = 2


def is_one_of(number, members):
    return functools.reduce(jnp.logical_or, [number == member for member in members])


def look_up(number, values):
    found = values[0]
    for value in sorted(set(values) - {values[0]}):
        found = jnp.where(
            is_one_of(number, [at for at, other in enumerate(values) if other == value]), value, found
        )
    return found


def block_kernel(table, value_ref, weight_ref, out_ref, wide, tall, arrived, *, blocks, tile, tiles):
    section = table[0]
    block = look_up(table[1], blocks)
    step = pl.program_id(0)
    width = tile * tiles

    def copy_of(index, is_wide):
        whole = pl.ds(pl.multiple_of(block * width, width), width)
        part = pl.ds(pl.multiple_of(block * width + index * tile, tile), tile)
        if is_wide:
            return pltpu.make_async_copy(weight_ref.at[:, part], wide.at[index], arrived.at[index])
        rows = pl.ds(pl.multiple_of(index * tile, tile), tile)
        return pltpu.make_async_copy(weight_ref.at[rows, whole], tall.at[index], arrived.at[index])

    for number, is_wide in ((0, True), (1, False)):

        @pl.when(section == number)
        def _():
            @pl.when(step == 0)
            def _():
                for index in range(min(AHEAD, tiles)):
                    copy_of(index, is_wide).start()

            @pl.when(step + AHEAD < tiles)
            def _():
                copy_of(step + AHEAD, is_wide).start()

            copy_of(step, is_wide).wait()
            if is_wide:
                out_ref[...] = jnp.dot(value_ref[...], wide[step], preferred_element_type=F32)
            else:
                out_ref[...] = lax.dot_general(
                    value_ref[...], tall[step], CONTRACT_LAST, preferred_element_type=F32
                )


def block_product(table, value, weight, blocks):
    rows, width = value.shape
    tile = min(512, width)
    tiles = width // tile
    return pl.pallas_call(
        functools.partial(block_kernel, blocks=blocks, tile=tile, tiles=tiles),
        grid_spec=pltpu.PrefetchScalarGridSpec(
            num_scalar_prefetch=1,
            grid=(tiles,),
            in_specs=[
                pl.BlockSpec((rows, width), lambda step, table: (0, 0)),
                pl.BlockSpec(memory_space=pl.ANY),
            ],
            out_specs=pl.BlockSpec((rows, tile), lambda step, table: (0, step)),
            scratch_shapes=[
                pltpu.VMEM((tiles, width, tile), BF16),
                pltpu.VMEM((tiles, tile, width), BF16),
                pltpu.SemaphoreType.DMA((tiles,)),
            ],
        ),
        out_shape=jax.ShapeDtypeStruct((rows, width), F32),
        compiler_params=pltpu.CompilerParams(vmem_limit_bytes=24 * 1024 * 1024),
        cost_estimate=pl.CostEstimate(
            flops=8 * rows * width * width, bytes_accessed=2 * width * width, transcendentals=0
        ),
    )(table, value, weight)


def transposed_times(left, right):
    return lax.dot_general(left, right, CONTRACT_FIRST, preferred_element_type=F32)


def own_gradient_kernel(table, early, late, small_early, small_late, down_ref, up_ref):
    @pl.when(table[0] == 0)
    def _():
        down_ref[...] = transposed_times(early[...], small_late[...])
        up_ref[...] = transposed_times(small_early[...], late[...])

    @pl.when(table[0] == 1)
    def _():
        down_ref[...] = transposed_times(late[...], small_early[...])
        up_ref[...] = transposed_times(small_late[...], early[...])


def other_gradient_kernel(
    table, gain_ref, down_sum, up_sum, early, cotangent, pulled, hidden, small_early, small_late,
    down_ref, up_ref,
):
    ranks = down_ref.shape[1]
    late = small_late[:, :ranks]
    inverse = small_late[:, ranks : ranks + 1].astype(F32)
    toward = small_late[:, ranks + 64 : ranks + 65].astype(F32)

    @pl.when(table[0] == 0)
    def _():
        grad = (
            cotangent[...].astype(F32)
            + inverse * pulled[...].astype(F32)
            - toward * hidden[...].astype(F32)
        ).astype(BF16)
        down_ref[...] = down_sum[...] + transposed_times(early[...], late)
        up_ref[...] = up_sum[...] + transposed_times(small_early[...], grad)

    @pl.when(table[0] == 1)
    def _():
        scaled = (hidden[...].astype(F32) * gain_ref[...]).astype(BF16)
        weighed = (small_early[...].astype(F32) * inverse).astype(BF16)
        down_ref[...] = down_sum[...] + transposed_times(scaled, weighed)
        up_ref[...] = up_sum[...] + transposed_times(late, early[...])


def gradient_call(kernel, table, sums, by_column, whole, width, ranks, rows):
    tile = min(512, width)
    down_spec = pl.BlockSpec((tile, ranks), lambda step, table: (step, 0))
    up_spec = pl.BlockSpec((ranks, tile), lambda step, table: (0, step))
    leading = [array for array in by_column if array.shape[0] == 1]
    columns = [array for array in by_column if array.shape[0] != 1]
    return pl.pallas_call(
        kernel,
        grid_spec=pltpu.PrefetchScalarGridSpec(
            num_scalar_prefetch=1,
            grid=(width // tile,),
            in_specs=[pl.BlockSpec((1, tile), lambda step, table: (0, step)) for _ in leading]
            + [down_spec, up_spec][: len(sums)]
            + [pl.BlockSpec((rows, tile), lambda step, table: (0, step)) for _ in columns]
            + [pl.BlockSpec(array.shape, lambda step, table: (0, 0)) for array in whole],
            out_specs=[down_spec, up_spec],
        ),
        out_shape=[
            jax.ShapeDtypeStruct((width, ranks), F32),
            jax.ShapeDtypeStruct((ranks, width), F32),
        ],
        compiler_params=pltpu.CompilerParams(vmem_limit_bytes=20 * 1024 * 1024),
        cost_estimate=pl.CostEstimate(
            flops=4 * rows * width * ranks,
            bytes_accessed=8 * width * ranks * (1 + len(sums) // 2) + 2 * rows * width * len(columns),
            transcendentals=0,
        ),
    )(table, *leading, *sums, *columns, *whole)


def orders(count):
    first, first_slots, second, second_slots = [], [], [], []
    for z in range(count):
        sends = [(slot, 0, count - slot + z) for slot in range(z + 1, count)]
        sends += [(slot, 1, slot - count + z) for slot in range(count - z, count)]
        sends.sort()
        first.append([block for _, _, block in sends] + [z])
        first_slots.append({(slot, side): at for at, (slot, side, _) in enumerate(sends)})
        arrivals = [(slot, 0, z - 1 - slot) for slot in range(z)]
        arrivals += [(slot, 1, z + 1 + slot) for slot in range(count - 1 - z)]
        arrivals.sort()
        second.append([z] + [block for _, _, block in arrivals])
        second_slots.append([None] + [(slot, side) for slot, side, _ in arrivals])
    return first, first_slots, second, second_slots


def pick(number, choice, cases):
    chosen = cases[0]
    for at in range(1, len(cases)):
        members = [device for device, wanted in enumerate(choice) if wanted == at]
        chosen = jnp.where(is_one_of(number, members), cases[at], chosen)
    return chosen


def doubling_steps():
    count = lax.axis_size("tensor")
    return [
        [(place, place ^ (1 << bit)) for place in range(count)]
        for bit in range(count.bit_length() - 1)
    ]


def sum_step(value, pairs, wire=BF16, after=()):
    other = lax.ppermute(value.astype(wire), "tensor", pairs)
    if after:
        other = lax.optimization_barrier((other, *after))[0]
    return value + other.astype(F32)


def with_other_replicas(value, sections=(0, 1)):
    count = lax.axis_size("replica")
    return [value] + [
        lax.ppermute(
            value,
            ("section", "replica"),
            [(s * count + r, s * count + (r + step) % count) for s in sections for r in range(count)],
        )
        for step in range(1, count)
    ]


def on_device(
    tokens,
    cotangent,
    gain,
    frozen_base_weight,
    adapter_down_factors,
    adapter_up_factors,
    tenant_adapter_scale,
    row_tenant_owner,
):
    section = lax.axis_index("section")
    place = lax.axis_index("tensor")
    count = lax.axis_size("tensor")
    is_first = section == 0
    weight = frozen_base_weight[0]
    gain_row = gain[0][None, :]
    down = adapter_down_factors[0]
    up = adapter_up_factors[0]
    rows, width = tokens.shape
    features = width * count
    replicas = lax.axis_size("replica")
    ranks = down.shape[1]

    tenant_of_column = jnp.arange(ranks, dtype=jnp.int32) // (ranks // TENANT_COUNT)
    coefficients = jnp.where(
        row_tenant_owner[:, None] == tenant_of_column[None, :],
        jnp.repeat(tenant_adapter_scale, ranks // TENANT_COUNT)[None, :],
        0.0,
    )

    first_order, first_slots, second_order, second_slots = orders(count)
    place_of = section * count + place
    table = jnp.stack([section, place_of]).astype(jnp.int32)

    def times_down(value):
        return jnp.dot(value, down, preferred_element_type=F32)

    def times_up_transposed(value):
        return lax.dot_general(value, up, CONTRACT_LAST, preferred_element_type=F32)

    def line(value, first_pairs, second_pairs, toward):
        pairs = [(2 * z, 2 * (z + toward)) for z in first_pairs] + [
            (2 * z + 1, 2 * (z + toward) + 1) for z in second_pairs
        ]
        return lax.ppermute(value, ("tensor", "section"), pairs)

    token_float = tokens.astype(F32)
    early = jnp.where(is_first, (token_float * gain_row).astype(BF16), cotangent)
    early = lax.optimization_barrier(early)

    def small_columns(value, plain):
        small = jnp.where(is_first, times_down(value), times_up_transposed(value))
        squares = jnp.sum(plain.astype(F32) ** 2, axis=1)
        squares = jnp.pad(squares, (0, -rows % ranks)).reshape(-1, ranks)
        return jnp.concatenate([small, jnp.pad(squares, ((0, -len(squares) % 16), (0, 0)))], axis=0)

    everyone = range(count)
    steps_left = doubling_steps()
    arrivals = [
        (
            line(early, [], [z for z in everyone if z + 1 < count], 1),
            line(early, [], [z for z in everyone if z > 0], -1),
        )
    ]
    parts = []
    for stage in range(count):
        wanted = [None if stage == 0 else second_slots[z][stage] for z in everyone]
        cases = sorted({slot for slot in wanted if slot is not None})
        here = [early] + [arrivals[slot][side] for slot, side in cases]
        if stage == 1:
            small_sum = small_columns(*lax.optimization_barrier((early, tokens, *sent))[:2])
        elif stage > 1 and steps_left:
            small_sum = sum_step(small_sum, steps_left.pop(0), after=sent)
        if stage > 0:
            *here, small_sum = lax.optimization_barrier((*here, small_sum, *sent))[: len(here) + 1]
        value = pick(
            place_of,
            [0] * count + [0 if slot is None else 1 + cases.index(slot) for slot in wanted],
            here,
        )
        order = [blocks[stage] for blocks in first_order + second_order]
        part = block_product(table, value, weight, order)
        if stage == 0:
            part, after = lax.optimization_barrier((part, early))
            early_all = [early] + with_other_replicas(after)[1:]
        if stage == min(2, count - 1):
            part, *early_all = lax.optimization_barrier((part, *early_all))
        parts.append(part)
        slot = stage + 1
        if slot == count:
            break
        sent = []
        for side in (0, 1):
            needed = [first_slots[z].get((slot, side)) for z in everyone]
            stages = sorted({at for at in needed if at is not None})
            own = pick(
                place_of,
                [0 if at is None else stages.index(at) for at in needed] + [0] * count,
                [parts[at] for at in stages],
            )
            arrived = arrivals[-1][side]
            if side == 1:
                arrived, _ = lax.optimization_barrier((arrived, sent[0]))
            arrived = arrived.astype(F32)
            sent.append((arrived + jnp.where(is_first, own, 0.0)).astype(BF16))
        arrivals.append(
            (
                line(
                    sent[0],
                    [z for z in everyone if z < slot and z + 1 < count],
                    [z for z in everyone if slot + 1 < count and z >= slot and z + 1 < count],
                    1,
                ),
                line(
                    sent[1],
                    [z for z in everyone if z >= count - slot and z > 0],
                    [z for z in everyone if slot + 1 < count and z < count - slot and z > 0],
                    -1,
                ),
            )
        )
    from_left, from_right = arrivals[-1]

    while steps_left:
        small_sum = sum_step(small_sum, steps_left.pop(0))
    inv_first = lax.rsqrt(
        small_sum[rows:].reshape(-1)[:rows][:, None] / features + EPSILON
    )
    small_early = (coefficients * small_sum[:rows]).astype(BF16)
    small_early_all = with_other_replicas(
        (small_early.astype(F32) * jnp.where(is_first, inv_first, 1.0)).astype(BF16)
    )
    low_product = jnp.where(
        is_first,
        jnp.dot(small_early, up, preferred_element_type=F32),
        lax.dot_general(small_early, down, CONTRACT_LAST, preferred_element_type=F32),
    )

    pulled_here = (gain_row * (sum(parts) + low_product)).astype(BF16)
    swap = [(0, 1), (1, 0)]
    pulled = lax.ppermute(pulled_here, "section", swap)
    pulled_others = with_other_replicas(pulled_here, (1,))[1:]
    from_left, from_right, _ = lax.optimization_barrier((from_left, from_right, pulled_here))

    projected = parts[-1] + from_left.astype(F32) + from_right.astype(F32) + low_product
    hidden = (token_float + inv_first * projected).astype(BF16)
    swapped = [
        lax.ppermute(jnp.where(is_first, hidden, other), "section", swap) for other in early_all[1:]
    ]
    hidden_on_second = swapped[0] if swapped else lax.ppermute(hidden, "section", swap)
    cotangent_all = [cotangent] + swapped
    hidden_float = hidden.astype(F32)
    pulled_float = pulled.astype(F32)
    row_sums = jnp.stack(
        [jnp.sum(hidden_float * hidden_float, axis=1), jnp.sum(hidden_float * pulled_float, axis=1)]
    )
    if count <= 4:
        row_sums = row_sums + sum(
            lax.ppermute(row_sums, "tensor", [(z, (z + step) % count) for z in everyone])
            for step in range(1, count)
        )
    else:
        for step in doubling_steps():
            row_sums = sum_step(row_sums, step, F32)
    row_sums, *pulled_others = lax.optimization_barrier((row_sums, *pulled_others))
    inv_second = lax.rsqrt(row_sums[0] / features + EPSILON)
    inv_on_second = lax.ppermute(inv_second, "section", swap)[:, None]
    inv_second = inv_second[:, None]
    toward_hidden = row_sums[1][:, None] * inv_second * inv_second * inv_second / features
    hidden_grad = cotangent.astype(F32) + inv_second * pulled_float - toward_hidden * hidden_float
    late = jnp.where(
        is_first,
        hidden_grad.astype(BF16),
        (hidden_on_second.astype(F32) * gain_row).astype(BF16),
    )
    rank_late = jnp.where(is_first, times_up_transposed(late), times_down(late))
    hidden_others = with_other_replicas(
        lax.optimization_barrier((hidden, rank_late))[0], (0,)
    )[1:]
    for at, step in enumerate(doubling_steps()):
        rank_late = sum_step(rank_late, step)
        if at == 0:
            rank_late, *small_early_all = lax.optimization_barrier((rank_late, *small_early_all))

    inv_second = jnp.where(is_first, inv_second, inv_on_second)
    row_scale = jnp.where(is_first, inv_first, inv_second)
    small_late = (coefficients * rank_late * row_scale).astype(BF16)
    beside = jnp.concatenate(
        [
            small_late,
            jnp.broadcast_to(inv_second, (rows, 64)).astype(BF16),
            jnp.broadcast_to(toward_hidden, (rows, 64)).astype(BF16),
        ],
        axis=1,
    )
    small_late_all = with_other_replicas(beside)
    swapped = [
        lax.ppermute(
            lax.optimization_barrier((jnp.where(is_first, *pair), beside))[0], "section", swap
        )
        for pair in zip(hidden_others, pulled_others)
    ]
    hidden_all = [hidden] + [jnp.where(is_first, *pair) for pair in zip(hidden_others, swapped)]
    pulled_all = [pulled] + swapped
    small_early_own = (small_early.astype(F32) * row_scale).astype(BF16)
    sums = gradient_call(
        own_gradient_kernel,
        table, [], [early, late], [small_early_own, small_late], width, ranks, rows,
    )
    for at in range(1, replicas):
        sums = gradient_call(
            other_gradient_kernel,
            table,
            sums,
            [gain_row, early_all[at], cotangent_all[at], pulled_all[at], hidden_all[at]],
            [small_early_all[at], small_late_all[at]],
            width,
            ranks,
            rows,
        )
    grad_down, grad_up = sums
    return (grad_down[None], grad_up[None])


def solution(mesh):
    return jax.shard_map(
        on_device,
        mesh=mesh,
        in_specs=(
            P(("groups", "replica"), "tensor"),
            P(("groups", "replica"), "tensor"),
            P("section", "tensor"),
            P("section", "tensor", None),
            P("section", "tensor", None),
            P("section", None, "tensor"),
            P(),
            P(("groups", "replica")),
        ),
        out_specs=(P("section", "tensor", "groups"), P("section", "groups", "tensor")),
        check_vma=False,
    )
```

```python
import functools

import jax
import jax.numpy as jnp
from jax import lax
from jax.experimental import pallas as pl
from jax.experimental.pallas import tpu as pltpu
from jax.sharding import PartitionSpec as P

TENANT_COUNT = 4
EPSILON = 1e-05
CONTRACT_LAST = (((1,), (1,)), ((), ()))
CONTRACT_FIRST = (((0,), (0,)), ((), ()))
BF16 = jnp.bfloat16
F32 = jnp.float32
AHEAD = 2


def is_one_of(number, members):
    return functools.reduce(jnp.logical_or, [number == member for member in members])


def look_up(number, values):
    found = values[0]
    for value in sorted(set(values) - {values[0]}):
        found = jnp.where(
            is_one_of(number, [at for at, other in enumerate(values) if other == value]), value, found
        )
    return found


def block_kernel(table, value_ref, weight_ref, out_ref, wide, tall, arrived, *, blocks, tile, tiles):
    section = table[0]
    block = look_up(table[1], blocks)
    step = pl.program_id(0)
    width = tile * tiles

    def copy_of(index, is_wide):
        whole = pl.ds(pl.multiple_of(block * width, width), width)
        part = pl.ds(pl.multiple_of(block * width + index * tile, tile), tile)
        if is_wide:
            return pltpu.make_async_copy(weight_ref.at[:, part], wide.at[index], arrived.at[index])
        rows = pl.ds(pl.multiple_of(index * tile, tile), tile)
        return pltpu.make_async_copy(weight_ref.at[rows, whole], tall.at[index], arrived.at[index])

    for number, is_wide in ((0, True), (1, False)):

        @pl.when(section == number)
        def _():
            @pl.when(step == 0)
            def _():
                for index in range(min(AHEAD, tiles)):
                    copy_of(index, is_wide).start()

            @pl.when(step + AHEAD < tiles)
            def _():
                copy_of(step + AHEAD, is_wide).start()

            copy_of(step, is_wide).wait()
            if is_wide:
                out_ref[...] = jnp.dot(value_ref[...], wide[step], preferred_element_type=F32)
            else:
                out_ref[...] = lax.dot_general(
                    value_ref[...], tall[step], CONTRACT_LAST, preferred_element_type=F32
                )


def block_product(table, value, weight, blocks):
    rows, width = value.shape
    tile = min(512, width)
    tiles = width // tile
    return pl.pallas_call(
        functools.partial(block_kernel, blocks=blocks, tile=tile, tiles=tiles),
        grid_spec=pltpu.PrefetchScalarGridSpec(
            num_scalar_prefetch=1,
            grid=(tiles,),
            in_specs=[
                pl.BlockSpec((rows, width), lambda step, table: (0, 0)),
                pl.BlockSpec(memory_space=pl.ANY),
            ],
            out_specs=pl.BlockSpec((rows, tile), lambda step, table: (0, step)),
            scratch_shapes=[
                pltpu.VMEM((tiles, width, tile), BF16),
                pltpu.VMEM((tiles, tile, width), BF16),
                pltpu.SemaphoreType.DMA((tiles,)),
            ],
        ),
        out_shape=jax.ShapeDtypeStruct((rows, width), F32),
        compiler_params=pltpu.CompilerParams(vmem_limit_bytes=24 * 1024 * 1024),
        cost_estimate=pl.CostEstimate(
            flops=8 * rows * width * width, bytes_accessed=2 * width * width, transcendentals=0
        ),
    )(table, value, weight)


def transposed_times(left, right):
    return lax.dot_general(left, right, CONTRACT_FIRST, preferred_element_type=F32)


def own_gradient_kernel(table, early, late, small_early, small_late, down_ref, up_ref):
    @pl.when(table[0] == 0)
    def _():
        down_ref[...] = transposed_times(early[...], small_late[...])
        up_ref[...] = transposed_times(small_early[...], late[...])

    @pl.when(table[0] == 1)
    def _():
        down_ref[...] = transposed_times(late[...], small_early[...])
        up_ref[...] = transposed_times(small_late[...], early[...])


def other_gradient_kernel(
    table, gain_ref, down_sum, up_sum, early, cotangent, pulled, hidden, small_early, small_late,
    down_ref, up_ref,
):
    ranks = down_ref.shape[1]
    late = small_late[:, :ranks]
    inverse = small_late[:, ranks : ranks + 1].astype(F32)
    toward = small_late[:, ranks + 64 : ranks + 65].astype(F32)

    @pl.when(table[0] == 0)
    def _():
        grad = (
            cotangent[...].astype(F32)
            + inverse * pulled[...].astype(F32)
            - toward * hidden[...].astype(F32)
        ).astype(BF16)
        down_ref[...] = down_sum[...] + transposed_times(early[...], late)
        up_ref[...] = up_sum[...] + transposed_times(small_early[...], grad)

    @pl.when(table[0] == 1)
    def _():
        scaled = (hidden[...].astype(F32) * gain_ref[...]).astype(BF16)
        weighed = (small_early[...].astype(F32) * inverse).astype(BF16)
        down_ref[...] = down_sum[...] + transposed_times(scaled, weighed)
        up_ref[...] = up_sum[...] + transposed_times(late, early[...])


def gradient_call(kernel, table, sums, by_column, whole, width, ranks, rows):
    tile = min(512, width)
    down_spec = pl.BlockSpec((tile, ranks), lambda step, table: (step, 0))
    up_spec = pl.BlockSpec((ranks, tile), lambda step, table: (0, step))
    leading = [array for array in by_column if array.shape[0] == 1]
    columns = [array for array in by_column if array.shape[0] != 1]
    return pl.pallas_call(
        kernel,
        grid_spec=pltpu.PrefetchScalarGridSpec(
            num_scalar_prefetch=1,
            grid=(width // tile,),
            in_specs=[pl.BlockSpec((1, tile), lambda step, table: (0, step)) for _ in leading]
            + [down_spec, up_spec][: len(sums)]
            + [pl.BlockSpec((rows, tile), lambda step, table: (0, step)) for _ in columns]
            + [pl.BlockSpec(array.shape, lambda step, table: (0, 0)) for array in whole],
            out_specs=[down_spec, up_spec],
        ),
        out_shape=[
            jax.ShapeDtypeStruct((width, ranks), F32),
            jax.ShapeDtypeStruct((ranks, width), F32),
        ],
        compiler_params=pltpu.CompilerParams(vmem_limit_bytes=20 * 1024 * 1024),
        cost_estimate=pl.CostEstimate(
            flops=4 * rows * width * ranks,
            bytes_accessed=8 * width * ranks * (1 + len(sums) // 2) + 2 * rows * width * len(columns),
            transcendentals=0,
        ),
    )(table, *leading, *sums, *columns, *whole)


def orders(count):
    first, first_slots, second, second_slots = [], [], [], []
    for z in range(count):
        sends = [(slot, 0, count - slot + z) for slot in range(z + 1, count)]
        sends += [(slot, 1, slot - count + z) for slot in range(count - z, count)]
        sends.sort()
        first.append([block for _, _, block in sends] + [z])
        first_slots.append({(slot, side): at for at, (slot, side, _) in enumerate(sends)})
        arrivals = [(slot, 0, z - 1 - slot) for slot in range(z)]
        arrivals += [(slot, 1, z + 1 + slot) for slot in range(count - 1 - z)]
        arrivals.sort()
        second.append([z] + [block for _, _, block in arrivals])
        second_slots.append([None] + [(slot, side) for slot, side, _ in arrivals])
    return first, first_slots, second, second_slots


def pick(number, choice, cases):
    chosen = cases[0]
    for at in range(1, len(cases)):
        members = [device for device, wanted in enumerate(choice) if wanted == at]
        chosen = jnp.where(is_one_of(number, members), cases[at], chosen)
    return chosen


def doubling_steps():
    count = lax.axis_size("tensor")
    return [
        [(place, place ^ (1 << bit)) for place in range(count)]
        for bit in range(count.bit_length() - 1)
    ]


def sum_step(value, pairs, wire=BF16, after=()):
    other = lax.ppermute(value.astype(wire), "tensor", pairs)
    if after:
        other = lax.optimization_barrier((other, *after))[0]
    return value + other.astype(F32)


def with_other_replicas(value, sections=(0, 1)):
    count = lax.axis_size("replica")
    return [value] + [
        lax.ppermute(
            value,
            ("section", "replica"),
            [(s * count + r, s * count + (r + step) % count) for s in sections for r in range(count)],
        )
        for step in range(1, count)
    ]


def on_device(
    tokens,
    cotangent,
    gain,
    frozen_base_weight,
    adapter_down_factors,
    adapter_up_factors,
    tenant_adapter_scale,
    row_tenant_owner,
):
    section = lax.axis_index("section")
    place = lax.axis_index("tensor")
    count = lax.axis_size("tensor")
    is_first = section == 0
    weight = frozen_base_weight[0]
    gain_row = gain[0][None, :]
    down = adapter_down_factors[0]
    up = adapter_up_factors[0]
    rows, width = tokens.shape
    features = width * count
    replicas = lax.axis_size("replica")
    ranks = down.shape[1]

    tenant_of_column = jnp.arange(ranks, dtype=jnp.int32) // (ranks // TENANT_COUNT)
    coefficients = jnp.where(
        row_tenant_owner[:, None] == tenant_of_column[None, :],
        jnp.repeat(tenant_adapter_scale, ranks // TENANT_COUNT)[None, :],
        0.0,
    )

    first_order, first_slots, second_order, second_slots = orders(count)
    place_of = section * count + place
    table = jnp.stack([section, place_of]).astype(jnp.int32)

    def times_down(value):
        return jnp.dot(value, down, preferred_element_type=F32)

    def times_up_transposed(value):
        return lax.dot_general(value, up, CONTRACT_LAST, preferred_element_type=F32)

    def line(value, first_pairs, second_pairs, toward):
        pairs = [(2 * z, 2 * (z + toward)) for z in first_pairs] + [
            (2 * z + 1, 2 * (z + toward) + 1) for z in second_pairs
        ]
        return lax.ppermute(value, ("tensor", "section"), pairs)

    token_float = tokens.astype(F32)
    early = jnp.where(is_first, (token_float * gain_row).astype(BF16), cotangent)
    early = lax.optimization_barrier(early)

    def small_columns(value, plain):
        small = jnp.where(is_first, times_down(value), times_up_transposed(value))
        squares = jnp.sum(plain.astype(F32) ** 2, axis=1)
        squares = jnp.pad(squares, (0, -rows % ranks)).reshape(-1, ranks)
        return jnp.concatenate([small, jnp.pad(squares, ((0, -len(squares) % 16), (0, 0)))], axis=0)

    everyone = range(count)
    steps_left = doubling_steps()
    arrivals = [
        (
            line(early, [], [z for z in everyone if z + 1 < count], 1),
            line(early, [], [z for z in everyone if z > 0], -1),
        )
    ]
    parts = []
    for stage in range(count):
        wanted = [None if stage == 0 else second_slots[z][stage] for z in everyone]
        cases = sorted({slot for slot in wanted if slot is not None})
        here = [early] + [arrivals[slot][side] for slot, side in cases]
        if stage == 1:
            small_sum = small_columns(*lax.optimization_barrier((early, tokens, *sent))[:2])
        elif stage > 1 and steps_left:
            small_sum = sum_step(small_sum, steps_left.pop(0), after=sent)
        if stage > 0:
            *here, small_sum = lax.optimization_barrier((*here, small_sum, *sent))[: len(here) + 1]
        value = pick(
            place_of,
            [0] * count + [0 if slot is None else 1 + cases.index(slot) for slot in wanted],
            here,
        )
        order = [blocks[stage] for blocks in first_order + second_order]
        part = block_product(table, value, weight, order)
        if stage == 0:
            part, after = lax.optimization_barrier((part, early))
            early_all = [early] + with_other_replicas(after)[1:]
        if stage == min(2, count - 1):
            part, *early_all = lax.optimization_barrier((part, *early_all))
        parts.append(part)
        slot = stage + 1
        if slot == count:
            break
        sent = []
        for side in (0, 1):
            needed = [first_slots[z].get((slot, side)) for z in everyone]
            stages = sorted({at for at in needed if at is not None})
            own = pick(
                place_of,
                [0 if at is None else stages.index(at) for at in needed] + [0] * count,
                [parts[at] for at in stages],
            )
            arrived = arrivals[-1][side]
            if side == 1:
                arrived, _ = lax.optimization_barrier((arrived, sent[0]))
            arrived = arrived.astype(F32)
            sent.append((arrived + jnp.where(is_first, own, 0.0)).astype(BF16))
        arrivals.append(
            (
                line(
                    sent[0],
                    [z for z in everyone if z < slot and z + 1 < count],
                    [z for z in everyone if slot + 1 < count and z >= slot and z + 1 < count],
                    1,
                ),
                line(
                    sent[1],
                    [z for z in everyone if z >= count - slot and z > 0],
                    [z for z in everyone if slot + 1 < count and z < count - slot and z > 0],
                    -1,
                ),
            )
        )
    from_left, from_right = arrivals[-1]

    while steps_left:
        small_sum = sum_step(small_sum, steps_left.pop(0))
    inv_first = lax.rsqrt(
        small_sum[rows:].reshape(-1)[:rows][:, None] / features + EPSILON
    )
    small_early = (coefficients * small_sum[:rows]).astype(BF16)
    small_early_all = with_other_replicas(
        (small_early.astype(F32) * jnp.where(is_first, inv_first, 1.0)).astype(BF16)
    )
    low_product = jnp.where(
        is_first,
        jnp.dot(small_early, up, preferred_element_type=F32),
        lax.dot_general(small_early, down, CONTRACT_LAST, preferred_element_type=F32),
    )

    pulled_here = (gain_row * (sum(parts) + low_product)).astype(BF16)
    swap = [(0, 1), (1, 0)]
    pulled = lax.ppermute(pulled_here, "section", swap)
    from_left, from_right, _ = lax.optimization_barrier((from_left, from_right, pulled_here))

    projected = parts[-1] + from_left.astype(F32) + from_right.astype(F32) + low_product
    hidden = (token_float + inv_first * projected).astype(BF16)
    late_others = with_other_replicas(jnp.where(is_first, hidden, pulled_here))[1:]
    swapped = [
        lax.ppermute(jnp.where(is_first, hidden, other), "section", swap) for other in early_all[1:]
    ]
    hidden_on_second = swapped[0] if swapped else lax.ppermute(hidden, "section", swap)
    cotangent_all = [cotangent] + swapped
    hidden_float = hidden.astype(F32)
    pulled_float = pulled.astype(F32)
    row_sums = jnp.stack(
        [jnp.sum(hidden_float * hidden_float, axis=1), jnp.sum(hidden_float * pulled_float, axis=1)]
    )
    if count <= 4:
        row_sums = row_sums + sum(
            lax.ppermute(row_sums, "tensor", [(z, (z + step) % count) for z in everyone])
            for step in range(1, count)
        )
    else:
        for step in doubling_steps():
            row_sums = sum_step(row_sums, step, F32)
    row_sums, *small_early_all = lax.optimization_barrier((row_sums, *small_early_all))
    inv_second = lax.rsqrt(row_sums[0] / features + EPSILON)
    inv_on_second = lax.ppermute(inv_second, "section", swap)[:, None]
    inv_second = inv_second[:, None]
    toward_hidden = row_sums[1][:, None] * inv_second * inv_second * inv_second / features
    hidden_grad = cotangent.astype(F32) + inv_second * pulled_float - toward_hidden * hidden_float
    late = jnp.where(
        is_first,
        hidden_grad.astype(BF16),
        (hidden_on_second.astype(F32) * gain_row).astype(BF16),
    )
    rank_late = jnp.where(is_first, times_up_transposed(late), times_down(late))
    for step in doubling_steps():
        rank_late = sum_step(rank_late, step)

    inv_second = jnp.where(is_first, inv_second, inv_on_second)
    row_scale = jnp.where(is_first, inv_first, inv_second)
    small_late = (coefficients * rank_late * row_scale).astype(BF16)
    small_late_all = with_other_replicas(
        jnp.concatenate(
            [
                small_late,
                jnp.broadcast_to(inv_second, (rows, 64)).astype(BF16),
                jnp.broadcast_to(toward_hidden, (rows, 64)).astype(BF16),
            ],
            axis=1,
        )
    )
    small_early_own = (small_early.astype(F32) * row_scale).astype(BF16)
    sums = gradient_call(
        own_gradient_kernel,
        table, [], [early, late], [small_early_own, small_late], width, ranks, rows,
    )
    swapped = [
        lax.ppermute(lax.optimization_barrier((other, *sums))[0], "section", swap)
        for other in late_others
    ]
    hidden_all = [hidden] + [jnp.where(is_first, *pair) for pair in zip(late_others, swapped)]
    pulled_all = [pulled] + swapped
    for at in range(1, replicas):
        sums = gradient_call(
            other_gradient_kernel,
            table,
            sums,
            [gain_row, early_all[at], cotangent_all[at], pulled_all[at], hidden_all[at]],
            [small_early_all[at], small_late_all[at]],
            width,
            ranks,
            rows,
        )
    grad_down, grad_up = sums
    return (grad_down[None], grad_up[None])


def solution(mesh):
    return jax.shard_map(
        on_device,
        mesh=mesh,
        in_specs=(
            P(("groups", "replica"), "tensor"),
            P(("groups", "replica"), "tensor"),
            P("section", "tensor"),
            P("section", "tensor", None),
            P("section", "tensor", None),
            P("section", None, "tensor"),
            P(),
            P(("groups", "replica")),
        ),
        out_specs=(P("section", "tensor", "groups"), P("section", "groups", "tensor")),
        check_vma=False,
    )
```

```python
import functools

import jax
import jax.numpy as jnp
from jax import lax
from jax.experimental import pallas as pl
from jax.experimental.pallas import tpu as pltpu
from jax.sharding import PartitionSpec as P

TENANT_COUNT = 4
EPSILON = 1e-05
CONTRACT_LAST = (((1,), (1,)), ((), ()))
CONTRACT_FIRST = (((0,), (0,)), ((), ()))
BF16 = jnp.bfloat16
F32 = jnp.float32
AHEAD = 2


def is_one_of(number, members):
    return functools.reduce(jnp.logical_or, [number == member for member in members])


def look_up(number, values):
    found = values[0]
    for value in sorted(set(values) - {values[0]}):
        found = jnp.where(
            is_one_of(number, [at for at, other in enumerate(values) if other == value]), value, found
        )
    return found


def block_kernel(table, value_ref, weight_ref, out_ref, wide, tall, arrived, *, blocks, tile, tiles):
    section = table[0]
    block = look_up(table[1], blocks)
    step = pl.program_id(0)
    width = tile * tiles

    def copy_of(index, is_wide):
        whole = pl.ds(pl.multiple_of(block * width, width), width)
        part = pl.ds(pl.multiple_of(block * width + index * tile, tile), tile)
        if is_wide:
            return pltpu.make_async_copy(weight_ref.at[:, part], wide.at[index], arrived.at[index])
        rows = pl.ds(pl.multiple_of(index * tile, tile), tile)
        return pltpu.make_async_copy(weight_ref.at[rows, whole], tall.at[index], arrived.at[index])

    for number, is_wide in ((0, True), (1, False)):

        @pl.when(section == number)
        def _():
            @pl.when(step == 0)
            def _():
                for index in range(min(AHEAD, tiles)):
                    copy_of(index, is_wide).start()

            @pl.when(step + AHEAD < tiles)
            def _():
                copy_of(step + AHEAD, is_wide).start()

            copy_of(step, is_wide).wait()
            if is_wide:
                out_ref[...] = jnp.dot(value_ref[...], wide[step], preferred_element_type=F32)
            else:
                out_ref[...] = lax.dot_general(
                    value_ref[...], tall[step], CONTRACT_LAST, preferred_element_type=F32
                )


def block_product(table, value, weight, blocks):
    rows, width = value.shape
    tile = min(512, width)
    tiles = width // tile
    return pl.pallas_call(
        functools.partial(block_kernel, blocks=blocks, tile=tile, tiles=tiles),
        grid_spec=pltpu.PrefetchScalarGridSpec(
            num_scalar_prefetch=1,
            grid=(tiles,),
            in_specs=[
                pl.BlockSpec((rows, width), lambda step, table: (0, 0)),
                pl.BlockSpec(memory_space=pl.ANY),
            ],
            out_specs=pl.BlockSpec((rows, tile), lambda step, table: (0, step)),
            scratch_shapes=[
                pltpu.VMEM((tiles, width, tile), BF16),
                pltpu.VMEM((tiles, tile, width), BF16),
                pltpu.SemaphoreType.DMA((tiles,)),
            ],
        ),
        out_shape=jax.ShapeDtypeStruct((rows, width), F32),
        compiler_params=pltpu.CompilerParams(vmem_limit_bytes=24 * 1024 * 1024),
        cost_estimate=pl.CostEstimate(
            flops=8 * rows * width * width, bytes_accessed=2 * width * width, transcendentals=0
        ),
    )(table, value, weight)


def transposed_times(left, right):
    return lax.dot_general(left, right, CONTRACT_FIRST, preferred_element_type=F32)


def own_gradient_kernel(table, early, late, small_early, small_late, down_ref, up_ref):
    @pl.when(table[0] == 0)
    def _():
        down_ref[...] = transposed_times(early[...], small_late[...])
        up_ref[...] = transposed_times(small_early[...], late[...])

    @pl.when(table[0] == 1)
    def _():
        down_ref[...] = transposed_times(late[...], small_early[...])
        up_ref[...] = transposed_times(small_late[...], early[...])


def other_gradient_kernel(
    table, gain_ref, down_sum, up_sum, early, cotangent, pulled, hidden, small_early, small_late,
    down_ref, up_ref,
):
    ranks = down_ref.shape[1]
    late = small_late[:, :ranks]
    inverse = small_late[:, ranks : ranks + 1].astype(F32)
    toward = small_late[:, ranks + 64 : ranks + 65].astype(F32)

    @pl.when(table[0] == 0)
    def _():
        grad = (
            cotangent[...].astype(F32)
            + inverse * pulled[...].astype(F32)
            - toward * hidden[...].astype(F32)
        ).astype(BF16)
        down_ref[...] = down_sum[...] + transposed_times(early[...], late)
        up_ref[...] = up_sum[...] + transposed_times(small_early[...], grad)

    @pl.when(table[0] == 1)
    def _():
        scaled = (hidden[...].astype(F32) * gain_ref[...]).astype(BF16)
        weighed = (small_early[...].astype(F32) * inverse).astype(BF16)
        down_ref[...] = down_sum[...] + transposed_times(scaled, weighed)
        up_ref[...] = up_sum[...] + transposed_times(late, early[...])


def gradient_call(kernel, table, sums, by_column, whole, width, ranks, rows):
    tile = min(512, width)
    down_spec = pl.BlockSpec((tile, ranks), lambda step, table: (step, 0))
    up_spec = pl.BlockSpec((ranks, tile), lambda step, table: (0, step))
    leading = [array for array in by_column if array.shape[0] == 1]
    columns = [array for array in by_column if array.shape[0] != 1]
    return pl.pallas_call(
        kernel,
        grid_spec=pltpu.PrefetchScalarGridSpec(
            num_scalar_prefetch=1,
            grid=(width // tile,),
            in_specs=[pl.BlockSpec((1, tile), lambda step, table: (0, step)) for _ in leading]
            + [down_spec, up_spec][: len(sums)]
            + [pl.BlockSpec((rows, tile), lambda step, table: (0, step)) for _ in columns]
            + [pl.BlockSpec(array.shape, lambda step, table: (0, 0)) for array in whole],
            out_specs=[down_spec, up_spec],
        ),
        out_shape=[
            jax.ShapeDtypeStruct((width, ranks), F32),
            jax.ShapeDtypeStruct((ranks, width), F32),
        ],
        compiler_params=pltpu.CompilerParams(vmem_limit_bytes=20 * 1024 * 1024),
        cost_estimate=pl.CostEstimate(
            flops=4 * rows * width * ranks,
            bytes_accessed=8 * width * ranks * (1 + len(sums) // 2) + 2 * rows * width * len(columns),
            transcendentals=0,
        ),
    )(table, *leading, *sums, *columns, *whole)


def orders(count):
    first, first_slots, second, second_slots = [], [], [], []
    for z in range(count):
        sends = [(slot, 0, count - slot + z) for slot in range(z + 1, count)]
        sends += [(slot, 1, slot - count + z) for slot in range(count - z, count)]
        sends.sort()
        first.append([block for _, _, block in sends] + [z])
        first_slots.append({(slot, side): at for at, (slot, side, _) in enumerate(sends)})
        arrivals = [(slot, 0, z - 1 - slot) for slot in range(z)]
        arrivals += [(slot, 1, z + 1 + slot) for slot in range(count - 1 - z)]
        arrivals.sort()
        second.append([z] + [block for _, _, block in arrivals])
        second_slots.append([None] + [(slot, side) for slot, side, _ in arrivals])
    return first, first_slots, second, second_slots


def pick(number, choice, cases):
    chosen = cases[0]
    for at in range(1, len(cases)):
        members = [device for device, wanted in enumerate(choice) if wanted == at]
        chosen = jnp.where(is_one_of(number, members), cases[at], chosen)
    return chosen


def doubling_steps():
    count = lax.axis_size("tensor")
    return [
        [(place, place ^ (1 << bit)) for place in range(count)]
        for bit in range(count.bit_length() - 1)
    ]


def sum_step(value, pairs, wire=BF16, after=()):
    other = lax.ppermute(value.astype(wire), "tensor", pairs)
    if after:
        other = lax.optimization_barrier((other, *after))[0]
    return value + other.astype(F32)


def with_other_replicas(value, sections=(0, 1)):
    count = lax.axis_size("replica")
    return [value] + [
        lax.ppermute(
            value,
            ("section", "replica"),
            [(s * count + r, s * count + (r + step) % count) for s in sections for r in range(count)],
        )
        for step in range(1, count)
    ]


def on_device(
    tokens,
    cotangent,
    gain,
    frozen_base_weight,
    adapter_down_factors,
    adapter_up_factors,
    tenant_adapter_scale,
    row_tenant_owner,
):
    section = lax.axis_index("section")
    place = lax.axis_index("tensor")
    count = lax.axis_size("tensor")
    is_first = section == 0
    weight = frozen_base_weight[0]
    gain_row = gain[0][None, :]
    down = adapter_down_factors[0]
    up = adapter_up_factors[0]
    rows, width = tokens.shape
    features = width * count
    replicas = lax.axis_size("replica")
    ranks = down.shape[1]

    tenant_of_column = jnp.arange(ranks, dtype=jnp.int32) // (ranks // TENANT_COUNT)
    coefficients = jnp.where(
        row_tenant_owner[:, None] == tenant_of_column[None, :],
        jnp.repeat(tenant_adapter_scale, ranks // TENANT_COUNT)[None, :],
        0.0,
    )

    first_order, first_slots, second_order, second_slots = orders(count)
    place_of = section * count + place
    table = jnp.stack([section, place_of]).astype(jnp.int32)

    def times_down(value):
        return jnp.dot(value, down, preferred_element_type=F32)

    def times_up_transposed(value):
        return lax.dot_general(value, up, CONTRACT_LAST, preferred_element_type=F32)

    def line(value, first_pairs, second_pairs, toward):
        pairs = [(2 * z, 2 * (z + toward)) for z in first_pairs] + [
            (2 * z + 1, 2 * (z + toward) + 1) for z in second_pairs
        ]
        return lax.ppermute(value, ("tensor", "section"), pairs)

    token_float = tokens.astype(F32)
    early = jnp.where(is_first, (token_float * gain_row).astype(BF16), cotangent)
    early = lax.optimization_barrier(early)

    def small_columns(value, plain):
        small = jnp.where(is_first, times_down(value), times_up_transposed(value))
        squares = jnp.sum(plain.astype(F32) ** 2, axis=1)
        squares = jnp.pad(squares, (0, -rows % ranks)).reshape(-1, ranks)
        return jnp.concatenate([small, jnp.pad(squares, ((0, -len(squares) % 16), (0, 0)))], axis=0)

    everyone = range(count)
    steps_left = doubling_steps()
    arrivals = [
        (
            line(early, [], [z for z in everyone if z + 1 < count], 1),
            line(early, [], [z for z in everyone if z > 0], -1),
        )
    ]
    parts = []
    for stage in range(count):
        wanted = [None if stage == 0 else second_slots[z][stage] for z in everyone]
        cases = sorted({slot for slot in wanted if slot is not None})
        here = [early] + [arrivals[slot][side] for slot, side in cases]
        if stage == 1:
            small_sum = small_columns(*lax.optimization_barrier((early, tokens, *sent))[:2])
        elif stage > 1 and steps_left:
            small_sum = sum_step(small_sum, steps_left.pop(0), after=sent)
        if stage > 0:
            *here, small_sum = lax.optimization_barrier((*here, small_sum, *sent))[: len(here) + 1]
        value = pick(
            place_of,
            [0] * count + [0 if slot is None else 1 + cases.index(slot) for slot in wanted],
            here,
        )
        order = [blocks[stage] for blocks in first_order + second_order]
        part = block_product(table, value, weight, order)
        if stage == 1:
            part, after = lax.optimization_barrier((part, early))
            early_all = [early] + with_other_replicas(after)[1:]
        if stage == count - 1:
            part, *early_all = lax.optimization_barrier((part, *early_all))
        parts.append(part)
        slot = stage + 1
        if slot == count:
            break
        sent = []
        for side in (0, 1):
            needed = [first_slots[z].get((slot, side)) for z in everyone]
            stages = sorted({at for at in needed if at is not None})
            own = pick(
                place_of,
                [0 if at is None else stages.index(at) for at in needed] + [0] * count,
                [parts[at] for at in stages],
            )
            arrived = arrivals[-1][side]
            if side == 1:
                arrived, _ = lax.optimization_barrier((arrived, sent[0]))
            arrived = arrived.astype(F32)
            sent.append((arrived + jnp.where(is_first, own, 0.0)).astype(BF16))
        arrivals.append(
            (
                line(
                    sent[0],
                    [z for z in everyone if z < slot and z + 1 < count],
                    [z for z in everyone if slot + 1 < count and z >= slot and z + 1 < count],
                    1,
                ),
                line(
                    sent[1],
                    [z for z in everyone if z >= count - slot and z > 0],
                    [z for z in everyone if slot + 1 < count and z < count - slot and z > 0],
                    -1,
                ),
            )
        )
    from_left, from_right = arrivals[-1]

    while steps_left:
        small_sum = sum_step(small_sum, steps_left.pop(0))
    inv_first = lax.rsqrt(
        small_sum[rows:].reshape(-1)[:rows][:, None] / features + EPSILON
    )
    small_early = (coefficients * small_sum[:rows]).astype(BF16)
    small_early_all = with_other_replicas(
        (small_early.astype(F32) * jnp.where(is_first, inv_first, 1.0)).astype(BF16)
    )
    low_product = jnp.where(
        is_first,
        jnp.dot(small_early, up, preferred_element_type=F32),
        lax.dot_general(small_early, down, CONTRACT_LAST, preferred_element_type=F32),
    )

    pulled_here = (gain_row * (sum(parts) + low_product)).astype(BF16)
    swap = [(0, 1), (1, 0)]
    pulled = lax.ppermute(pulled_here, "section", swap)
    from_left, from_right, *small_early_all, _ = lax.optimization_barrier(
        (from_left, from_right, *small_early_all, pulled_here)
    )

    projected = parts[-1] + from_left.astype(F32) + from_right.astype(F32) + low_product
    hidden = (token_float + inv_first * projected).astype(BF16)
    late_others = with_other_replicas(jnp.where(is_first, hidden, pulled_here))[1:]
    swapped = [
        lax.ppermute(jnp.where(is_first, hidden, other), "section", swap) for other in early_all[1:]
    ]
    hidden_on_second = swapped[0] if swapped else lax.ppermute(hidden, "section", swap)
    cotangent_all = [cotangent] + swapped
    hidden_float = hidden.astype(F32)
    pulled_float = pulled.astype(F32)
    row_sums = jnp.stack(
        [jnp.sum(hidden_float * hidden_float, axis=1), jnp.sum(hidden_float * pulled_float, axis=1)]
    )
    if count <= 4:
        row_sums = row_sums + sum(
            lax.ppermute(row_sums, "tensor", [(z, (z + step) % count) for z in everyone])
            for step in range(1, count)
        )
    else:
        for step in doubling_steps():
            row_sums = sum_step(row_sums, step, F32)
    inv_second = lax.rsqrt(row_sums[0] / features + EPSILON)
    inv_second = inv_second[:, None]
    toward_hidden = row_sums[1][:, None] * inv_second * inv_second * inv_second / features
    hidden_grad = cotangent.astype(F32) + inv_second * pulled_float - toward_hidden * hidden_float
    late = jnp.where(
        is_first,
        hidden_grad.astype(BF16),
        (hidden_on_second.astype(F32) * gain_row).astype(BF16),
    )
    rank_late = jnp.where(is_first, times_up_transposed(late), times_down(late))
    inv_on_second = lax.ppermute(
        lax.optimization_barrier((inv_second[:, 0], rank_late))[0], "section", swap
    )[:, None]
    for step in doubling_steps():
        rank_late = sum_step(rank_late, step)

    inv_second = jnp.where(is_first, inv_second, inv_on_second)
    row_scale = jnp.where(is_first, inv_first, inv_second)
    small_late = (coefficients * rank_late * row_scale).astype(BF16)
    small_late_all = with_other_replicas(
        jnp.concatenate(
            [
                small_late,
                jnp.broadcast_to(inv_second, (rows, 64)).astype(BF16),
                jnp.broadcast_to(toward_hidden, (rows, 64)).astype(BF16),
            ],
            axis=1,
        )
    )
    small_early_own = (small_early.astype(F32) * row_scale).astype(BF16)
    sums = gradient_call(
        own_gradient_kernel,
        table, [], [early, late], [small_early_own, small_late], width, ranks, rows,
    )
    swapped = [
        lax.ppermute(lax.optimization_barrier((other, rank_late))[0], "section", swap)
        for other in late_others
    ]
    hidden_all = [hidden] + [jnp.where(is_first, *pair) for pair in zip(late_others, swapped)]
    pulled_all = [pulled] + swapped
    for at in range(1, replicas):
        sums = gradient_call(
            other_gradient_kernel,
            table,
            sums,
            [gain_row, early_all[at], cotangent_all[at], pulled_all[at], hidden_all[at]],
            [small_early_all[at], small_late_all[at]],
            width,
            ranks,
            rows,
        )
    grad_down, grad_up = sums
    return (grad_down[None], grad_up[None])


def solution(mesh):
    return jax.shard_map(
        on_device,
        mesh=mesh,
        in_specs=(
            P(("groups", "replica"), "tensor"),
            P(("groups", "replica"), "tensor"),
            P("section", "tensor"),
            P("section", "tensor", None),
            P("section", "tensor", None),
            P("section", None, "tensor"),
            P(),
            P(("groups", "replica")),
        ),
        out_specs=(P("section", "tensor", "groups"), P("section", "groups", "tensor")),
        check_vma=False,
    )
```

```python
import functools

import jax
import jax.numpy as jnp
from jax import lax
from jax.experimental import pallas as pl
from jax.experimental.pallas import tpu as pltpu
from jax.sharding import PartitionSpec as P

TENANT_COUNT = 4
EPSILON = 1e-05
CONTRACT_LAST = (((1,), (1,)), ((), ()))
CONTRACT_FIRST = (((0,), (0,)), ((), ()))
BF16 = jnp.bfloat16
F32 = jnp.float32
AHEAD = 2


def is_one_of(number, members):
    return functools.reduce(jnp.logical_or, [number == member for member in members])


def look_up(number, values):
    found = values[0]
    for value in sorted(set(values) - {values[0]}):
        found = jnp.where(
            is_one_of(number, [at for at, other in enumerate(values) if other == value]), value, found
        )
    return found


def block_kernel(table, value_ref, weight_ref, out_ref, wide, tall, arrived, *, blocks, tile, tiles):
    section = table[0]
    block = look_up(table[1], blocks)
    step = pl.program_id(0)
    width = tile * tiles

    def copy_of(index, is_wide):
        whole = pl.ds(pl.multiple_of(block * width, width), width)
        part = pl.ds(pl.multiple_of(block * width + index * tile, tile), tile)
        if is_wide:
            return pltpu.make_async_copy(weight_ref.at[:, part], wide.at[index], arrived.at[index])
        rows = pl.ds(pl.multiple_of(index * tile, tile), tile)
        return pltpu.make_async_copy(weight_ref.at[rows, whole], tall.at[index], arrived.at[index])

    for number, is_wide in ((0, True), (1, False)):

        @pl.when(section == number)
        def _():
            @pl.when(step == 0)
            def _():
                for index in range(min(AHEAD, tiles)):
                    copy_of(index, is_wide).start()

            @pl.when(step + AHEAD < tiles)
            def _():
                copy_of(step + AHEAD, is_wide).start()

            copy_of(step, is_wide).wait()
            if is_wide:
                out_ref[...] = jnp.dot(value_ref[...], wide[step], preferred_element_type=F32)
            else:
                out_ref[...] = lax.dot_general(
                    value_ref[...], tall[step], CONTRACT_LAST, preferred_element_type=F32
                )


def block_product(table, value, weight, blocks):
    rows, width = value.shape
    tile = min(512, width)
    tiles = width // tile
    return pl.pallas_call(
        functools.partial(block_kernel, blocks=blocks, tile=tile, tiles=tiles),
        grid_spec=pltpu.PrefetchScalarGridSpec(
            num_scalar_prefetch=1,
            grid=(tiles,),
            in_specs=[
                pl.BlockSpec((rows, width), lambda step, table: (0, 0)),
                pl.BlockSpec(memory_space=pl.ANY),
            ],
            out_specs=pl.BlockSpec((rows, tile), lambda step, table: (0, step)),
            scratch_shapes=[
                pltpu.VMEM((tiles, width, tile), BF16),
                pltpu.VMEM((tiles, tile, width), BF16),
                pltpu.SemaphoreType.DMA((tiles,)),
            ],
        ),
        out_shape=jax.ShapeDtypeStruct((rows, width), F32),
        compiler_params=pltpu.CompilerParams(vmem_limit_bytes=24 * 1024 * 1024),
        cost_estimate=pl.CostEstimate(
            flops=8 * rows * width * width, bytes_accessed=2 * width * width, transcendentals=0
        ),
    )(table, value, weight)


def transposed_times(left, right):
    return lax.dot_general(left, right, CONTRACT_FIRST, preferred_element_type=F32)


def own_gradient_kernel(table, early, late, small_early, small_late, down_ref, up_ref):
    @pl.when(table[0] == 0)
    def _():
        down_ref[...] = transposed_times(early[...], small_late[...])
        up_ref[...] = transposed_times(small_early[...], late[...])

    @pl.when(table[0] == 1)
    def _():
        down_ref[...] = transposed_times(late[...], small_early[...])
        up_ref[...] = transposed_times(small_late[...], early[...])


def other_gradient_kernel(
    table, gain_ref, down_sum, up_sum, early, cotangent, pulled, hidden, small_early, small_late,
    down_ref, up_ref,
):
    ranks = down_ref.shape[1]
    late = small_late[:, :ranks]
    inverse = small_late[:, ranks : ranks + 1].astype(F32)
    toward = small_late[:, ranks + 64 : ranks + 65].astype(F32)

    @pl.when(table[0] == 0)
    def _():
        grad = (
            cotangent[...].astype(F32)
            + inverse * pulled[...].astype(F32)
            - toward * hidden[...].astype(F32)
        ).astype(BF16)
        down_ref[...] = down_sum[...] + transposed_times(early[...], late)
        up_ref[...] = up_sum[...] + transposed_times(small_early[...], grad)

    @pl.when(table[0] == 1)
    def _():
        scaled = (hidden[...].astype(F32) * gain_ref[...]).astype(BF16)
        weighed = (small_early[...].astype(F32) * inverse).astype(BF16)
        down_ref[...] = down_sum[...] + transposed_times(scaled, weighed)
        up_ref[...] = up_sum[...] + transposed_times(late, early[...])


def gradient_call(kernel, table, sums, by_column, whole, width, ranks, rows):
    tile = min(512, width)
    down_spec = pl.BlockSpec((tile, ranks), lambda step, table: (step, 0))
    up_spec = pl.BlockSpec((ranks, tile), lambda step, table: (0, step))
    leading = [array for array in by_column if array.shape[0] == 1]
    columns = [array for array in by_column if array.shape[0] != 1]
    return pl.pallas_call(
        kernel,
        grid_spec=pltpu.PrefetchScalarGridSpec(
            num_scalar_prefetch=1,
            grid=(width // tile,),
            in_specs=[pl.BlockSpec((1, tile), lambda step, table: (0, step)) for _ in leading]
            + [down_spec, up_spec][: len(sums)]
            + [pl.BlockSpec((rows, tile), lambda step, table: (0, step)) for _ in columns]
            + [pl.BlockSpec(array.shape, lambda step, table: (0, 0)) for array in whole],
            out_specs=[down_spec, up_spec],
        ),
        out_shape=[
            jax.ShapeDtypeStruct((width, ranks), F32),
            jax.ShapeDtypeStruct((ranks, width), F32),
        ],
        compiler_params=pltpu.CompilerParams(vmem_limit_bytes=20 * 1024 * 1024),
        cost_estimate=pl.CostEstimate(
            flops=4 * rows * width * ranks,
            bytes_accessed=8 * width * ranks * (1 + len(sums) // 2) + 2 * rows * width * len(columns),
            transcendentals=0,
        ),
    )(table, *leading, *sums, *columns, *whole)


def orders(count):
    first, first_slots, second, second_slots = [], [], [], []
    for z in range(count):
        sends = [(slot, 0, count - slot + z) for slot in range(z + 1, count)]
        sends += [(slot, 1, slot - count + z) for slot in range(count - z, count)]
        sends.sort()
        first.append([block for _, _, block in sends] + [z])
        first_slots.append({(slot, side): at for at, (slot, side, _) in enumerate(sends)})
        arrivals = [(slot, 0, z - 1 - slot) for slot in range(z)]
        arrivals += [(slot, 1, z + 1 + slot) for slot in range(count - 1 - z)]
        arrivals.sort()
        second.append([z] + [block for _, _, block in arrivals])
        second_slots.append([None] + [(slot, side) for slot, side, _ in arrivals])
    return first, first_slots, second, second_slots


def pick(number, choice, cases):
    chosen = cases[0]
    for at in range(1, len(cases)):
        members = [device for device, wanted in enumerate(choice) if wanted == at]
        chosen = jnp.where(is_one_of(number, members), cases[at], chosen)
    return chosen


def doubling_steps():
    count = lax.axis_size("tensor")
    return [
        [(place, place ^ (1 << bit)) for place in range(count)]
        for bit in range(count.bit_length() - 1)
    ]


def sum_step(value, pairs, wire=BF16, after=()):
    other = lax.ppermute(value.astype(wire), "tensor", pairs)
    if after:
        other = lax.optimization_barrier((other, *after))[0]
    return value + other.astype(F32)


def with_other_replicas(value, sections=(0, 1)):
    count = lax.axis_size("replica")
    return [value] + [
        lax.ppermute(
            value,
            ("section", "replica"),
            [(s * count + r, s * count + (r + step) % count) for s in sections for r in range(count)],
        )
        for step in range(1, count)
    ]


def on_device(
    tokens,
    cotangent,
    gain,
    frozen_base_weight,
    adapter_down_factors,
    adapter_up_factors,
    tenant_adapter_scale,
    row_tenant_owner,
):
    section = lax.axis_index("section")
    place = lax.axis_index("tensor")
    count = lax.axis_size("tensor")
    is_first = section == 0
    weight = frozen_base_weight[0]
    gain_row = gain[0][None, :]
    down = adapter_down_factors[0]
    up = adapter_up_factors[0]
    rows, width = tokens.shape
    features = width * count
    replicas = lax.axis_size("replica")
    ranks = down.shape[1]

    tenant_of_column = jnp.arange(ranks, dtype=jnp.int32) // (ranks // TENANT_COUNT)
    coefficients = jnp.where(
        row_tenant_owner[:, None] == tenant_of_column[None, :],
        jnp.repeat(tenant_adapter_scale, ranks // TENANT_COUNT)[None, :],
        0.0,
    )

    first_order, first_slots, second_order, second_slots = orders(count)
    place_of = section * count + place
    table = jnp.stack([section, place_of]).astype(jnp.int32)

    def times_down(value):
        return jnp.dot(value, down, preferred_element_type=F32)

    def times_up_transposed(value):
        return lax.dot_general(value, up, CONTRACT_LAST, preferred_element_type=F32)

    def line(value, first_pairs, second_pairs, toward):
        pairs = [(2 * z, 2 * (z + toward)) for z in first_pairs] + [
            (2 * z + 1, 2 * (z + toward) + 1) for z in second_pairs
        ]
        return lax.ppermute(value, ("tensor", "section"), pairs)

    token_float = tokens.astype(F32)
    early = jnp.where(is_first, (token_float * gain_row).astype(BF16), cotangent)
    early = lax.optimization_barrier(early)

    def small_columns(value, plain):
        small = jnp.where(is_first, times_down(value), times_up_transposed(value))
        squares = jnp.sum(plain.astype(F32) ** 2, axis=1)
        squares = jnp.pad(squares, (0, -rows % ranks)).reshape(-1, ranks)
        return jnp.concatenate([small, jnp.pad(squares, ((0, -len(squares) % 16), (0, 0)))], axis=0)

    everyone = range(count)
    steps_left = doubling_steps()
    arrivals = [
        (
            line(early, [], [z for z in everyone if z + 1 < count], 1),
            line(early, [], [z for z in everyone if z > 0], -1),
        )
    ]
    parts = []
    for stage in range(count):
        wanted = [None if stage == 0 else second_slots[z][stage] for z in everyone]
        cases = sorted({slot for slot in wanted if slot is not None})
        here = [early] + [arrivals[slot][side] for slot, side in cases]
        if stage == 1:
            small_sum = small_columns(*lax.optimization_barrier((early, tokens, *sent))[:2])
        elif stage > 1 and steps_left:
            small_sum = sum_step(small_sum, steps_left.pop(0), after=sent)
        if stage > 0:
            *here, small_sum = lax.optimization_barrier((*here, small_sum, *sent))[: len(here) + 1]
        value = pick(
            place_of,
            [0] * count + [0 if slot is None else 1 + cases.index(slot) for slot in wanted],
            here,
        )
        order = [blocks[stage] for blocks in first_order + second_order]
        part = block_product(table, value, weight, order)
        if stage == 0:
            part, after = lax.optimization_barrier((part, early))
            early_all = [early] + with_other_replicas(after)[1:]
        if stage == min(2, count - 1):
            part, *early_all = lax.optimization_barrier((part, *early_all))
        parts.append(part)
        slot = stage + 1
        if slot == count:
            break
        sent = []
        for side in (0, 1):
            needed = [first_slots[z].get((slot, side)) for z in everyone]
            stages = sorted({at for at in needed if at is not None})
            own = pick(
                place_of,
                [0 if at is None else stages.index(at) for at in needed] + [0] * count,
                [parts[at] for at in stages],
            )
            arrived = arrivals[-1][side]
            if side == 1:
                arrived, _ = lax.optimization_barrier((arrived, sent[0]))
            arrived = arrived.astype(F32)
            sent.append((arrived + jnp.where(is_first, own, 0.0)).astype(BF16))
        arrivals.append(
            (
                line(
                    sent[0],
                    [z for z in everyone if z < slot and z + 1 < count],
                    [z for z in everyone if slot + 1 < count and z >= slot and z + 1 < count],
                    1,
                ),
                line(
                    sent[1],
                    [z for z in everyone if z >= count - slot and z > 0],
                    [z for z in everyone if slot + 1 < count and z < count - slot and z > 0],
                    -1,
                ),
            )
        )
    from_left, from_right = arrivals[-1]

    while steps_left:
        small_sum = sum_step(small_sum, steps_left.pop(0))
    inv_first = lax.rsqrt(
        small_sum[rows:].reshape(-1)[:rows][:, None] / features + EPSILON
    )
    small_early = (coefficients * small_sum[:rows]).astype(BF16)
    small_early_all = with_other_replicas(
        (small_early.astype(F32) * jnp.where(is_first, inv_first, 1.0)).astype(BF16)
    )
    low_product = jnp.where(
        is_first,
        jnp.dot(small_early, up, preferred_element_type=F32),
        lax.dot_general(small_early, down, CONTRACT_LAST, preferred_element_type=F32),
    )

    pulled_here = (gain_row * (sum(parts) + low_product)).astype(BF16)
    swap = [(0, 1), (1, 0)]
    pulled = lax.ppermute(pulled_here, "section", swap)
    from_left, from_right, *small_early_all, _ = lax.optimization_barrier(
        (from_left, from_right, *small_early_all, pulled_here)
    )

    projected = parts[-1] + from_left.astype(F32) + from_right.astype(F32) + low_product
    hidden = (token_float + inv_first * projected).astype(BF16)
    late_others = with_other_replicas(jnp.where(is_first, hidden, pulled_here))[1:]
    swapped = [
        lax.ppermute(jnp.where(is_first, hidden, other), "section", swap) for other in early_all[1:]
    ]
    hidden_on_second = swapped[0] if swapped else lax.ppermute(hidden, "section", swap)
    cotangent_all = [cotangent] + swapped
    hidden_float = hidden.astype(F32)
    pulled_float = pulled.astype(F32)
    row_sums = jnp.stack(
        [jnp.sum(hidden_float * hidden_float, axis=1), jnp.sum(hidden_float * pulled_float, axis=1)]
    )
    if count <= 4:
        row_sums = row_sums + sum(
            lax.ppermute(row_sums, "tensor", [(z, (z + step) % count) for z in everyone])
            for step in range(1, count)
        )
    else:
        for step in doubling_steps():
            row_sums = sum_step(row_sums, step, F32)
    inv_second = lax.rsqrt(row_sums[0] / features + EPSILON)
    inv_second = inv_second[:, None]
    toward_hidden = row_sums[1][:, None] * inv_second * inv_second * inv_second / features
    hidden_grad = cotangent.astype(F32) + inv_second * pulled_float - toward_hidden * hidden_float
    late = jnp.where(
        is_first,
        hidden_grad.astype(BF16),
        (hidden_on_second.astype(F32) * gain_row).astype(BF16),
    )
    rank_late = jnp.where(is_first, times_up_transposed(late), times_down(late))
    inv_on_second = lax.ppermute(
        lax.optimization_barrier((inv_second[:, 0], rank_late))[0], "section", swap
    )[:, None]
    for step in doubling_steps():
        rank_late = sum_step(rank_late, step)

    inv_second = jnp.where(is_first, inv_second, inv_on_second)
    row_scale = jnp.where(is_first, inv_first, inv_second)
    small_late = (coefficients * rank_late * row_scale).astype(BF16)
    small_late_all = with_other_replicas(
        jnp.concatenate(
            [
                small_late,
                jnp.broadcast_to(inv_second, (rows, 64)).astype(BF16),
                jnp.broadcast_to(toward_hidden, (rows, 64)).astype(BF16),
            ],
            axis=1,
        )
    )
    small_early_own = (small_early.astype(F32) * row_scale).astype(BF16)
    sums = gradient_call(
        own_gradient_kernel,
        table, [], [early, late], [small_early_own, small_late], width, ranks, rows,
    )
    swapped = [
        lax.ppermute(lax.optimization_barrier((other, rank_late))[0], "section", swap)
        for other in late_others
    ]
    hidden_all = [hidden] + [jnp.where(is_first, *pair) for pair in zip(late_others, swapped)]
    pulled_all = [pulled] + swapped
    for at in range(1, replicas):
        sums = gradient_call(
            other_gradient_kernel,
            table,
            sums,
            [gain_row, early_all[at], cotangent_all[at], pulled_all[at], hidden_all[at]],
            [small_early_all[at], small_late_all[at]],
            width,
            ranks,
            rows,
        )
    grad_down, grad_up = sums
    return (grad_down[None], grad_up[None])


def solution(mesh):
    return jax.shard_map(
        on_device,
        mesh=mesh,
        in_specs=(
            P(("groups", "replica"), "tensor"),
            P(("groups", "replica"), "tensor"),
            P("section", "tensor"),
            P("section", "tensor", None),
            P("section", "tensor", None),
            P("section", None, "tensor"),
            P(),
            P(("groups", "replica")),
        ),
        out_specs=(P("section", "tensor", "groups"), P("section", "groups", "tensor")),
        check_vma=False,
    )
```

```python
import functools

import jax
import jax.numpy as jnp
from jax import lax
from jax.experimental import pallas as pl
from jax.experimental.pallas import tpu as pltpu
from jax.sharding import PartitionSpec as P

TENANT_COUNT = 4
EPSILON = 1e-05
CONTRACT_LAST = (((1,), (1,)), ((), ()))
CONTRACT_FIRST = (((0,), (0,)), ((), ()))
BF16 = jnp.bfloat16
F32 = jnp.float32
AHEAD = 2


def is_one_of(number, members):
    return functools.reduce(jnp.logical_or, [number == member for member in members])


def look_up(number, values):
    found = values[0]
    for value in sorted(set(values) - {values[0]}):
        found = jnp.where(
            is_one_of(number, [at for at, other in enumerate(values) if other == value]), value, found
        )
    return found


def block_kernel(table, value_ref, weight_ref, out_ref, wide, tall, arrived, *, blocks, tile, tiles):
    section = table[0]
    block = look_up(table[1], blocks)
    step = pl.program_id(0)
    width = tile * tiles

    def copy_of(index, is_wide):
        whole = pl.ds(pl.multiple_of(block * width, width), width)
        part = pl.ds(pl.multiple_of(block * width + index * tile, tile), tile)
        if is_wide:
            return pltpu.make_async_copy(weight_ref.at[:, part], wide.at[index], arrived.at[index])
        rows = pl.ds(pl.multiple_of(index * tile, tile), tile)
        return pltpu.make_async_copy(weight_ref.at[rows, whole], tall.at[index], arrived.at[index])

    for number, is_wide in ((0, True), (1, False)):

        @pl.when(section == number)
        def _():
            @pl.when(step == 0)
            def _():
                for index in range(min(AHEAD, tiles)):
                    copy_of(index, is_wide).start()

            @pl.when(step + AHEAD < tiles)
            def _():
                copy_of(step + AHEAD, is_wide).start()

            copy_of(step, is_wide).wait()
            if is_wide:
                out_ref[...] = jnp.dot(value_ref[...], wide[step], preferred_element_type=F32)
            else:
                out_ref[...] = lax.dot_general(
                    value_ref[...], tall[step], CONTRACT_LAST, preferred_element_type=F32
                )


def block_product(table, value, weight, blocks):
    rows, width = value.shape
    tile = min(512, width)
    tiles = width // tile
    return pl.pallas_call(
        functools.partial(block_kernel, blocks=blocks, tile=tile, tiles=tiles),
        grid_spec=pltpu.PrefetchScalarGridSpec(
            num_scalar_prefetch=1,
            grid=(tiles,),
            in_specs=[
                pl.BlockSpec((rows, width), lambda step, table: (0, 0)),
                pl.BlockSpec(memory_space=pl.ANY),
            ],
            out_specs=pl.BlockSpec((rows, tile), lambda step, table: (0, step)),
            scratch_shapes=[
                pltpu.VMEM((tiles, width, tile), BF16),
                pltpu.VMEM((tiles, tile, width), BF16),
                pltpu.SemaphoreType.DMA((tiles,)),
            ],
        ),
        out_shape=jax.ShapeDtypeStruct((rows, width), F32),
        compiler_params=pltpu.CompilerParams(vmem_limit_bytes=24 * 1024 * 1024),
        cost_estimate=pl.CostEstimate(
            flops=8 * rows * width * width, bytes_accessed=2 * width * width, transcendentals=0
        ),
    )(table, value, weight)


def transposed_times(left, right):
    return lax.dot_general(left, right, CONTRACT_FIRST, preferred_element_type=F32)


def own_gradient_kernel(table, early, late, small_early, small_late, down_ref, up_ref):
    @pl.when(table[0] == 0)
    def _():
        down_ref[...] = transposed_times(early[...], small_late[...])
        up_ref[...] = transposed_times(small_early[...], late[...])

    @pl.when(table[0] == 1)
    def _():
        down_ref[...] = transposed_times(late[...], small_early[...])
        up_ref[...] = transposed_times(small_late[...], early[...])


def other_gradient_kernel(
    table, gain_ref, down_sum, up_sum, early, cotangent, pulled, hidden, small_early, small_late,
    down_ref, up_ref,
):
    ranks = down_ref.shape[1]
    late = small_late[:, :ranks]
    inverse = small_late[:, ranks : ranks + 1].astype(F32)
    toward = small_late[:, ranks + 64 : ranks + 65].astype(F32)

    @pl.when(table[0] == 0)
    def _():
        grad = (
            cotangent[...].astype(F32)
            + inverse * pulled[...].astype(F32)
            - toward * hidden[...].astype(F32)
        ).astype(BF16)
        down_ref[...] = down_sum[...] + transposed_times(early[...], late)
        up_ref[...] = up_sum[...] + transposed_times(small_early[...], grad)

    @pl.when(table[0] == 1)
    def _():
        scaled = (hidden[...].astype(F32) * gain_ref[...]).astype(BF16)
        weighed = (small_early[...].astype(F32) * inverse).astype(BF16)
        down_ref[...] = down_sum[...] + transposed_times(scaled, weighed)
        up_ref[...] = up_sum[...] + transposed_times(late, early[...])


def gradient_call(kernel, table, sums, by_column, whole, width, ranks, rows):
    tile = min(512, width)
    down_spec = pl.BlockSpec((tile, ranks), lambda step, table: (step, 0))
    up_spec = pl.BlockSpec((ranks, tile), lambda step, table: (0, step))
    leading = [array for array in by_column if array.shape[0] == 1]
    columns = [array for array in by_column if array.shape[0] != 1]
    return pl.pallas_call(
        kernel,
        grid_spec=pltpu.PrefetchScalarGridSpec(
            num_scalar_prefetch=1,
            grid=(width // tile,),
            in_specs=[pl.BlockSpec((1, tile), lambda step, table: (0, step)) for _ in leading]
            + [down_spec, up_spec][: len(sums)]
            + [pl.BlockSpec((rows, tile), lambda step, table: (0, step)) for _ in columns]
            + [pl.BlockSpec(array.shape, lambda step, table: (0, 0)) for array in whole],
            out_specs=[down_spec, up_spec],
        ),
        out_shape=[
            jax.ShapeDtypeStruct((width, ranks), F32),
            jax.ShapeDtypeStruct((ranks, width), F32),
        ],
        compiler_params=pltpu.CompilerParams(vmem_limit_bytes=20 * 1024 * 1024),
        cost_estimate=pl.CostEstimate(
            flops=4 * rows * width * ranks,
            bytes_accessed=8 * width * ranks * (1 + len(sums) // 2) + 2 * rows * width * len(columns),
            transcendentals=0,
        ),
    )(table, *leading, *sums, *columns, *whole)


def orders(count):
    first, first_slots, second, second_slots = [], [], [], []
    for z in range(count):
        sends = [(slot, 0, count - slot + z) for slot in range(z + 1, count)]
        sends += [(slot, 1, slot - count + z) for slot in range(count - z, count)]
        sends.sort()
        first.append([block for _, _, block in sends] + [z])
        first_slots.append({(slot, side): at for at, (slot, side, _) in enumerate(sends)})
        arrivals = [(slot, 0, z - 1 - slot) for slot in range(z)]
        arrivals += [(slot, 1, z + 1 + slot) for slot in range(count - 1 - z)]
        arrivals.sort()
        second.append([z] + [block for _, _, block in arrivals])
        second_slots.append([None] + [(slot, side) for slot, side, _ in arrivals])
    return first, first_slots, second, second_slots


def pick(number, choice, cases):
    chosen = cases[0]
    for at in range(1, len(cases)):
        members = [device for device, wanted in enumerate(choice) if wanted == at]
        chosen = jnp.where(is_one_of(number, members), cases[at], chosen)
    return chosen


def doubling_steps():
    count = lax.axis_size("tensor")
    return [
        [(place, place ^ (1 << bit)) for place in range(count)]
        for bit in range(count.bit_length() - 1)
    ]


def sum_step(value, pairs, wire=BF16, after=()):
    other = lax.ppermute(value.astype(wire), "tensor", pairs)
    if after:
        other = lax.optimization_barrier((other, *after))[0]
    return value + other.astype(F32)


def with_other_replicas(value, sections=(0, 1)):
    count = lax.axis_size("replica")
    return [value] + [
        lax.ppermute(
            value,
            ("section", "replica"),
            [(s * count + r, s * count + (r + step) % count) for s in sections for r in range(count)],
        )
        for step in range(1, count)
    ]


def on_device(
    tokens,
    cotangent,
    gain,
    frozen_base_weight,
    adapter_down_factors,
    adapter_up_factors,
    tenant_adapter_scale,
    row_tenant_owner,
):
    section = lax.axis_index("section")
    place = lax.axis_index("tensor")
    count = lax.axis_size("tensor")
    is_first = section == 0
    weight = frozen_base_weight[0]
    gain_row = gain[0][None, :]
    down = adapter_down_factors[0]
    up = adapter_up_factors[0]
    rows, width = tokens.shape
    features = width * count
    replicas = lax.axis_size("replica")
    ranks = down.shape[1]

    tenant_of_column = jnp.arange(ranks, dtype=jnp.int32) // (ranks // TENANT_COUNT)
    coefficients = jnp.where(
        row_tenant_owner[:, None] == tenant_of_column[None, :],
        jnp.repeat(tenant_adapter_scale, ranks // TENANT_COUNT)[None, :],
        0.0,
    )

    first_order, first_slots, second_order, second_slots = orders(count)
    place_of = section * count + place
    table = jnp.stack([section, place_of]).astype(jnp.int32)

    def times_down(value):
        return jnp.dot(value, down, preferred_element_type=F32)

    def times_up_transposed(value):
        return lax.dot_general(value, up, CONTRACT_LAST, preferred_element_type=F32)

    def line(value, first_pairs, second_pairs, toward):
        pairs = [(2 * z, 2 * (z + toward)) for z in first_pairs] + [
            (2 * z + 1, 2 * (z + toward) + 1) for z in second_pairs
        ]
        return lax.ppermute(value, ("tensor", "section"), pairs)

    token_float = tokens.astype(F32)
    early = jnp.where(is_first, (token_float * gain_row).astype(BF16), cotangent)
    early = lax.optimization_barrier(early)

    def small_columns(value, plain):
        small = jnp.where(is_first, times_down(value), times_up_transposed(value))
        squares = jnp.sum(plain.astype(F32) ** 2, axis=1)
        squares = jnp.pad(squares, (0, -rows % ranks)).reshape(-1, ranks)
        return jnp.concatenate([small, jnp.pad(squares, ((0, -len(squares) % 16), (0, 0)))], axis=0)

    everyone = range(count)
    steps_left = doubling_steps()
    arrivals = [
        (
            lax.ppermute(
                cotangent,
                ("tensor", "section"),
                [(2 * z, 2 * (z + 1) + 1) for z in everyone if z + 1 < count],
            ),
            line(cotangent, [], [z for z in everyone if z > 0], -1),
        )
    ]
    parts = []
    for stage in range(count):
        wanted = [None if stage == 0 else second_slots[z][stage] for z in everyone]
        cases = sorted({slot for slot in wanted if slot is not None})
        here = [early] + [arrivals[slot][side] for slot, side in cases]
        if stage == 1:
            small_sum = small_columns(*lax.optimization_barrier((early, tokens, *sent))[:2])
        elif stage > 1 and steps_left:
            small_sum = sum_step(small_sum, steps_left.pop(0), after=sent)
        if stage > 0:
            *here, small_sum = lax.optimization_barrier((*here, small_sum, *sent))[: len(here) + 1]
        value = pick(
            place_of,
            [0] * count + [0 if slot is None else 1 + cases.index(slot) for slot in wanted],
            here,
        )
        order = [blocks[stage] for blocks in first_order + second_order]
        part = block_product(table, value, weight, order)
        if stage == 1:
            part, after = lax.optimization_barrier((part, early))
            early_all = [early] + with_other_replicas(after)[1:]
        if stage == count - 1:
            part, *early_all = lax.optimization_barrier((part, *early_all))
        parts.append(part)
        slot = stage + 1
        if slot == count:
            break
        sent = []
        for side in (0, 1):
            needed = [first_slots[z].get((slot, side)) for z in everyone]
            stages = sorted({at for at in needed if at is not None})
            own = pick(
                place_of,
                [0 if at is None else stages.index(at) for at in needed] + [0] * count,
                [parts[at] for at in stages],
            )
            arrived = arrivals[-1][side]
            if side == 1:
                arrived, _ = lax.optimization_barrier((arrived, sent[0]))
            arrived = arrived.astype(F32)
            sent.append((arrived + jnp.where(is_first, own, 0.0)).astype(BF16))
        arrivals.append(
            (
                line(
                    sent[0],
                    [z for z in everyone if z < slot and z + 1 < count],
                    [z for z in everyone if slot + 1 < count and z >= slot and z + 1 < count],
                    1,
                ),
                line(
                    sent[1],
                    [z for z in everyone if z >= count - slot and z > 0],
                    [z for z in everyone if slot + 1 < count and z < count - slot and z > 0],
                    -1,
                ),
            )
        )
    from_left, from_right = arrivals[-1]

    while steps_left:
        small_sum = sum_step(small_sum, steps_left.pop(0))
    inv_first = lax.rsqrt(
        small_sum[rows:].reshape(-1)[:rows][:, None] / features + EPSILON
    )
    small_early = (coefficients * small_sum[:rows]).astype(BF16)
    small_early_all = with_other_replicas(
        (small_early.astype(F32) * jnp.where(is_first, inv_first, 1.0)).astype(BF16)
    )
    low_product = jnp.where(
        is_first,
        jnp.dot(small_early, up, preferred_element_type=F32),
        lax.dot_general(small_early, down, CONTRACT_LAST, preferred_element_type=F32),
    )

    pulled_here = (gain_row * (sum(parts) + low_product)).astype(BF16)
    swap = [(0, 1), (1, 0)]
    pulled = lax.ppermute(pulled_here, "section", swap)
    from_left, from_right, *small_early_all, _ = lax.optimization_barrier(
        (from_left, from_right, *small_early_all, pulled_here)
    )

    projected = parts[-1] + from_left.astype(F32) + from_right.astype(F32) + low_product
    hidden = (token_float + inv_first * projected).astype(BF16)
    half = width // 2 if width % 256 == 0 else width
    exchanged = jnp.where(is_first, hidden, pulled_here)
    first_halves = with_other_replicas(exchanged[:, :half])[1:]
    second_halves = with_other_replicas(exchanged[:, half:])[1:] if half < width else None
    swapped = [
        lax.ppermute(jnp.where(is_first, hidden, other), "section", swap) for other in early_all[1:]
    ]
    hidden_on_second = swapped[0] if swapped else lax.ppermute(hidden, "section", swap)
    cotangent_all = [cotangent] + swapped
    hidden_float = hidden.astype(F32)
    pulled_float = pulled.astype(F32)
    row_sums = jnp.stack(
        [jnp.sum(hidden_float * hidden_float, axis=1), jnp.sum(hidden_float * pulled_float, axis=1)]
    )
    if count <= 4:
        row_sums = row_sums + sum(
            lax.ppermute(row_sums, "tensor", [(z, (z + step) % count) for z in everyone])
            for step in range(1, count)
        )
    else:
        for step in doubling_steps():
            row_sums = sum_step(row_sums, step, F32)
    row_sums, *first_halves = lax.optimization_barrier((row_sums, *first_halves))
    inv_second = lax.rsqrt(row_sums[0] / features + EPSILON)
    inv_second = inv_second[:, None]
    toward_hidden = row_sums[1][:, None] * inv_second * inv_second * inv_second / features
    hidden_grad = cotangent.astype(F32) + inv_second * pulled_float - toward_hidden * hidden_float
    late = jnp.where(
        is_first,
        hidden_grad.astype(BF16),
        (hidden_on_second.astype(F32) * gain_row).astype(BF16),
    )
    rank_late = jnp.where(is_first, times_up_transposed(late), times_down(late))
    inv_on_second = lax.ppermute(
        lax.optimization_barrier((inv_second[:, 0], rank_late))[0], "section", swap
    )[:, None]
    for step in doubling_steps():
        rank_late = sum_step(rank_late, step)

    late_others = first_halves
    if second_halves is not None:
        *second_halves, _ = lax.optimization_barrier((*second_halves, rank_late))
        late_others = [
            jnp.concatenate(halves, axis=1) for halves in zip(first_halves, second_halves)
        ]
    inv_second = jnp.where(is_first, inv_second, inv_on_second)
    row_scale = jnp.where(is_first, inv_first, inv_second)
    small_late = (coefficients * rank_late * row_scale).astype(BF16)
    small_late_all = with_other_replicas(
        jnp.concatenate(
            [
                small_late,
                jnp.broadcast_to(inv_second, (rows, 64)).astype(BF16),
                jnp.broadcast_to(toward_hidden, (rows, 64)).astype(BF16),
            ],
            axis=1,
        )
    )
    small_early_own = (small_early.astype(F32) * row_scale).astype(BF16)
    sums = gradient_call(
        own_gradient_kernel,
        table, [], [early, late], [small_early_own, small_late], width, ranks, rows,
    )
    swapped = [
        lax.ppermute(lax.optimization_barrier((other, rank_late))[0], "section", swap)
        for other in late_others
    ]
    hidden_all = [hidden] + [jnp.where(is_first, *pair) for pair in zip(late_others, swapped)]
    pulled_all = [pulled] + swapped
    for at in range(1, replicas):
        sums = gradient_call(
            other_gradient_kernel,
            table,
            sums,
            [gain_row, early_all[at], cotangent_all[at], pulled_all[at], hidden_all[at]],
            [small_early_all[at], small_late_all[at]],
            width,
            ranks,
            rows,
        )
    grad_down, grad_up = sums
    return (grad_down[None], grad_up[None])


def solution(mesh):
    return jax.shard_map(
        on_device,
        mesh=mesh,
        in_specs=(
            P(("groups", "replica"), "tensor"),
            P(("groups", "replica"), "tensor"),
            P("section", "tensor"),
            P("section", "tensor", None),
            P("section", "tensor", None),
            P("section", None, "tensor"),
            P(),
            P(("groups", "replica")),
        ),
        out_specs=(P("section", "tensor", "groups"), P("section", "groups", "tensor")),
        check_vma=False,
    )
```

```python
import functools

import jax
import jax.numpy as jnp
from jax import lax
from jax.experimental import pallas as pl
from jax.experimental.pallas import tpu as pltpu
from jax.sharding import PartitionSpec as P

TENANT_COUNT = 4
EPSILON = 1e-05
CONTRACT_LAST = (((1,), (1,)), ((), ()))
CONTRACT_FIRST = (((0,), (0,)), ((), ()))
BF16 = jnp.bfloat16
F32 = jnp.float32
AHEAD = 2


def is_one_of(number, members):
    return functools.reduce(jnp.logical_or, [number == member for member in members])


def look_up(number, values):
    found = values[0]
    for value in sorted(set(values) - {values[0]}):
        found = jnp.where(
            is_one_of(number, [at for at, other in enumerate(values) if other == value]), value, found
        )
    return found


def block_kernel(table, value_ref, weight_ref, out_ref, wide, tall, arrived, *, blocks, tile, tiles):
    section = table[0]
    block = look_up(table[1], blocks)
    step = pl.program_id(0)
    width = tile * tiles

    def copy_of(index, is_wide):
        whole = pl.ds(pl.multiple_of(block * width, width), width)
        part = pl.ds(pl.multiple_of(block * width + index * tile, tile), tile)
        if is_wide:
            return pltpu.make_async_copy(weight_ref.at[:, part], wide.at[index], arrived.at[index])
        rows = pl.ds(pl.multiple_of(index * tile, tile), tile)
        return pltpu.make_async_copy(weight_ref.at[rows, whole], tall.at[index], arrived.at[index])

    for number, is_wide in ((0, True), (1, False)):

        @pl.when(section == number)
        def _():
            @pl.when(step == 0)
            def _():
                for index in range(min(AHEAD, tiles)):
                    copy_of(index, is_wide).start()

            @pl.when(step + AHEAD < tiles)
            def _():
                copy_of(step + AHEAD, is_wide).start()

            copy_of(step, is_wide).wait()
            if is_wide:
                out_ref[...] = jnp.dot(value_ref[...], wide[step], preferred_element_type=F32)
            else:
                out_ref[...] = lax.dot_general(
                    value_ref[...], tall[step], CONTRACT_LAST, preferred_element_type=F32
                )


def block_product(table, value, weight, blocks):
    rows, width = value.shape
    tile = min(512, width)
    tiles = width // tile
    return pl.pallas_call(
        functools.partial(block_kernel, blocks=blocks, tile=tile, tiles=tiles),
        grid_spec=pltpu.PrefetchScalarGridSpec(
            num_scalar_prefetch=1,
            grid=(tiles,),
            in_specs=[
                pl.BlockSpec((rows, width), lambda step, table: (0, 0)),
                pl.BlockSpec(memory_space=pl.ANY),
            ],
            out_specs=pl.BlockSpec((rows, tile), lambda step, table: (0, step)),
            scratch_shapes=[
                pltpu.VMEM((tiles, width, tile), BF16),
                pltpu.VMEM((tiles, tile, width), BF16),
                pltpu.SemaphoreType.DMA((tiles,)),
            ],
        ),
        out_shape=jax.ShapeDtypeStruct((rows, width), F32),
        compiler_params=pltpu.CompilerParams(vmem_limit_bytes=24 * 1024 * 1024),
        cost_estimate=pl.CostEstimate(
            flops=8 * rows * width * width, bytes_accessed=2 * width * width, transcendentals=0
        ),
    )(table, value, weight)


def transposed_times(left, right):
    return lax.dot_general(left, right, CONTRACT_FIRST, preferred_element_type=F32)


def own_gradient_kernel(table, early, late, small_early, small_late, down_ref, up_ref):
    @pl.when(table[0] == 0)
    def _():
        down_ref[...] = transposed_times(early[...], small_late[...])
        up_ref[...] = transposed_times(small_early[...], late[...])

    @pl.when(table[0] == 1)
    def _():
        down_ref[...] = transposed_times(late[...], small_early[...])
        up_ref[...] = transposed_times(small_late[...], early[...])


def other_gradient_kernel(
    table, gain_ref, down_sum, up_sum, early, cotangent, pulled, hidden, small_early, small_late,
    down_ref, up_ref,
):
    ranks = down_ref.shape[1]
    late = small_late[:, :ranks]
    inverse = small_late[:, ranks : ranks + 1].astype(F32)
    toward = small_late[:, ranks + 64 : ranks + 65].astype(F32)

    @pl.when(table[0] == 0)
    def _():
        grad = (
            cotangent[...].astype(F32)
            + inverse * pulled[...].astype(F32)
            - toward * hidden[...].astype(F32)
        ).astype(BF16)
        down_ref[...] = down_sum[...] + transposed_times(early[...], late)
        up_ref[...] = up_sum[...] + transposed_times(small_early[...], grad)

    @pl.when(table[0] == 1)
    def _():
        scaled = (hidden[...].astype(F32) * gain_ref[...]).astype(BF16)
        weighed = (small_early[...].astype(F32) * inverse).astype(BF16)
        down_ref[...] = down_sum[...] + transposed_times(scaled, weighed)
        up_ref[...] = up_sum[...] + transposed_times(late, early[...])


def gradient_call(kernel, table, sums, by_column, whole, width, ranks, rows):
    tile = min(512, width)
    down_spec = pl.BlockSpec((tile, ranks), lambda step, table: (step, 0))
    up_spec = pl.BlockSpec((ranks, tile), lambda step, table: (0, step))
    leading = [array for array in by_column if array.shape[0] == 1]
    columns = [array for array in by_column if array.shape[0] != 1]
    return pl.pallas_call(
        kernel,
        grid_spec=pltpu.PrefetchScalarGridSpec(
            num_scalar_prefetch=1,
            grid=(width // tile,),
            in_specs=[pl.BlockSpec((1, tile), lambda step, table: (0, step)) for _ in leading]
            + [down_spec, up_spec][: len(sums)]
            + [pl.BlockSpec((rows, tile), lambda step, table: (0, step)) for _ in columns]
            + [pl.BlockSpec(array.shape, lambda step, table: (0, 0)) for array in whole],
            out_specs=[down_spec, up_spec],
        ),
        out_shape=[
            jax.ShapeDtypeStruct((width, ranks), F32),
            jax.ShapeDtypeStruct((ranks, width), F32),
        ],
        compiler_params=pltpu.CompilerParams(vmem_limit_bytes=20 * 1024 * 1024),
        cost_estimate=pl.CostEstimate(
            flops=4 * rows * width * ranks,
            bytes_accessed=8 * width * ranks * (1 + len(sums) // 2) + 2 * rows * width * len(columns),
            transcendentals=0,
        ),
    )(table, *leading, *sums, *columns, *whole)


def orders(count):
    first, first_slots, second, second_slots = [], [], [], []
    for z in range(count):
        sends = [(slot, 0, count - slot + z) for slot in range(z + 1, count)]
        sends += [(slot, 1, slot - count + z) for slot in range(count - z, count)]
        sends.sort()
        first.append([block for _, _, block in sends] + [z])
        first_slots.append({(slot, side): at for at, (slot, side, _) in enumerate(sends)})
        arrivals = [(slot, 0, z - 1 - slot) for slot in range(z)]
        arrivals += [(slot, 1, z + 1 + slot) for slot in range(count - 1 - z)]
        arrivals.sort()
        second.append([z] + [block for _, _, block in arrivals])
        second_slots.append([None] + [(slot, side) for slot, side, _ in arrivals])
    return first, first_slots, second, second_slots


def pick(number, choice, cases):
    chosen = cases[0]
    for at in range(1, len(cases)):
        members = [device for device, wanted in enumerate(choice) if wanted == at]
        chosen = jnp.where(is_one_of(number, members), cases[at], chosen)
    return chosen


def doubling_steps():
    count = lax.axis_size("tensor")
    return [
        [(place, place ^ (1 << bit)) for place in range(count)]
        for bit in range(count.bit_length() - 1)
    ]


def sum_step(value, pairs, wire=BF16, after=()):
    other = lax.ppermute(value.astype(wire), "tensor", pairs)
    if after:
        other = lax.optimization_barrier((other, *after))[0]
    return value + other.astype(F32)


def with_other_replicas(value, sections=(0, 1)):
    count = lax.axis_size("replica")
    return [value] + [
        lax.ppermute(
            value,
            ("section", "replica"),
            [(s * count + r, s * count + (r + step) % count) for s in sections for r in range(count)],
        )
        for step in range(1, count)
    ]


def on_device(
    tokens,
    cotangent,
    gain,
    frozen_base_weight,
    adapter_down_factors,
    adapter_up_factors,
    tenant_adapter_scale,
    row_tenant_owner,
):
    section = lax.axis_index("section")
    place = lax.axis_index("tensor")
    count = lax.axis_size("tensor")
    is_first = section == 0
    weight = frozen_base_weight[0]
    gain_row = gain[0][None, :]
    down = adapter_down_factors[0]
    up = adapter_up_factors[0]
    rows, width = tokens.shape
    features = width * count
    replicas = lax.axis_size("replica")
    ranks = down.shape[1]

    tenant_of_column = jnp.arange(ranks, dtype=jnp.int32) // (ranks // TENANT_COUNT)
    coefficients = jnp.where(
        row_tenant_owner[:, None] == tenant_of_column[None, :],
        jnp.repeat(tenant_adapter_scale, ranks // TENANT_COUNT)[None, :],
        0.0,
    )

    first_order, first_slots, second_order, second_slots = orders(count)
    place_of = section * count + place
    table = jnp.stack([section, place_of]).astype(jnp.int32)

    def times_down(value):
        return jnp.dot(value, down, preferred_element_type=F32)

    def times_up_transposed(value):
        return lax.dot_general(value, up, CONTRACT_LAST, preferred_element_type=F32)

    def line(value, first_pairs, second_pairs, toward):
        pairs = [(2 * z, 2 * (z + toward)) for z in first_pairs] + [
            (2 * z + 1, 2 * (z + toward) + 1) for z in second_pairs
        ]
        return lax.ppermute(value, ("tensor", "section"), pairs)

    token_float = tokens.astype(F32)
    early = jnp.where(is_first, (token_float * gain_row).astype(BF16), cotangent)
    early = lax.optimization_barrier(early)

    def small_columns(value, plain):
        small = jnp.where(is_first, times_down(value), times_up_transposed(value))
        squares = jnp.sum(plain.astype(F32) ** 2, axis=1)
        squares = jnp.pad(squares, (0, -rows % ranks)).reshape(-1, ranks)
        return jnp.concatenate([small, jnp.pad(squares, ((0, -len(squares) % 16), (0, 0)))], axis=0)

    everyone = range(count)
    steps_left = doubling_steps()
    arrivals = [
        (
            lax.ppermute(
                cotangent,
                ("tensor", "section"),
                [(2 * z, 2 * (z + 1) + 1) for z in everyone if z + 1 < count],
            ),
            line(cotangent, [], [z for z in everyone if z > 0], -1),
        )
    ]
    parts = []
    for stage in range(count):
        wanted = [None if stage == 0 else second_slots[z][stage] for z in everyone]
        cases = sorted({slot for slot in wanted if slot is not None})
        here = [early] + [arrivals[slot][side] for slot, side in cases]
        if stage == 1:
            small_sum = small_columns(*lax.optimization_barrier((early, tokens, *sent))[:2])
        elif stage > 1 and steps_left:
            small_sum = sum_step(small_sum, steps_left.pop(0), after=sent)
        if stage > 0:
            *here, small_sum = lax.optimization_barrier((*here, small_sum, *sent))[: len(here) + 1]
        value = pick(
            place_of,
            [0] * count + [0 if slot is None else 1 + cases.index(slot) for slot in wanted],
            here,
        )
        order = [blocks[stage] for blocks in first_order + second_order]
        part = block_product(table, value, weight, order)
        if stage == 1:
            part, after = lax.optimization_barrier((part, early))
            early_all = [early] + with_other_replicas(after)[1:]
        if stage == count - 1:
            part, *early_all = lax.optimization_barrier((part, *early_all))
        parts.append(part)
        slot = stage + 1
        if slot == count:
            break
        sent = []
        for side in (0, 1):
            needed = [first_slots[z].get((slot, side)) for z in everyone]
            stages = sorted({at for at in needed if at is not None})
            own = pick(
                place_of,
                [0 if at is None else stages.index(at) for at in needed] + [0] * count,
                [parts[at] for at in stages],
            )
            arrived = arrivals[-1][side]
            if side == 1:
                arrived, _ = lax.optimization_barrier((arrived, sent[0]))
            arrived = arrived.astype(F32)
            sent.append((arrived + jnp.where(is_first, own, 0.0)).astype(BF16))
        arrivals.append(
            (
                line(
                    sent[0],
                    [z for z in everyone if z < slot and z + 1 < count],
                    [z for z in everyone if slot + 1 < count and z >= slot and z + 1 < count],
                    1,
                ),
                line(
                    sent[1],
                    [z for z in everyone if z >= count - slot and z > 0],
                    [z for z in everyone if slot + 1 < count and z < count - slot and z > 0],
                    -1,
                ),
            )
        )
    from_left, from_right = arrivals[-1]

    while steps_left:
        small_sum = sum_step(small_sum, steps_left.pop(0))
    inv_first = lax.rsqrt(
        small_sum[rows:].reshape(-1)[:rows][:, None] / features + EPSILON
    )
    small_early = (coefficients * small_sum[:rows]).astype(BF16)
    small_early_all = with_other_replicas(
        (small_early.astype(F32) * jnp.where(is_first, inv_first, 1.0)).astype(BF16)
    )
    low_product = jnp.where(
        is_first,
        jnp.dot(small_early, up, preferred_element_type=F32),
        lax.dot_general(small_early, down, CONTRACT_LAST, preferred_element_type=F32),
    )

    pulled_here = (gain_row * (sum(parts) + low_product)).astype(BF16)
    swap = [(0, 1), (1, 0)]
    pulled = lax.ppermute(pulled_here, "section", swap)
    from_left, from_right, *small_early_all, _ = lax.optimization_barrier(
        (from_left, from_right, *small_early_all, pulled_here)
    )

    projected = parts[-1] + from_left.astype(F32) + from_right.astype(F32) + low_product
    hidden = (token_float + inv_first * projected).astype(BF16)
    cut = width // 4 if width % 512 == 0 else width
    exchanged = jnp.where(is_first, hidden, pulled_here)
    first_columns = with_other_replicas(exchanged[:, :cut])[1:]
    other_columns = with_other_replicas(exchanged[:, cut:])[1:] if cut < width else None
    swapped = [
        lax.ppermute(jnp.where(is_first, hidden, other), "section", swap) for other in early_all[1:]
    ]
    hidden_on_second = swapped[0] if swapped else lax.ppermute(hidden, "section", swap)
    cotangent_all = [cotangent] + swapped
    hidden_float = hidden.astype(F32)
    pulled_float = pulled.astype(F32)
    row_sums = jnp.stack(
        [jnp.sum(hidden_float * hidden_float, axis=1), jnp.sum(hidden_float * pulled_float, axis=1)]
    )
    if count <= 4:
        row_sums = row_sums + sum(
            lax.ppermute(row_sums, "tensor", [(z, (z + step) % count) for z in everyone])
            for step in range(1, count)
        )
    else:
        for step in doubling_steps():
            row_sums = sum_step(row_sums, step, F32)
    row_sums, *first_columns = lax.optimization_barrier((row_sums, *first_columns))
    inv_second = lax.rsqrt(row_sums[0] / features + EPSILON)
    inv_second = inv_second[:, None]
    toward_hidden = row_sums[1][:, None] * inv_second * inv_second * inv_second / features
    hidden_grad = cotangent.astype(F32) + inv_second * pulled_float - toward_hidden * hidden_float
    late = jnp.where(
        is_first,
        hidden_grad.astype(BF16),
        (hidden_on_second.astype(F32) * gain_row).astype(BF16),
    )
    rank_late = jnp.where(is_first, times_up_transposed(late), times_down(late))
    inv_on_second = lax.ppermute(
        lax.optimization_barrier((inv_second[:, 0], rank_late))[0], "section", swap
    )[:, None]
    for step in doubling_steps():
        rank_late = sum_step(rank_late, step)

    late_others = first_columns
    if other_columns is not None:
        *other_columns, _ = lax.optimization_barrier((*other_columns, rank_late))
        late_others = [
            jnp.concatenate(both, axis=1) for both in zip(first_columns, other_columns)
        ]
    inv_second = jnp.where(is_first, inv_second, inv_on_second)
    row_scale = jnp.where(is_first, inv_first, inv_second)
    small_late = (coefficients * rank_late * row_scale).astype(BF16)
    small_late_all = with_other_replicas(
        jnp.concatenate(
            [
                small_late,
                jnp.broadcast_to(inv_second, (rows, 64)).astype(BF16),
                jnp.broadcast_to(toward_hidden, (rows, 64)).astype(BF16),
            ],
            axis=1,
        )
    )
    small_early_own = (small_early.astype(F32) * row_scale).astype(BF16)
    sums = gradient_call(
        own_gradient_kernel,
        table, [], [early, late], [small_early_own, small_late], width, ranks, rows,
    )
    swapped = [
        lax.ppermute(lax.optimization_barrier((other, rank_late))[0], "section", swap)
        for other in late_others
    ]
    hidden_all = [hidden] + [jnp.where(is_first, *pair) for pair in zip(late_others, swapped)]
    pulled_all = [pulled] + swapped
    for at in range(1, replicas):
        sums = gradient_call(
            other_gradient_kernel,
            table,
            sums,
            [gain_row, early_all[at], cotangent_all[at], pulled_all[at], hidden_all[at]],
            [small_early_all[at], small_late_all[at]],
            width,
            ranks,
            rows,
        )
    grad_down, grad_up = sums
    return (grad_down[None], grad_up[None])


def solution(mesh):
    return jax.shard_map(
        on_device,
        mesh=mesh,
        in_specs=(
            P(("groups", "replica"), "tensor"),
            P(("groups", "replica"), "tensor"),
            P("section", "tensor"),
            P("section", "tensor", None),
            P("section", "tensor", None),
            P("section", None, "tensor"),
            P(),
            P(("groups", "replica")),
        ),
        out_specs=(P("section", "tensor", "groups"), P("section", "groups", "tensor")),
        check_vma=False,
    )
```

```python
import functools

import jax
import jax.numpy as jnp
from jax import lax
from jax.experimental import pallas as pl
from jax.experimental.pallas import tpu as pltpu
from jax.sharding import PartitionSpec as P

TENANT_COUNT = 4
EPSILON = 1e-05
CONTRACT_LAST = (((1,), (1,)), ((), ()))
CONTRACT_FIRST = (((0,), (0,)), ((), ()))
BF16 = jnp.bfloat16
F32 = jnp.float32
AHEAD = 2


def is_one_of(number, members):
    return functools.reduce(jnp.logical_or, [number == member for member in members])


def look_up(number, values):
    found = values[0]
    for value in sorted(set(values) - {values[0]}):
        found = jnp.where(
            is_one_of(number, [at for at, other in enumerate(values) if other == value]), value, found
        )
    return found


def block_kernel(table, value_ref, weight_ref, out_ref, wide, tall, arrived, *, blocks, tile, tiles):
    section = table[0]
    block = look_up(table[1], blocks)
    step = pl.program_id(0)
    width = tile * tiles

    def copy_of(index, is_wide):
        whole = pl.ds(pl.multiple_of(block * width, width), width)
        part = pl.ds(pl.multiple_of(block * width + index * tile, tile), tile)
        if is_wide:
            return pltpu.make_async_copy(weight_ref.at[:, part], wide.at[index], arrived.at[index])
        rows = pl.ds(pl.multiple_of(index * tile, tile), tile)
        return pltpu.make_async_copy(weight_ref.at[rows, whole], tall.at[index], arrived.at[index])

    for number, is_wide in ((0, True), (1, False)):

        @pl.when(section == number)
        def _():
            @pl.when(step == 0)
            def _():
                for index in range(min(AHEAD, tiles)):
                    copy_of(index, is_wide).start()

            @pl.when(step + AHEAD < tiles)
            def _():
                copy_of(step + AHEAD, is_wide).start()

            copy_of(step, is_wide).wait()
            if is_wide:
                out_ref[...] = jnp.dot(value_ref[...], wide[step], preferred_element_type=F32)
            else:
                out_ref[...] = lax.dot_general(
                    value_ref[...], tall[step], CONTRACT_LAST, preferred_element_type=F32
                )


def block_product(table, value, weight, blocks):
    rows, width = value.shape
    tile = min(512, width)
    tiles = width // tile
    return pl.pallas_call(
        functools.partial(block_kernel, blocks=blocks, tile=tile, tiles=tiles),
        grid_spec=pltpu.PrefetchScalarGridSpec(
            num_scalar_prefetch=1,
            grid=(tiles,),
            in_specs=[
                pl.BlockSpec((rows, width), lambda step, table: (0, 0)),
                pl.BlockSpec(memory_space=pl.ANY),
            ],
            out_specs=pl.BlockSpec((rows, tile), lambda step, table: (0, step)),
            scratch_shapes=[
                pltpu.VMEM((tiles, width, tile), BF16),
                pltpu.VMEM((tiles, tile, width), BF16),
                pltpu.SemaphoreType.DMA((tiles,)),
            ],
        ),
        out_shape=jax.ShapeDtypeStruct((rows, width), F32),
        compiler_params=pltpu.CompilerParams(vmem_limit_bytes=24 * 1024 * 1024),
        cost_estimate=pl.CostEstimate(
            flops=8 * rows * width * width, bytes_accessed=2 * width * width, transcendentals=0
        ),
    )(table, value, weight)


def transposed_times(left, right):
    return lax.dot_general(left, right, CONTRACT_FIRST, preferred_element_type=F32)


def own_gradient_kernel(table, early, late, small_early, small_late, down_ref, up_ref):
    @pl.when(table[0] == 0)
    def _():
        down_ref[...] = transposed_times(early[...], small_late[...])
        up_ref[...] = transposed_times(small_early[...], late[...])

    @pl.when(table[0] == 1)
    def _():
        down_ref[...] = transposed_times(late[...], small_early[...])
        up_ref[...] = transposed_times(small_late[...], early[...])


def other_gradient_kernel(
    table, gain_ref, down_sum, up_sum, early, cotangent, pulled, hidden, small_early, small_late,
    down_ref, up_ref,
):
    ranks = down_ref.shape[1]
    late = small_late[:, :ranks]
    inverse = small_late[:, ranks : ranks + 1].astype(F32)
    toward = small_late[:, ranks + 64 : ranks + 65].astype(F32)

    @pl.when(table[0] == 0)
    def _():
        grad = (
            cotangent[...].astype(F32)
            + inverse * pulled[...].astype(F32)
            - toward * hidden[...].astype(F32)
        ).astype(BF16)
        down_ref[...] = down_sum[...] + transposed_times(early[...], late)
        up_ref[...] = up_sum[...] + transposed_times(small_early[...], grad)

    @pl.when(table[0] == 1)
    def _():
        scaled = (hidden[...].astype(F32) * gain_ref[...]).astype(BF16)
        weighed = (small_early[...].astype(F32) * inverse).astype(BF16)
        down_ref[...] = down_sum[...] + transposed_times(scaled, weighed)
        up_ref[...] = up_sum[...] + transposed_times(late, early[...])


def gradient_call(kernel, table, sums, by_column, whole, width, ranks, rows):
    tile = min(512, width)
    down_spec = pl.BlockSpec((tile, ranks), lambda step, table: (step, 0))
    up_spec = pl.BlockSpec((ranks, tile), lambda step, table: (0, step))
    leading = [array for array in by_column if array.shape[0] == 1]
    columns = [array for array in by_column if array.shape[0] != 1]
    return pl.pallas_call(
        kernel,
        grid_spec=pltpu.PrefetchScalarGridSpec(
            num_scalar_prefetch=1,
            grid=(width // tile,),
            in_specs=[pl.BlockSpec((1, tile), lambda step, table: (0, step)) for _ in leading]
            + [down_spec, up_spec][: len(sums)]
            + [pl.BlockSpec((rows, tile), lambda step, table: (0, step)) for _ in columns]
            + [pl.BlockSpec(array.shape, lambda step, table: (0, 0)) for array in whole],
            out_specs=[down_spec, up_spec],
        ),
        out_shape=[
            jax.ShapeDtypeStruct((width, ranks), F32),
            jax.ShapeDtypeStruct((ranks, width), F32),
        ],
        compiler_params=pltpu.CompilerParams(vmem_limit_bytes=20 * 1024 * 1024),
        cost_estimate=pl.CostEstimate(
            flops=4 * rows * width * ranks,
            bytes_accessed=8 * width * ranks * (1 + len(sums) // 2) + 2 * rows * width * len(columns),
            transcendentals=0,
        ),
    )(table, *leading, *sums, *columns, *whole)


def orders(count):
    first, first_slots, second, second_slots = [], [], [], []
    for z in range(count):
        sends = [(slot, 0, count - slot + z) for slot in range(z + 1, count)]
        sends += [(slot, 1, slot - count + z) for slot in range(count - z, count)]
        sends.sort()
        first.append([block for _, _, block in sends] + [z])
        first_slots.append({(slot, side): at for at, (slot, side, _) in enumerate(sends)})
        arrivals = [(slot, 0, z - 1 - slot) for slot in range(z)]
        arrivals += [(slot, 1, z + 1 + slot) for slot in range(count - 1 - z)]
        arrivals.sort()
        second.append([z] + [block for _, _, block in arrivals])
        second_slots.append([None] + [(slot, side) for slot, side, _ in arrivals])
    return first, first_slots, second, second_slots


def pick(number, choice, cases):
    chosen = cases[0]
    for at in range(1, len(cases)):
        members = [device for device, wanted in enumerate(choice) if wanted == at]
        chosen = jnp.where(is_one_of(number, members), cases[at], chosen)
    return chosen


def doubling_steps():
    count = lax.axis_size("tensor")
    return [
        [(place, place ^ (1 << bit)) for place in range(count)]
        for bit in range(count.bit_length() - 1)
    ]


def sum_step(value, pairs, wire=BF16, after=()):
    other = lax.ppermute(value.astype(wire), "tensor", pairs)
    if after:
        other = lax.optimization_barrier((other, *after))[0]
    return value + other.astype(F32)


def with_other_replicas(value, sections=(0, 1)):
    count = lax.axis_size("replica")
    return [value] + [
        lax.ppermute(
            value,
            ("section", "replica"),
            [(s * count + r, s * count + (r + step) % count) for s in sections for r in range(count)],
        )
        for step in range(1, count)
    ]


def on_device(
    tokens,
    cotangent,
    gain,
    frozen_base_weight,
    adapter_down_factors,
    adapter_up_factors,
    tenant_adapter_scale,
    row_tenant_owner,
):
    section = lax.axis_index("section")
    place = lax.axis_index("tensor")
    count = lax.axis_size("tensor")
    is_first = section == 0
    weight = frozen_base_weight[0]
    gain_row = gain[0][None, :]
    down = adapter_down_factors[0]
    up = adapter_up_factors[0]
    rows, width = tokens.shape
    features = width * count
    replicas = lax.axis_size("replica")
    ranks = down.shape[1]

    tenant_of_column = jnp.arange(ranks, dtype=jnp.int32) // (ranks // TENANT_COUNT)
    coefficients = jnp.where(
        row_tenant_owner[:, None] == tenant_of_column[None, :],
        jnp.repeat(tenant_adapter_scale, ranks // TENANT_COUNT)[None, :],
        0.0,
    )

    first_order, first_slots, second_order, second_slots = orders(count)
    place_of = section * count + place
    table = jnp.stack([section, place_of]).astype(jnp.int32)

    def times_down(value):
        return jnp.dot(value, down, preferred_element_type=F32)

    def times_up_transposed(value):
        return lax.dot_general(value, up, CONTRACT_LAST, preferred_element_type=F32)

    def line(value, first_pairs, second_pairs, toward):
        pairs = [(2 * z, 2 * (z + toward)) for z in first_pairs] + [
            (2 * z + 1, 2 * (z + toward) + 1) for z in second_pairs
        ]
        return lax.ppermute(value, ("tensor", "section"), pairs)

    token_float = tokens.astype(F32)
    early = jnp.where(is_first, (token_float * gain_row).astype(BF16), cotangent)
    early = lax.optimization_barrier(early)

    def small_columns(value, plain):
        small = jnp.where(is_first, times_down(value), times_up_transposed(value))
        squares = jnp.sum(plain.astype(F32) ** 2, axis=1)
        squares = jnp.pad(squares, (0, -rows % ranks)).reshape(-1, ranks)
        return jnp.concatenate([small, jnp.pad(squares, ((0, -len(squares) % 16), (0, 0)))], axis=0)

    everyone = range(count)
    steps_left = doubling_steps()
    arrivals = [
        (
            lax.ppermute(
                cotangent,
                ("tensor", "section"),
                [(2 * z, 2 * (z + 1) + 1) for z in everyone if z + 1 < count],
            ),
            line(cotangent, [], [z for z in everyone if z > 0], -1),
        )
    ]
    parts = []
    for stage in range(count):
        wanted = [None if stage == 0 else second_slots[z][stage] for z in everyone]
        cases = sorted({slot for slot in wanted if slot is not None})
        here = [early] + [arrivals[slot][side] for slot, side in cases]
        if stage == 1:
            small_sum = small_columns(*lax.optimization_barrier((early, tokens, *sent))[:2])
        elif stage > 1 and steps_left:
            small_sum = sum_step(small_sum, steps_left.pop(0), after=sent)
        if stage > 0:
            *here, small_sum = lax.optimization_barrier((*here, small_sum, *sent))[: len(here) + 1]
        value = pick(
            place_of,
            [0] * count + [0 if slot is None else 1 + cases.index(slot) for slot in wanted],
            here,
        )
        order = [blocks[stage] for blocks in first_order + second_order]
        part = block_product(table, value, weight, order)
        if stage == 1:
            part, after = lax.optimization_barrier((part, early))
            early_all = [early] + with_other_replicas(after)[1:]
        if stage == count - 1:
            part, *early_all = lax.optimization_barrier((part, *early_all))
        parts.append(part)
        slot = stage + 1
        if slot == count:
            break
        sent = []
        for side in (0, 1):
            needed = [first_slots[z].get((slot, side)) for z in everyone]
            stages = sorted({at for at in needed if at is not None})
            own = pick(
                place_of,
                [0 if at is None else stages.index(at) for at in needed] + [0] * count,
                [parts[at] for at in stages],
            )
            arrived = arrivals[-1][side]
            if side == 1:
                arrived, _ = lax.optimization_barrier((arrived, sent[0]))
            arrived = arrived.astype(F32)
            sent.append((arrived + jnp.where(is_first, own, 0.0)).astype(BF16))
        arrivals.append(
            (
                line(
                    sent[0],
                    [z for z in everyone if z < slot and z + 1 < count],
                    [z for z in everyone if slot + 1 < count and z >= slot and z + 1 < count],
                    1,
                ),
                line(
                    sent[1],
                    [z for z in everyone if z >= count - slot and z > 0],
                    [z for z in everyone if slot + 1 < count and z < count - slot and z > 0],
                    -1,
                ),
            )
        )
    from_left, from_right = arrivals[-1]

    while steps_left:
        small_sum = sum_step(small_sum, steps_left.pop(0))
    inv_first = lax.rsqrt(
        small_sum[rows:].reshape(-1)[:rows][:, None] / features + EPSILON
    )
    small_early = (coefficients * small_sum[:rows]).astype(BF16)
    small_early_all = with_other_replicas(
        (small_early.astype(F32) * jnp.where(is_first, inv_first, 1.0)).astype(BF16)
    )
    low_product = jnp.where(
        is_first,
        jnp.dot(small_early, up, preferred_element_type=F32),
        lax.dot_general(small_early, down, CONTRACT_LAST, preferred_element_type=F32),
    )

    pulled_here = (gain_row * (sum(parts) + low_product)).astype(BF16)
    swap = [(0, 1), (1, 0)]
    pulled = lax.ppermute(pulled_here, "section", swap)
    from_left, from_right, *small_early_all, _ = lax.optimization_barrier(
        (from_left, from_right, *small_early_all, pulled_here)
    )

    projected = parts[-1] + from_left.astype(F32) + from_right.astype(F32) + low_product
    hidden = (token_float + inv_first * projected).astype(BF16)
    half = width // 2 if width % 256 == 0 else width
    exchanged = jnp.where(is_first, hidden, pulled_here)
    first_halves = with_other_replicas(exchanged[:, :half])[1:]
    second_halves = None
    swapped = [
        lax.ppermute(jnp.where(is_first, hidden, other), "section", swap) for other in early_all[1:]
    ]
    hidden_on_second = swapped[0] if swapped else lax.ppermute(hidden, "section", swap)
    cotangent_all = [cotangent] + swapped
    hidden_float = hidden.astype(F32)
    pulled_float = pulled.astype(F32)
    row_sums = jnp.stack(
        [jnp.sum(hidden_float * hidden_float, axis=1), jnp.sum(hidden_float * pulled_float, axis=1)]
    )
    if count <= 4:
        row_sums = row_sums + sum(
            lax.ppermute(row_sums, "tensor", [(z, (z + step) % count) for z in everyone])
            for step in range(1, count)
        )
    else:
        for step in doubling_steps():
            row_sums = sum_step(row_sums, step, F32)
    row_sums, *first_halves = lax.optimization_barrier((row_sums, *first_halves))
    inv_second = lax.rsqrt(row_sums[0] / features + EPSILON)
    inv_second = inv_second[:, None]
    toward_hidden = row_sums[1][:, None] * inv_second * inv_second * inv_second / features
    hidden_grad = cotangent.astype(F32) + inv_second * pulled_float - toward_hidden * hidden_float
    late = jnp.where(
        is_first,
        hidden_grad.astype(BF16),
        (hidden_on_second.astype(F32) * gain_row).astype(BF16),
    )
    rank_late = jnp.where(is_first, times_up_transposed(late), times_down(late))
    if half < width:
        second_halves = with_other_replicas(
            lax.optimization_barrier((exchanged[:, half:], rank_late))[0]
        )[1:]
    inv_on_second = lax.ppermute(
        lax.optimization_barrier((inv_second[:, 0], rank_late))[0], "section", swap
    )[:, None]
    for step in doubling_steps():
        rank_late = sum_step(rank_late, step)

    late_others = first_halves
    if second_halves is not None:
        *second_halves, _ = lax.optimization_barrier((*second_halves, rank_late))
        late_others = [
            jnp.concatenate(halves, axis=1) for halves in zip(first_halves, second_halves)
        ]
    inv_second = jnp.where(is_first, inv_second, inv_on_second)
    row_scale = jnp.where(is_first, inv_first, inv_second)
    small_late = (coefficients * rank_late * row_scale).astype(BF16)
    small_late_all = with_other_replicas(
        jnp.concatenate(
            [
                small_late,
                jnp.broadcast_to(inv_second, (rows, 64)).astype(BF16),
                jnp.broadcast_to(toward_hidden, (rows, 64)).astype(BF16),
            ],
            axis=1,
        )
    )
    small_early_own = (small_early.astype(F32) * row_scale).astype(BF16)
    sums = gradient_call(
        own_gradient_kernel,
        table, [], [early, late], [small_early_own, small_late], width, ranks, rows,
    )
    swapped = [
        lax.ppermute(lax.optimization_barrier((other, rank_late))[0], "section", swap)
        for other in late_others
    ]
    hidden_all = [hidden] + [jnp.where(is_first, *pair) for pair in zip(late_others, swapped)]
    pulled_all = [pulled] + swapped
    for at in range(1, replicas):
        sums = gradient_call(
            other_gradient_kernel,
            table,
            sums,
            [gain_row, early_all[at], cotangent_all[at], pulled_all[at], hidden_all[at]],
            [small_early_all[at], small_late_all[at]],
            width,
            ranks,
            rows,
        )
    grad_down, grad_up = sums
    return (grad_down[None], grad_up[None])


def solution(mesh):
    return jax.shard_map(
        on_device,
        mesh=mesh,
        in_specs=(
            P(("groups", "replica"), "tensor"),
            P(("groups", "replica"), "tensor"),
            P("section", "tensor"),
            P("section", "tensor", None),
            P("section", "tensor", None),
            P("section", None, "tensor"),
            P(),
            P(("groups", "replica")),
        ),
        out_specs=(P("section", "tensor", "groups"), P("section", "groups", "tensor")),
        check_vma=False,
    )
```
